32 devices in a mesh: dp: 2 (over y), seq: 16 (over z, x, core).
Axes of the slice: x: 2, y: 2, z: 4, core: 2. Of those that a mesh axis runs over, the one named last changes fastest.
Arguments:
- tokens: bfloat16 [5120, 768], P(('dp', 'seq')), may hold values from -6 to 6
- segment_ids: int32 [5120], P(('dp', 'seq')), may hold values from 0 to 15, as said below
- pad_mask: int32 [5120], P(('dp', 'seq')), may hold values from 0 to 1, as said below
- w_qkv: float32 [1, 768, 2304], P(None, ('dp', 'seq')), may hold values from -0.21875 to 0.21875
- w_out: float32 [1, 768, 768], P(None, ('dp', 'seq')), may hold values from -2.5 to 2.5
- w_gate: float32 [1, 768, 3072], P(None, ('dp', 'seq')), may hold values from -0.21875 to 0.21875
- w_up: float32 [1, 768, 3072], P(None, ('dp', 'seq')), may hold values from -0.21875 to 0.21875
- w_down: float32 [1, 3072, 768], P(None, ('dp', 'seq')), may hold values from -0.109375 to 0.109375
- ln_gain: float32 [1, 2, 768], P(None, None, ('dp', 'seq')), may hold values from 0.5 to 1.5
- ln_bias: float32 [1, 2, 768], P(None, None, ('dp', 'seq')), may hold values from -2 to 2
- cotangent: bfloat16 [5120, 768], P(('dp', 'seq')), may hold values from -6 to 6
Outputs:
- output: bfloat16 [5120, 768], P(('dp', 'seq'))
- grad_input: float32 [5120, 768], P(('dp', 'seq'))
- grad_qkv: float32 [1, 768, 2304], P(None, ('dp', 'seq'))
- grad_out: float32 [1, 768, 768], P(None, ('dp', 'seq'))
- grad_gate: float32 [1, 768, 3072], P(None, ('dp', 'seq'))
- grad_up: float32 [1, 768, 3072], P(None, ('dp', 'seq'))
- grad_down: float32 [1, 3072, 768], P(None, ('dp', 'seq'))
- grad_gain: float32 [1, 2, 768], P(None, None, ('dp', 'seq'))
- grad_bias: float32 [1, 2, 768], P(None, None, ('dp', 'seq'))
The draws below stay inside these ranges and needn't reach their ends.
Inputs may be any that keep to these rules, and one draw needn't show every extreme that they name: `segment_ids`: within each sequence of 2560 tokens, tokens with equal ids form one document; the first 4 tokens of every 160 belong to document 0, and the other ids never fall along a sequence. `pad_mask`: 0 exactly on the tokens whose segment id is the largest of their sequence.
All inputs are finite; a program needn't handle non-finite values.
Results may differ from the reference program's by a relative error of at most 0.02.
Values may be sent and summed in bfloat16 or wider, within the bound.
No kernel may reach another device: no remote copies, remote signals or barrier semaphores. Data moves between devices by JAX's collectives and lax.ppermute only.
A program may use at most 384 MiB of HBM per device.

```python
import jax
import jax.numpy as jnp
from jax import lax

D = 768
HEADS = 12
HEAD_DIM = 64
FF = 3072
LAYERS = 1
SPREAD = 4
TOK_DEV = 160
LENGTH = 2560
SEQS = 2
TOKENS = 5120


def layout(key):
    doc_slots = LENGTH // 200 + 1
    drawn_total = LENGTH - SPREAD * (LENGTH // TOK_DEV)
    places = jnp.arange(LENGTH, dtype=jnp.int32)
    offset_in = places % TOK_DEV
    device = places // TOK_DEV
    drawn_rank = device * (TOK_DEV - SPREAD) + offset_in - SPREAD
    spread = offset_in < SPREAD
    seg_rows = []
    mask_rows = []
    for sequence in range(SEQS):
        seq_key = jax.random.fold_in(key, sequence)
        length_key, pad_key = jax.random.split(seq_key)
        lengths = jax.random.randint(length_key, (doc_slots,), 200, 2001, dtype=jnp.int32)
        bounds = jnp.cumsum(lengths).astype(jnp.int32)
        doc_number = 1 + jnp.sum((bounds[None, :] <= drawn_rank[:, None]).astype(jnp.int32), axis=1)
        padding = jax.random.randint(pad_key, (), max(drawn_total // 16, 1), max(drawn_total // 4, 2), dtype=jnp.int32)
        padded = drawn_rank >= drawn_total - padding
        seg_row = jnp.where(spread, 0, jnp.where(padded, doc_slots + 2, doc_number)).astype(jnp.int32)
        mask_row = jnp.where(spread | jnp.logical_not(padded), 1, 0).astype(jnp.int32)
        seg_rows.append(seg_row)
        mask_rows.append(mask_row)
    return (jnp.concatenate(seg_rows), jnp.concatenate(mask_rows))


def draw_segment_ids(key, part):
    return layout(key)[0]


def draw_pad_mask(key, part):
    return layout(key)[1]


def shard_levels(own_key, extent, pieces, smallest, top_value):
    level = 1.0
    for position, parts in pieces:
        heights = jax.random.uniform(jax.random.fold_in(jax.random.fold_in(own_key, 6), position), (parts,), jnp.float32, smallest / len(pieces), top_value / len(pieces))
        level = level * jnp.repeat(jnp.exp(heights), extent[position] // parts).reshape((-1,) + (1,) * (len(extent) - 1 - position))
    return level


def gaussian(rng, shape, deviation, limit, pieces=(), kind=jnp.bfloat16):
    factor_of = shard_levels(rng, shape, pieces, -0.22, 0.18) if pieces else 1.0
    entries = jax.random.normal(rng, shape, jnp.float32) * deviation * factor_of
    return jnp.minimum(jnp.maximum(entries, -limit), limit).astype(kind)


def setup_inputs(seed: int = 0) -> dict:
    key_list = jax.random.split(jax.random.key(seed), 12)
    tokens = gaussian(key_list[0], (TOKENS, D), 1.0, 6.0, ((0, 32),))
    segment_ids = draw_segment_ids(jax.random.fold_in(key_list[11], 71), 0)
    pad_mask = draw_pad_mask(jax.random.fold_in(key_list[11], 71), 0)
    w_qkv = gaussian(key_list[3], (LAYERS, D, 3 * D), D ** -0.5, 0.21875, ((1, 32),), jnp.float32)
    w_out = gaussian(key_list[4], (LAYERS, D, D), (max(D // 128, 1)) ** -0.5, 2.5, ((1, 32),), jnp.float32)
    w_gate = gaussian(key_list[5], (LAYERS, D, FF), D ** -0.5, 0.21875, ((1, 32),), jnp.float32)
    w_up = gaussian(key_list[6], (LAYERS, D, FF), D ** -0.5, 0.21875, ((1, 32),), jnp.float32)
    w_down = gaussian(key_list[7], (LAYERS, FF, D), FF ** -0.5, 0.109375, ((1, 32),), jnp.float32)
    ln_gain = jnp.clip(1.0 + 0.1 * jax.random.normal(key_list[8], (LAYERS, 2, D), jnp.float32), 0.5, 1.5)
    ln_bias = gaussian(key_list[9], (LAYERS, 2, D), 0.3, 2.0, ((2, 32),), jnp.float32)
    cotangent = gaussian(key_list[10], (TOKENS, D), 1.0, 6.0, ((0, 32),))
    return dict(tokens=tokens, segment_ids=segment_ids, pad_mask=pad_mask, w_qkv=w_qkv, w_out=w_out, w_gate=w_gate, w_up=w_up, w_down=w_down, ln_gain=ln_gain, ln_bias=ln_bias, cotangent=cotangent)


epsilon = 1e-05
rope_base = 10000.0
highest = lax.Precision.HIGHEST

@jax.custom_vjp
def low(v):
    return lax.optimization_barrier(v.astype(jnp.bfloat16)).astype(jnp.float32)

@jax.custom_vjp
def low_back(v):
    return v

def low_keep(v):
    return (low(v), None)

def low_pass(kept, grad):
    return (grad,)

def back_keep(v):
    return (v, None)

def back_low(kept, grad):
    return (low(grad),)
low.defvjp(low_keep, low_pass)
low_back.defvjp(back_keep, back_low)

def product(left, right):
    return jnp.dot(left, right, precision=highest)

def doc_positions(seq_ids):
    block_size = min(512, LENGTH)
    places = jnp.arange(LENGTH, dtype=jnp.int32)

    def one_block(offset):
        seg_block = lax.dynamic_slice_in_dim(seq_ids, offset, block_size)
        rows_at = offset + jnp.arange(block_size, dtype=jnp.int32)
        earlier = (seg_block[:, None] == seq_ids[None, :]) & (places[None, :] < rows_at[:, None])
        return lax.optimization_barrier(jnp.sum(earlier.astype(jnp.int32), axis=1))
    offsets = jnp.arange(LENGTH // block_size, dtype=jnp.int32) * block_size
    return lax.map(one_block, offsets).reshape(LENGTH)

def rope_tables(positions):
    half_size = HEAD_DIM // 2
    frequency = jnp.exp(-jnp.log(rope_base) * jnp.arange(half_size, dtype=jnp.float32) * (2.0 / HEAD_DIM))
    angles = positions.astype(jnp.float32)[:, None] * frequency[None, :]
    return (jnp.cos(angles)[:, None, :], jnp.sin(angles)[:, None, :])

def rotate(values, cos_table, sin_table):
    half_size = values.shape[-1] // 2
    leading = values[..., :half_size]
    trailing = values[..., half_size:]
    return jnp.concatenate([leading * cos_table - trailing * sin_table, trailing * cos_table + leading * sin_table], axis=-1)

def layer_norm(values, gain_row, bias_row):
    average = lax.optimization_barrier(jnp.mean(values, axis=-1, keepdims=True))
    centred = values - average
    variance = lax.optimization_barrier(jnp.mean(centred * centred, axis=-1, keepdims=True))
    return centred * lax.rsqrt(variance + epsilon) * gain_row + bias_row

def attend(queries, key_rows, value_rows, seq_ids):
    block_size = min(512, LENGTH)
    factor = HEAD_DIM ** (-0.5)

    def one_block(offset):
        query_block = lax.dynamic_slice_in_dim(queries, offset, block_size)
        seg_block = lax.dynamic_slice_in_dim(seq_ids, offset, block_size)
        scores = low_back(jnp.einsum('qhd,khd->hqk', query_block, key_rows, precision=highest) * factor)
        allowed = (seg_block[:, None] == seq_ids[None, :])[None]
        masked_scores = jnp.where(allowed, scores, -1e+30)
        top_score = lax.optimization_barrier(jnp.max(masked_scores, axis=-1, keepdims=True))
        expo = jnp.where(allowed, jnp.exp(masked_scores - top_score), 0.0)
        weights_now = expo / lax.optimization_barrier(jnp.sum(expo, axis=-1, keepdims=True))
        return jnp.einsum('hqk,khd->qhd', low(weights_now), value_rows, precision=highest)
    offsets = jnp.arange(LENGTH // block_size, dtype=jnp.int32) * block_size
    return lax.map(jax.checkpoint(one_block), offsets).reshape(LENGTH, HEADS, HEAD_DIM)

def block_layer(hidden_in, seq_ids, keep_rows, cos_table, sin_table, qkv_w, out_w, gate_w, up_w, down_w, gain_rows, bias_rows):
    projected = low_back(product(low(hidden_in), qkv_w))
    shaped = projected.reshape(LENGTH, 3, HEADS, HEAD_DIM)
    queries = low_back(low(rotate(shaped[:, 0], cos_table, sin_table)))
    key_rows = low_back(low(rotate(shaped[:, 1], cos_table, sin_table)))
    value_rows = low_back(low(shaped[:, 2]))
    attended = attend(queries, key_rows, value_rows, seq_ids).reshape(LENGTH, D)
    attended = low_back(low(attended))
    mixed_sum = hidden_in + low_back(product(attended, out_w))
    middle = layer_norm(mixed_sum, gain_rows[0], bias_rows[0])
    middle_low = low(middle)
    gate_vals = low_back(product(middle_low, gate_w))
    up_vals = low_back(product(middle_low, up_w))
    hidden_low = low(jax.nn.silu(gate_vals) * up_vals)
    second = middle + low_back(product(hidden_low, down_w))
    return layer_norm(second, gain_rows[1], bias_rows[1]) * keep_rows

def reference(tokens, segment_ids, pad_mask, w_qkv, w_out, w_gate, w_up, w_down, ln_gain, ln_bias, cotangent):
    seq_ids = segment_ids.reshape(SEQS, LENGTH)
    row_keep = pad_mask.reshape(SEQS, LENGTH, 1).astype(jnp.float32)
    tables = [rope_tables(doc_positions(seq_ids[seq_index])) for seq_index in range(SEQS)]

    def forward(inputs, qkv_all, out_all, gate_all, up_all, down_all, gain_all, bias_all):
        lowered = []
        for layer_index in range(LAYERS):
            lowered.append((low(qkv_all[layer_index]), low(out_all[layer_index]), low(gate_all[layer_index]), low(up_all[layer_index]), low(down_all[layer_index]), low(gain_all[layer_index]), low(bias_all[layer_index])))
        sequences = inputs.reshape(SEQS, LENGTH, D)
        results = []
        for seq_index in range(SEQS):
            hidden = sequences[seq_index]
            for layer_index in range(LAYERS):
                params = lowered[layer_index]
                hidden = block_layer(hidden, seq_ids[seq_index], row_keep[seq_index], tables[seq_index][0], tables[seq_index][1], params[0], params[1], params[2], params[3], params[4], params[5], params[6])
            results.append(hidden)
        return jnp.stack(results).reshape(TOKENS, D)
    output, pullback = jax.vjp(forward, tokens.astype(jnp.float32), w_qkv, w_out, w_gate, w_up, w_down, ln_gain, ln_bias)
    gradients = pullback(cotangent.astype(jnp.float32))
    return (output.astype(jnp.bfloat16), gradients[0], gradients[1], gradients[2], gradients[3], gradients[4], gradients[5], gradients[6], gradients[7])
```

```python
import functools

import jax
import jax.numpy as jnp
from jax import lax
from jax.experimental import pallas as pl
from jax.experimental.pallas import tpu as pltpu
from jax.sharding import PartitionSpec as P

HEADS = 12
EPS = 1e-05
BASE = 10000.0
AXES = ("dp", "seq")
BF = jnp.bfloat16
F32 = jnp.float32
FAR = -1e30
ONES = 64


def dot(a, b):
    return jnp.dot(a, b, preferred_element_type=F32)


def dot_t(a, b):
    return lax.dot_general(a, b, (((1,), (1,)), ((), ())), preferred_element_type=F32)


def t_dot(a, b):
    return lax.dot_general(a, b, (((0,), (0,)), ((), ())), preferred_element_type=F32)


def lanes(shape):
    return lax.broadcasted_iota(jnp.int32, shape, len(shape) - 1)


def swap_halves(u):
    width = u.shape[-1]
    low = lanes(u.shape) % 64 < 32
    return jnp.where(low, pltpu.roll(u, width - 32, 1), pltpu.roll(u, 32, 1))


def split3(v):
    hi = v.astype(BF).astype(F32)
    rest = v - hi
    mid = rest.astype(BF).astype(F32)
    return hi, mid, rest - mid


def with_units(base, v):
    at = lanes(base.shape)
    hi, mid, low = split3(v)
    return jnp.where(
        at == ONES,
        -hi,
        jnp.where(at == ONES + 1, -mid, jnp.where(at == ONES + 2, -low, base)),
    )


def project_kernel(x_ref, w_ref, cos_ref, sin_ref, ext_ref, q_ref, k_ref, v_ref):
    x = x_ref[...]
    cos, sin, ext = cos_ref[...], sin_ref[...], ext_ref[...]

    def rope(u):
        return u * cos + swap_halves(u) * sin

    kv = dot(x, w_ref[:, 384:])
    for p in range(3):
        k = rope(kv[:, p * 128 : (p + 1) * 128])
        k_ref[p, :, :128] = k.astype(BF)
        k_ref[p, :, 128:] = ext
        v_ref[p, :, :128] = kv[:, 384 + p * 128 : 384 + (p + 1) * 128].astype(BF)
        v_ref[p, :, 128:] = ext

    @pl.when(pl.program_id(0) == 0)
    def _():
        q = dot(x, w_ref[:, :384])
        for p in range(3):
            r = rope(q[:, p * 128 : (p + 1) * 128]).astype(BF)
            q_ref[:, p * 128 : (p + 1) * 128] = r * jnp.asarray(0.125, BF)


def project(x_all, w, cos, sin, ext, own):
    count, width = x_all.shape
    return pl.pallas_call(
        project_kernel,
        grid=(count // own,),
        in_specs=[
            pl.BlockSpec((own, width), lambda i: (i, 0)),
            pl.BlockSpec((width, 1152), lambda i: (0, 0)),
            pl.BlockSpec((own, 128), lambda i: (i, 0)),
            pl.BlockSpec((own, 128), lambda i: (i, 0)),
            pl.BlockSpec((own, 128), lambda i: (i, 0)),
        ],
        out_specs=[
            pl.BlockSpec((own, 384), lambda i: (0, 0)),
            pl.BlockSpec((3, own, 256), lambda i: (0, i, 0)),
            pl.BlockSpec((3, own, 256), lambda i: (0, i, 0)),
        ],
        out_shape=[
            jax.ShapeDtypeStruct((own, 384), BF),
            jax.ShapeDtypeStruct((3, count, 256), BF),
            jax.ShapeDtypeStruct((3, count, 256), BF),
        ],
        compiler_params=pltpu.CompilerParams(vmem_limit_bytes=32 << 20),
        cost_estimate=pl.CostEstimate(
            flops=2 * count * width * 768, bytes_accessed=count * 5000, transcendentals=0
        ),
        name="project",
    )(x_all, w, cos, sin, ext)


def attend_kernel(q_ref, k_ref, v_ref, ext_ref, att_ref, ob_ref, lse_ref, s_ref, *, chunk):
    keys = k_ref.shape[1]
    q = q_ref[...]
    own = q.shape[0]
    first = lanes(q.shape) < 64
    ext = ext_ref[...]
    parts = []
    for h in range(2):
        qh = jnp.where(first if h == 0 else ~first, q, jnp.zeros_like(q))
        qc = jnp.concatenate([qh, ext], axis=1)
        top = jnp.full((own, 128), FAR, F32)
        for j in range(0, keys, chunk):
            s = dot_t(qc, k_ref[0, j : j + chunk, :])
            s_ref[h, :, j : j + chunk] = s
            for i in range(0, chunk, 128):
                top = jnp.maximum(top, s[:, i : i + 128])
        m = jnp.max(top, axis=1, keepdims=True)
        acc = jnp.zeros((own, 256), F32)
        for j in range(0, keys, chunk):
            e = jnp.exp(s_ref[h, :, j : j + chunk] - m).astype(BF)
            acc = acc + dot(e, v_ref[0, j : j + chunk, :])
        total = acc[:, 128 + ONES : 129 + ONES]
        parts.append(acc[:, :128] / total)
        lse_ref[h] = with_units(ext.astype(F32), m + jnp.log(total)).astype(BF)
    att = jnp.where(first, parts[0], parts[1])
    att_ref[...] = att
    ob_ref[...] = att.astype(BF)


def attend(q, k, v, ext):
    own = q.shape[0]
    keys = k.shape[1]
    return pl.pallas_call(
        functools.partial(attend_kernel, chunk=512),
        grid=(3,),
        in_specs=[
            pl.BlockSpec((own, 128), lambda p: (0, p)),
            pl.BlockSpec((1, keys, 256), lambda p: (p, 0, 0)),
            pl.BlockSpec((1, keys, 256), lambda p: (p, 0, 0)),
            pl.BlockSpec((own, 128), lambda p: (0, 0)),
        ],
        out_specs=[
            pl.BlockSpec((own, 128), lambda p: (0, p)),
            pl.BlockSpec((own, 128), lambda p: (0, p)),
            pl.BlockSpec((2, own, 128), lambda p: (p, 0, 0)),
        ],
        out_shape=[
            jax.ShapeDtypeStruct((own, 384), F32),
            jax.ShapeDtypeStruct((own, 384), BF),
            jax.ShapeDtypeStruct((6, own, 128), BF),
        ],
        scratch_shapes=[pltpu.VMEM((2, own, keys), F32)],
        compiler_params=pltpu.CompilerParams(vmem_limit_bytes=56 << 20),
        cost_estimate=pl.CostEstimate(
            flops=4 * 6 * own * keys * 256,
            bytes_accessed=3 * keys * 1024,
            transcendentals=6 * own * keys,
        ),
        name="attend",
    )(q, k, v, ext)


def attend_back_kernel(
    q_ref, lse_ref, d_ref, att_ref, k_ref, v_ref, cos_ref, sin_ref, cosq_ref, sinq_ref,
    dq_ref, dk_ref, dv_ref, qc_s, dc_s, dq_s,
):
    j = pl.program_id(1)
    own = q_ref.shape[0]

    @pl.when(j == 0)
    def _():
        q, d = q_ref[...], d_ref[...]
        first = lanes(q.shape) < 64
        prod = d.astype(F32) * att_ref[...]
        for h in range(2):
            keep = first if h == 0 else ~first
            rows = slice(h * own, (h + 1) * own)
            qc_s[rows, :128] = jnp.where(keep, q, jnp.zeros_like(q))
            qc_s[rows, 128:] = lse_ref[h]
            dc_s[rows, :128] = jnp.where(keep, d, jnp.zeros_like(d))
            delta = jnp.sum(jnp.where(keep, prod, 0.0), axis=1, keepdims=True)
            dc_s[rows, 128:] = with_units(jnp.zeros((own, 128), F32), delta).astype(BF)
        dq_s[...] = jnp.zeros_like(dq_s)

    k = k_ref[0]
    v = v_ref[0]
    e = jnp.exp(dot_t(k, qc_s[...]))
    ds = (e * dot_t(v, dc_s[...])).astype(BF)
    dv_ref[...] = dot(e.astype(BF), dc_s[:, :128]).astype(BF)
    dk = dot(ds, qc_s[:, :128]).astype(BF).astype(F32)
    dk_ref[...] = (dk * cos_ref[...] - swap_halves(dk) * sin_ref[...]).astype(BF)
    dq_s[...] += t_dot(k[:, :128], ds)

    @pl.when(j == pl.num_programs(1) - 1)
    def _():
        t = dq_s[...].T
        first = lanes((own, 128)) < 64
        dq = jnp.where(first, t[:own], t[own:])
        dq = (dq * 0.125).astype(BF).astype(F32)
        dq_ref[...] = (dq * cosq_ref[...] - swap_halves(dq) * sinq_ref[...]).astype(BF)


def attend_back(q, lse, d, att, k, v, cos, sin):
    own = q.shape[0]
    keys = k.shape[1]
    chunk = 512
    return pl.pallas_call(
        attend_back_kernel,
        grid=(3, keys // chunk),
        in_specs=[
            pl.BlockSpec((own, 128), lambda p, j: (0, p)),
            pl.BlockSpec((2, own, 128), lambda p, j: (p, 0, 0)),
            pl.BlockSpec((own, 128), lambda p, j: (0, p)),
            pl.BlockSpec((own, 128), lambda p, j: (0, p)),
            pl.BlockSpec((1, chunk, 256), lambda p, j: (p, j, 0)),
            pl.BlockSpec((1, chunk, 256), lambda p, j: (p, j, 0)),
            pl.BlockSpec((chunk, 128), lambda p, j: (j, 0)),
            pl.BlockSpec((chunk, 128), lambda p, j: (j, 0)),
            pl.BlockSpec((own, 128), lambda p, j: (0, 0)),
            pl.BlockSpec((own, 128), lambda p, j: (0, 0)),
        ],
        out_specs=[
            pl.BlockSpec((own, 128), lambda p, j: (0, p)),
            pl.BlockSpec((chunk, 128), lambda p, j: (j, p)),
            pl.BlockSpec((chunk, 128), lambda p, j: (j, p)),
        ],
        out_shape=[
            jax.ShapeDtypeStruct((own, 384), BF),
            jax.ShapeDtypeStruct((keys, 384), BF),
            jax.ShapeDtypeStruct((keys, 384), BF),
        ],
        scratch_shapes=[
            pltpu.VMEM((2 * own, 256), BF),
            pltpu.VMEM((2 * own, 256), BF),
            pltpu.VMEM((128, 2 * own), F32),
        ],
        compiler_params=pltpu.CompilerParams(vmem_limit_bytes=32 << 20),
        cost_estimate=pl.CostEstimate(
            flops=10 * 6 * own * keys * 256,
            bytes_accessed=3 * keys * 1600,
            transcendentals=6 * own * keys,
        ),
        name="attend_back",
    )(q, lse, d, att, k, v, cos, sin, cos[:own], sin[:own])


def normalize(values):
    average = jnp.mean(values, axis=-1, keepdims=True)
    centred = values - average
    factor = lax.rsqrt(jnp.mean(centred * centred, axis=-1, keepdims=True) + EPS)
    return centred * factor, factor


def norm_back(gradient, normed, factor):
    return factor * (
        gradient
        - jnp.mean(gradient, axis=-1, keepdims=True)
        - normed * jnp.mean(gradient * normed, axis=-1, keepdims=True)
    )


class Grid:
    def __init__(self, ndp, nseq):
        self.ny, self.nz = ndp, nseq // 4
        self.count = ndp * nseq
        self.ring = [0, 1, 3, 2] if self.nz == 4 else list(range(self.nz))
        self.place = [self.ring.index(z) for z in range(self.nz)]
        step = {z: self.ring[(self.place[z] + 1) % self.nz] for z in range(self.nz)}
        self.across = {
            "c": self.pairs(lambda y, z, x, c: (y, z, x, 1 - c)),
            "x": self.pairs(lambda y, z, x, c: (y, z, 1 - x, c)),
            "y": self.pairs(lambda y, z, x, c: (1 - y, z, x, c)),
            "up": self.pairs(lambda y, z, x, c: (y, step[z], x, c)),
        }
        self.across["down"] = [(b, a) for a, b in self.across["up"]]
        self.across["spread"] = self.pairs(lambda y, z, x, c: (1 - y, z, x, c) if c == y else None)
        self.across["home"] = self.pairs(lambda y, z, x, c: (1 - y, z, x, c) if c != y else None)
        self.across["give"] = self.pairs(lambda y, z, x, c: (y, z, x, 1 - c) if c == y else None)

    def pairs(self, to):
        def index(y, z, x, c):
            return ((y * self.nz + z) * 2 + x) * 2 + c

        made = []
        for y in range(self.ny):
            for z in range(self.nz):
                for x in range(2):
                    for c in range(2):
                        there = to(y, z, x, c)
                        if there is not None:
                            made.append((index(y, z, x, c), index(*there)))
        return made

    def locate(self):
        s = lax.axis_index("seq")
        self.y = lax.axis_index("dp")
        self.z, self.x, self.c = s // 4, (s // 2) % 2, s % 2
        self.p = self.place_of(self.z)

    def place_of(self, z):
        return z ^ (z >> 1) if self.nz == 4 else z

    def move(self, way, a):
        return lax.ppermute(a, AXES, self.across[way])

    def ordered(self, bit, mine, theirs, axis):
        return jnp.where(
            bit == 0,
            jnp.concatenate([mine, theirs], axis=axis),
            jnp.concatenate([theirs, mine], axis=axis),
        )

    def gather(self, shard, order):
        a = shard[None, None, None]
        for axis in order:
            if axis == "z":
                held = [a]
                for _ in range(self.nz - 1):
                    held.append(self.move("up", held[-1]))
                if self.nz == 4:
                    pieces = []
                    for z in range(4):
                        back = (self.p - self.place[z]) % 4
                        pieces.append(
                            jnp.where(
                                back < 2,
                                jnp.where(back == 0, held[0], held[1]),
                                jnp.where(back == 2, held[2], held[3]),
                            )
                        )
                    a = jnp.concatenate(pieces, axis=1)
                else:
                    twice = jnp.concatenate(held[::-1] * 2, axis=1)
                    a = lax.dynamic_slice_in_dim(twice, self.nz - 1 - self.p, self.nz, 1)
            elif axis == "x":
                a = self.ordered(self.x, a, self.move("x", a), 2)
            else:
                a = self.ordered(self.y, a, self.move("y", a), 0)
        return a

    def blocks(self, order, count):
        i = jnp.arange(count, dtype=jnp.int32)
        y, z, x = (jnp.full((count,), v, jnp.int32) for v in (self.y, self.z, self.x))
        size = {"x": 2, "y": 2, "z": self.nz}
        for axis in reversed(order):
            if axis in size:
                d, i = i % size[axis], i // size[axis]
                if axis == "x":
                    x = x ^ d
                elif axis == "y":
                    y = y ^ d
                else:
                    z = self.place_of((self.p - d) % self.nz)
        return y, z, x

    def reduce(self, first, rest, order):
        raise NotImplementedError


def ring_sum(grid, blocks):
    part = blocks[-1]
    for d in range(len(blocks) - 2, -1, -1):
        part = grid.move("down", part.astype(BF)).astype(F32) + blocks[d]
    return part


def pair_sum(grid, axis, mine, theirs):
    return mine + grid.move(axis, theirs.astype(BF)).astype(F32)


def reduce_rows(grid, left, right, order):
    count = left.shape[0]
    head, tail = order[0], order[1:]
    if head == "z":
        whole = dot(left, right)
        size = count // grid.nz
        part = ring_sum(grid, [whole[d * size : (d + 1) * size] for d in range(grid.nz)])
    else:
        theirs = dot(left[count // 2 :], right).astype(BF)
        part = dot(left[: count // 2], right) + grid.move(head, theirs).astype(F32)
    for axis in tail:
        count = part.shape[0]
        if axis == "z":
            size = count // grid.nz
            part = ring_sum(grid, [part[d * size : (d + 1) * size] for d in range(grid.nz)])
        else:
            part = pair_sum(grid, axis, part[: count // 2], part[count // 2 :])
    return part


def body(grid, tokens, segment_ids, pad_mask, w_qkv, w_out, w_gate, w_up, w_down, ln_gain, ln_bias, cotangent):
    grid.locate()
    y, z, x, c = grid.y, grid.z, grid.x, grid.c
    local, width = tokens.shape
    own = 2 * local
    chips = grid.nz * 2
    rows = w_qkv.shape[1]
    down_rows = w_down.shape[1]
    half = width // 2
    ff = w_gate.shape[2] // 2
    move = grid.move

    def side(a, which, size):
        return jnp.where(which == 0, a[:, :size], a[:, size:])

    note = jnp.concatenate([segment_ids[None, :], pad_mask[None, :]], axis=0).astype(BF)
    note = jnp.pad(note, ((0, 6), (0, width - local)))
    message = jnp.concatenate([tokens, note], axis=0)
    held = [message]
    for _ in range(grid.nz - 1):
        held.append(move("up", held[-1]))
    along = jnp.stack(held)
    along = jnp.concatenate([along, move("x", along)], axis=0)
    beside = move("c", along)
    x_all = jnp.stack([along[:, :local], beside[:, :local]], axis=1).reshape(-1, width)
    ids = jnp.stack([along[:, local, :local], beside[:, local, :local]], axis=1)
    ids = ids.reshape(2 * chips, local)
    keep = jnp.concatenate([along[0, local + 1, :local], beside[0, local + 1, :local]])
    keep = keep.astype(F32)[:, None]
    cot = jnp.concatenate([cotangent, move("c", cotangent)], axis=0).astype(F32)

    w3 = [w_qkv[0, :, j * width : (j + 1) * width].astype(BF) for j in range(3)]
    gate_up = [w_gate[0].astype(BF), w_up[0].astype(BF)]
    mine = [side(w, c, half) for w in w3] + [side(w, c, ff) for w in gate_up]
    theirs = [side(w, 1 - c, half) for w in w3] + [side(w, 1 - c, ff) for w in gate_up]
    mine = jnp.concatenate(mine, axis=1)
    shard = grid.ordered(c, mine, move("c", jnp.concatenate(theirs, axis=1)), 0)
    n3 = 3 * half
    qkv_w = grid.gather(shard[:, :n3], "zxy").reshape(width, n3)

    extra = jnp.concatenate([ln_gain[0], ln_bias[0]], axis=0).astype(BF).reshape(1, 4 * rows)
    extra = jnp.pad(extra, ((0, 7), (0, width - 4 * rows)))
    out_shard = jnp.concatenate([w_out[0].astype(BF), extra], axis=0)
    out_half = grid.gather(out_shard, "yxz")
    out_both = grid.ordered(
        c, out_half[:, :, :, None], move("c", out_half)[:, :, :, None], 3
    ).reshape(grid.count, rows + 8, width)
    out_w = out_both[:, :rows].reshape(width, width)
    params = out_both[:, rows, : 4 * rows].reshape(grid.count, 4, rows)
    params = jnp.transpose(params, (1, 0, 2)).reshape(4, width).astype(F32)
    gain_one, gain_two, bias_one, bias_two = (params[i : i + 1] for i in range(4))

    gate_w = grid.gather(shard[:, n3 : n3 + ff], "zxy").reshape(width, ff)
    up_w = grid.gather(shard[:, n3 + ff :], "zyx").reshape(width, ff)
    down = w_down[0].astype(BF)
    down = grid.ordered(c, down, move("c", down), 0)
    down = jnp.where(c == y, down, move("spread", down))
    down_w = grid.gather(down, "zx").reshape(ff, width)

    onehot = (ids[:, :, None] == jnp.arange(64, dtype=jnp.int32).astype(BF)).astype(F32)
    at = jnp.arange(2 * chips, dtype=jnp.int32)
    _, bz, bx = grid.blocks("xz", chips)
    number = (bz * 2 + bx)[:, None] * 2 + jnp.stack([c, 1 - c])[None, :]
    number = number.reshape(2 * chips)
    tri = jnp.arange(local)
    before = jnp.einsum(
        "ij,bjs->bis", (tri[None, :] < tri[:, None]).astype(BF), onehot.astype(BF),
        preferred_element_type=F32,
    )
    counts = jnp.sum(onehot, axis=1)
    earlier = jnp.sum(
        jnp.where((number[None, :] < number[:, None])[:, :, None], counts[None], 0.0), axis=1
    )
    position = jnp.sum(onehot * (before + earlier[:, None, :]), axis=2).reshape(-1)
    del at
    lane = jnp.arange(128, dtype=jnp.int32)
    frequency = jnp.exp(-jnp.log(BASE) * (lane % 32).astype(F32) * (2.0 / 64))
    angle = position[:, None] * frequency[None, :]
    cos = jnp.cos(angle)
    sin = jnp.sin(angle) * jnp.where(lane % 64 < 32, -1.0, 1.0)
    flat = onehot.reshape(-1, 64)
    units = jnp.broadcast_to((jnp.arange(64) < 3).astype(F32), flat.shape)
    key_ext = jnp.concatenate([flat, units], axis=1).astype(BF)
    query_ext = jnp.concatenate(
        [(1.0 - flat[:own]) * FAR, jnp.zeros((own, 64), F32)], axis=1
    ).astype(BF)

    q, k, v = project(x_all, qkv_w, cos, sin, key_ext, own)
    att, ob, lse = attend(q, k, v, query_ext)

    def turned(a):
        return jnp.concatenate([a[local:], a[:local]], axis=0)

    ob_all = grid.ordered(c, ob, turned(move("c", ob)), 1)
    x_own = x_all[:own]
    n1, f1 = normalize(x_own.astype(F32) + dot(ob_all, out_w))
    h1 = n1 * gain_one + bias_one
    h1_low = h1.astype(BF)
    gate = dot(h1_low, gate_w)
    up = dot(h1_low, up_w)
    hidden = (jax.nn.silu(gate) * up).astype(BF)
    part = dot(hidden, down_w)
    n2, f2 = normalize(h1 + part + turned(move("c", part)))
    output = ((n2[:local] * gain_two + bias_two) * keep[:local]).astype(BF)

    masked = cot * keep
    grad_gain_two = jnp.sum(masked * n2, axis=0)
    grad_bias_two = jnp.sum(masked, axis=0)
    dr2 = norm_back(masked * gain_two, n2, f2)
    dm = dr2.astype(BF)
    dh = dot_t(dm, down_w)
    sigmoid = jax.nn.sigmoid(gate)
    dgate = (dh * up * sigmoid * (1.0 + gate * (1.0 - sigmoid))).astype(BF)
    dup = (dh * gate * sigmoid).astype(BF)

    def selector(order, per, size, both):
        blocks = size // per
        by, bz, bx = grid.blocks(order, blocks)
        start = ((by * grid.nz + bz) * 2 + bx) * per
        row = (start[:, None] + jnp.arange(per, dtype=jnp.int32)[None, :]).reshape(-1)
        del both
        return (jnp.arange(size, dtype=jnp.int32)[:, None] == row[None, :]).astype(BF)

    def turned_rows(order, a, per):
        return t_dot(selector(order, per, a.shape[1], True), a.T).astype(BF)

    two = 2 * rows

    size_d = 2 * down_rows
    by, bz, bx = grid.blocks("xz", chips)
    row = ((bz * 2 + bx) * size_d)[:, None] + jnp.arange(size_d, dtype=jnp.int32)[None, :]
    pick = (jnp.arange(ff, dtype=jnp.int32)[:, None] == row.reshape(1, -1)).astype(BF)
    hidden_t = lax.dot_general(
        pick, hidden, (((0,), (1,)), ((), ())), preferred_element_type=F32
    ).astype(BF)
    dd = reduce_rows(grid, hidden_t, dm, "xz")
    dd = dd + move("home", dd.astype(BF)).astype(F32)
    sent = jnp.where(c == 0, dd[down_rows:], dd[:down_rows])
    kept = jnp.where(c == 0, dd[:down_rows], dd[down_rows:])
    grad_down = jnp.where(c == y, kept, move("give", sent))

    def rows_in(order, a):
        sel = selector(order, two, width, True)
        return lax.dot_general(
            sel, a, (((0,), (1,)), ((), ())), preferred_element_type=F32
        ).astype(BF)

    def finish(part, size):
        sent = jnp.where(c == 0, part[rows:], part[:rows])
        kept = jnp.where(c == 0, part[:rows], part[rows:])
        got = move("c", sent)
        pieces = []
        for i in range(0, part.shape[1], size):
            pieces.append(grid.ordered(c, kept[:, i : i + size], got[:, i : i + size], 1))
        return jnp.concatenate(pieces, axis=1)

    h1_yx = rows_in("yxz", h1_low)
    h1_xy = rows_in("xyz", h1_low)
    grad_gate = finish(reduce_rows(grid, h1_yx, dgate, "yxz"), ff)
    grad_up = finish(reduce_rows(grid, h1_xy, dup, "xyz"), ff)

    part = dot_t(dgate, gate_w) + dot_t(dup, up_w)
    dh1 = dr2 + part + turned(move("c", part))
    grad_gain_one = jnp.sum(dh1 * n1, axis=0)
    grad_bias_one = jnp.sum(dh1, axis=0)
    dr1 = norm_back(dh1 * gain_one, n1, f1)
    da = dr1.astype(BF)
    my_out = jnp.where(c == 0, out_w[:half], out_w[half:])
    dob = dot_t(da, my_out).astype(BF)

    dq, dk, dv = attend_back(q, lse, dob, att, k, v, cos, sin)

    by, bz, bx = grid.blocks("yxz", grid.count // 2)
    start = (((by * grid.nz + bz) * 2 + bx) * 2 + c) * rows
    row = (start[:, None] + jnp.arange(rows, dtype=jnp.int32)[None, :]).reshape(1, -1)
    pick = (jnp.arange(width, dtype=jnp.int32)[:, None] == row).astype(BF)
    ob_t = lax.dot_general(
        pick, ob_all, (((0,), (1,)), ((), ())), preferred_element_type=F32
    ).astype(BF)
    do = dot(ob_t, da).reshape(grid.count // 2, rows, width)
    norms = jnp.stack([grad_gain_one, grad_gain_two, grad_bias_one, grad_bias_two])
    hi, mid, low = split3(norms)
    norms = dot(hi.astype(BF), pick) + dot(mid.astype(BF), pick) + dot(low.astype(BF), pick)
    norms = jnp.transpose(norms.reshape(4, grid.count // 2, rows), (1, 0, 2))
    norms = jnp.pad(norms.reshape(-1, 1, 4 * rows), ((0, 0), (0, 7), (0, width - 4 * rows)))
    part = jnp.concatenate([do, norms], axis=1)
    n = part.shape[0]
    part = pair_sum(grid, "y", part[: n // 2], part[n // 2 :])
    part = pair_sum(grid, "x", part[: n // 4], part[n // 4 :])
    part = ring_sum(grid, [part[d] for d in range(grid.nz)])
    grad_out = part[:rows]
    norms = part[rows, : 4 * rows].reshape(2, 2, rows)

    x_t = rows_in("yxz", x_all)
    grad_q = reduce_rows(grid, x_t[:, :own], dq, "yxz")
    dkv = jnp.concatenate([dk, dv], axis=1)
    grad_kv = reduce_rows(grid, x_t, dkv, "yxz")
    grad_qkv = finish(jnp.concatenate([grad_q, grad_kv], axis=1), half)
    dx = dot_t(dkv, qkv_w[:, half:]).reshape(chips, 2, local, width)
    dx_q = dot_t(dq, qkv_w[:, :half]).reshape(2, local, width)
    theirs = jnp.concatenate([dx[:1, 1] + dx_q[1], dx[1:, 1]], axis=0)
    mine = jnp.concatenate([dx[:1, 0] + dx_q[0], dx[1:, 0]], axis=0)
    part = mine + move("c", theirs.astype(BF)).astype(F32)
    part = pair_sum(grid, "x", part[: chips // 2], part[chips // 2 :])
    part = ring_sum(grid, [part[d] for d in range(grid.nz)])
    grad_input = dr1[:local] + part

    return (
        output,
        grad_input,
        grad_qkv[None],
        grad_out[None],
        grad_gate[None],
        grad_up[None],
        grad_down[None],
        norms[0][None],
        norms[1][None],
    )


def solution(mesh):
    grid = Grid(mesh.shape["dp"], mesh.shape["seq"])
    rows = P(AXES, None)
    weight = P(None, AXES, None)
    norm = P(None, None, AXES)
    return jax.shard_map(
        functools.partial(body, grid),
        mesh=mesh,
        in_specs=(rows, P(AXES), P(AXES)) + (weight,) * 5 + (norm,) * 2 + (rows,),
        out_specs=(rows, rows) + (weight,) * 5 + (norm,) * 2,
        check_vma=False,
    )
```

```python
import functools

import jax
import jax.numpy as jnp
import numpy as np
from jax import lax
from jax.experimental import pallas as pl
from jax.experimental.pallas import tpu as pltpu
from jax.sharding import PartitionSpec as P

HEADS = 12
EPS = 1e-05
BASE = 10000.0
AXES = ("dp", "seq")
BF = jnp.bfloat16
F32 = jnp.float32
FAR = -1e30
ONES = 64


ORDERS = {"X": "hx", "Q": "Zyx", "U": "hyx", "G": "xzy", "D": "xz", "d": "xZ", "g": "yzx", "u": "yxz", "q": "yxh", "r": "xyZ", "x": "h"}
STREAMS = "XPQUGDCdguqx"
SEQUENCE = [
    1, 2, 81, 17, 82, 18, 83, -82, 49, 33, -2, 11, 34, -33, -83, 65, 97, -97,
    84, 43, 4, -84, 58, 66, 85, -34, -35, -50, 51, 36, -4, -36, 37, 67, 5, -5,
    -51, 52, -67, 86, 76, 200, -37, 201, 69, 202, 203, -86, 95, -203, -68, -203, -52, -203,
    53, 204, -69, 205, -53, -87, 206, 207, -207, 208, -207, 209, -207, 210, 212, 213, 145, 211,
    129, 113, 214, -113, -145, 114, 115, 146, 177, 178, -177, 124, -114, -115, 147, 161, -146, -116,
    -129, 130, 148, -147, -130, 131, -178, 157, -161, 162, 179, -162, -131, -149, 163, 140, 117, 172,
    -179, 188, -132, -163, 133, -164, -133, 150, 134, 165, -117, -134, 118, -150, -118, -165, -148,
]


def dot(a, b):
    return jnp.dot(a, b, preferred_element_type=F32)


def dot_t(a, b):
    return lax.dot_general(a, b, (((1,), (1,)), ((), ())), preferred_element_type=F32)


def t_dot(a, b):
    return lax.dot_general(a, b, (((0,), (0,)), ((), ())), preferred_element_type=F32)


def lanes(shape):
    return lax.broadcasted_iota(jnp.int32, shape, len(shape) - 1)


def swap_halves(u):
    width = u.shape[-1]
    low = lanes(u.shape) % 64 < 32
    return jnp.where(low, pltpu.roll(u, width - 32, 1), pltpu.roll(u, 32, 1))


def split3(v):
    hi = v.astype(BF).astype(F32)
    rest = v - hi
    mid = rest.astype(BF).astype(F32)
    return hi, mid, rest - mid


def with_units(base, v):
    at = lanes(base.shape)
    hi, mid, low = split3(v)
    return jnp.where(
        at == ONES,
        -hi,
        jnp.where(at == ONES + 1, -mid, jnp.where(at == ONES + 2, -low, base)),
    )


def fill(target, pieces, places, per):
    n = 0
    for piece in pieces:
        for i in range(piece.shape[0]):
            target[pl.ds(pl.multiple_of(places[n] * per, 16), per), :] = piece[i]
            n += 1


def whole(shape):
    return pl.BlockSpec(shape, lambda *_: (0,) * len(shape))


def scalars():
    return pl.BlockSpec(memory_space=pltpu.SMEM)


def params(mib):
    return pltpu.CompilerParams(vmem_limit_bytes=mib << 20)


def like(*shape, dtype=F32):
    return jax.ShapeDtypeStruct(shape, dtype)


def far(*shape, dtype=F32):
    return pltpu.HBM(shape, dtype)


def kept_far(*arrays):
    return [pltpu.with_memory_space_constraint(a, pltpu.HBM) for a in arrays]


def message_kernel(x_ref, ids_ref, mask_ref, out_ref):
    local, width = x_ref.shape
    out_ref[:local] = x_ref[...]
    out_ref[local:] = jnp.zeros((8, width), BF)
    out_ref[local : local + 1, :local] = ids_ref[...].astype(F32).astype(BF)
    out_ref[local + 1 : local + 2, :local] = mask_ref[...].astype(F32).astype(BF)


def make_message(tokens, ids, mask):
    local, width = tokens.shape
    return pl.pallas_call(
        message_kernel,
        out_shape=like(local + 8, width, dtype=BF),
        compiler_params=params(8),
        cost_estimate=pl.CostEstimate(flops=1, bytes_accessed=1, transcendentals=0),
        name="message",
    )(tokens, ids.reshape(1, local), mask.reshape(1, local))


def columns_kernel(me_ref, qkv_ref, up_ref, out_w_ref, gate_ref, gain_ref, bias_ref, mine_ref, theirs_ref):
    c = me_ref[3]
    rows = qkv_ref.shape[1]

    def halves(ref, start, size, to):
        for target, which in ((mine_ref, c), (theirs_ref, 1 - c)):
            at = pl.ds(pl.multiple_of(start + which * size, 128), size)
            target[:, to : to + size] = ref[0, :, at].astype(BF)

    for j in range(3):
        halves(qkv_ref, j * 768, 384, j * 384)
    ff = up_ref.shape[2] // 2
    to = 1152
    halves(up_ref, 0, ff, to)
    halves(out_w_ref, 0, 384, to + ff)
    halves(gate_ref, 0, ff, to + ff + 512)
    for target in (mine_ref, theirs_ref):
        ext = slice(to + ff + 384, to + ff + 512)
        target[:, ext] = jnp.zeros((rows, 128), BF)
        target[0:2, to + ff + 384 : to + ff + 384 + rows] = gain_ref[0].astype(BF)
        target[2:4, to + ff + 384 : to + ff + 384 + rows] = bias_ref[0].astype(BF)


def make_columns(me, qkv, up, out_w, gate, gain, bias):
    rows = qkv.shape[1]
    shape = like(rows, 1152 + up.shape[2] + 512, dtype=BF)
    args = [qkv, up, out_w, gate, gain, bias]
    return pl.pallas_call(
        columns_kernel,
        grid=(1,),
        in_specs=[scalars()] + [whole(a.shape) for a in args],
        out_specs=[whole(shape.shape)] * 2,
        out_shape=[shape] * 2,
        compiler_params=params(12),
        cost_estimate=pl.CostEstimate(flops=1, bytes_accessed=1, transcendentals=0),
        name="columns",
    )(me, *args)


def angle_table(count, stride):
    angle = np.arange(count)[:, None] * float(stride) * BASE ** (-2.0 * (np.arange(128) % 32) / 64)[None, :]
    rest = np.concatenate([np.cos(angle), np.sin(angle)], axis=1)
    parts = []
    for _ in range(3):
        part = rest.astype(jnp.bfloat16)
        parts.append(part)
        rest = rest - part.astype(np.float64)
    return np.concatenate(parts, axis=0)


def rank_kernel(
    me_ref, along_ref, beside_ref, note_a_ref, note_b_ref, fine_ref, coarse_ref,
    t_ref, cos_ref, sin_ref, ext_ref, keep_ref, ext_s, count_s, before_s, *, numbers, coarse,
):
    local = cos_ref.shape[0] // 4
    chips = note_a_ref.shape[0]
    step = pl.program_id(0)
    lane = lanes((local, 128))

    @pl.when(step == 0)
    def _():
        def one(i, _):
            for h, ref in enumerate((note_a_ref, note_b_ref)):
                note = ref[i].astype(F32)[:, :256].T
                own = jnp.where(note[:local, 0:1] == lane.astype(F32), 1.0, 0.0)
                ext = jnp.where(lane < 64, own, jnp.where(lane < ONES + 3, 1.0, 0.0))
                ext_s[2 * i + h] = ext.astype(BF)
                count_s[pl.ds(2 * i + h, 1), :] = jnp.sum(own, axis=0, keepdims=True)
            return 0

        lax.fori_loop(0, chips, one, 0)
        for h, ref in enumerate((note_a_ref, note_b_ref)):
            note = ref[0].astype(F32)[:, :256].T
            keep_ref[h * local : (h + 1) * local] = jnp.broadcast_to(note[:local, 1:2], (local, 128))
        blocks = 2 * chips
        mine = numbers(lax.broadcasted_iota(jnp.int32, (blocks, blocks), 0), me_ref)
        other = numbers(lax.broadcasted_iota(jnp.int32, (blocks, blocks), 1), me_ref)
        before_s[...] = dot(jnp.where(other < mine, 1.0, 0.0).astype(BF), count_s[...].astype(BF))

    x = jnp.concatenate([r[i, :local] for i in range(2) for r in (along_ref, beside_ref)], axis=0)
    t_ref[...] = x.T
    up = lax.broadcasted_iota(jnp.int32, (local, local), 0) > lax.broadcasted_iota(jnp.int32, (local, local), 1)
    up = jnp.where(up, 1.0, 0.0).astype(BF)
    for b in range(4):
        block = 4 * step + b
        ext = ext_s[block]
        rank = dot(up, ext) + before_s[pl.ds(block, 1), :]
        position = jnp.sum(jnp.where(lane < 64, ext.astype(F32) * rank, 0.0), axis=1, keepdims=True)
        high = jnp.floor(position * (1.0 / 64))

        def pick(value, size, table_ref):
            at = lanes((local, 3 * size)) & (size - 1)
            chosen = jnp.where(at.astype(F32) == value, 1.0, 0.0).astype(BF)
            return dot(chosen, table_ref[...])

        low = pick(position - 64 * high, 64, fine_ref)
        high = pick(high, coarse, coarse_ref)
        cos = low[:, :128] * high[:, :128] - low[:, 128:] * high[:, 128:]
        sin = low[:, 128:] * high[:, :128] + low[:, :128] * high[:, 128:]
        rows = slice(b * local, (b + 1) * local)
        cos_ref[rows] = cos
        sin_ref[rows] = jnp.where(lane % 64 < 32, -sin, sin)
        ext_ref[rows] = ext


def rank(me, numbers, along, beside):
    chips, padded, width = along.shape
    local = padded - 8
    count = chips * 2 * local
    step = 4 * local
    coarse = max(64, 1 << (-(-count // 64) - 1).bit_length())
    note = pl.BlockSpec((chips, 8, width), lambda i: (0, local // 8, 0))
    rows = pl.BlockSpec((step, 128), lambda i: (i, 0))
    return pl.pallas_call(
        functools.partial(rank_kernel, numbers=numbers, coarse=coarse),
        grid=(chips // 2,),
        in_specs=[scalars()]
        + [pl.BlockSpec((2, padded, width), lambda i: (i, 0, 0))] * 2
        + [note, note, whole((192, 256)), whole((3 * coarse, 256))],
        out_specs=[pl.BlockSpec((width, step), lambda i: (0, i)), rows, rows, rows, whole((2 * local, 128))],
        out_shape=[
            far(width, count, dtype=BF), far(count, 128), far(count, 128), far(count, 128, dtype=BF),
            like(2 * local, 128),
        ],
        scratch_shapes=[
            pltpu.VMEM((2 * chips, local, 128), BF),
            pltpu.VMEM((2 * chips, 128), F32),
            pltpu.VMEM((2 * chips, 128), F32),
        ],
        compiler_params=params(16),
        cost_estimate=pl.CostEstimate(flops=1, bytes_accessed=1, transcendentals=0),
        name="rank",
    )(
        me, along, beside, along, beside,
        jnp.asarray(angle_table(64, 1)), jnp.asarray(angle_table(coarse, 64)),
    )


def project_kernel(me_ref, *refs, places, per, n):
    pieces = refs[:n]
    along_ref, beside_ref, cos_ref, sin_ref, q_ref, k_ref, v_ref, w_ref = refs[n:]
    local = cos_ref.shape[0] // 4
    first = pl.program_id(0) == 0

    @pl.when(first)
    def _():
        fill(w_ref, pieces, places(me_ref), per)

    x = jnp.concatenate([r[i, :local] for i in range(2) for r in (along_ref, beside_ref)], axis=0)
    cos, sin = cos_ref[...], sin_ref[...]
    kv = dot(x, w_ref[:, 384:])
    for p in range(3):
        at = slice(p * 128, p * 128 + 128)
        u = kv[:, at]
        k_ref[p] = (u * cos + swap_halves(u) * sin).astype(BF)
        v_ref[p] = kv[:, 384 + p * 128 : 512 + p * 128].astype(BF)

    @pl.when(first)
    def _():
        q = dot(x[: 2 * local], w_ref[:, :384])
        for p in range(3):
            at = slice(p * 128, p * 128 + 128)
            u = q[:, at]
            r = (u * cos[: 2 * local] + swap_halves(u) * sin[: 2 * local]).astype(BF)
            q_ref[:, at] = r * jnp.asarray(0.125, BF)


def project(me, pieces, places, per, along, beside, cos, sin):
    chips, padded, width = along.shape
    count = cos.shape[0]
    step = 2 * (count // chips)
    rows = pl.BlockSpec((step, 128), lambda i: (i, 0))
    heads = pl.BlockSpec((3, step, 128), lambda i: (0, i, 0))
    return pl.pallas_call(
        functools.partial(project_kernel, places=places, per=per, n=len(pieces)),
        grid=(chips // 2,),
        in_specs=[scalars()]
        + [whole(p.shape) for p in pieces]
        + [pl.BlockSpec((2, padded, width), lambda i: (i, 0, 0))] * 2
        + [rows] * 2,
        out_specs=[whole((step // 2, 384)), heads, heads, whole((width, 1152))],
        out_shape=[
            far(step // 2, 384, dtype=BF), far(3, count, 128, dtype=BF), far(3, count, 128, dtype=BF),
            far(width, 1152, dtype=BF),
        ],
        compiler_params=params(24),
        cost_estimate=pl.CostEstimate(flops=1, bytes_accessed=1, transcendentals=0),
        name="project",
    )(me, *pieces, along, beside, *kept_far(cos, sin))


def attend_kernel(q_ref, k_ref, v_ref, ext_ref, att_ref, ob_ref, lse_ref, *, chunk):
    keys = k_ref.shape[1]
    q = q_ref[...]
    own = q.shape[0]
    first = lanes(q.shape) < 64
    ext = ext_ref[:own].astype(F32)
    ext = jnp.where(lanes(ext.shape) < 64, (1.0 - ext) * FAR, 0.0).astype(BF)
    parts = []
    for h in range(2):
        qh = jnp.where(first if h == 0 else ~first, q, jnp.zeros_like(q))
        qc = jnp.concatenate([qh, ext], axis=1)
        top = jnp.full((own, 1), FAR, F32)
        acc = jnp.zeros((own, 256), F32)
        for j in range(0, keys, chunk):
            rows = slice(j, j + chunk)
            s = dot_t(qc, jnp.concatenate([k_ref[0, rows], ext_ref[rows]], axis=1))
            above = jnp.maximum(top, jnp.max(s, axis=1, keepdims=True))
            e = jnp.exp(s - above).astype(BF)
            acc = acc * jnp.exp(top - above) + dot(e, jnp.concatenate([v_ref[0, rows], ext_ref[rows]], axis=1))
            top = above
        total = acc[:, 128 + ONES : 129 + ONES]
        parts.append(acc[:, :128] / total)
        lse_ref[h] = with_units(ext.astype(F32), top + jnp.log(total)).astype(BF)
    att = jnp.where(first, parts[0], parts[1])
    att_ref[...] = att
    ob_ref[...] = att.astype(BF)


def attend(q, k, v, ext):
    own = q.shape[0]
    keys = k.shape[1]
    return pl.pallas_call(
        functools.partial(attend_kernel, chunk=512),
        grid=(3,),
        in_specs=[
            pl.BlockSpec((own, 128), lambda p: (0, p)),
            pl.BlockSpec((1, keys, 128), lambda p: (p, 0, 0)),
            pl.BlockSpec((1, keys, 128), lambda p: (p, 0, 0)),
            whole(ext.shape),
        ],
        out_specs=[
            pl.BlockSpec((own, 128), lambda p: (0, p)),
            pl.BlockSpec((own, 128), lambda p: (0, p)),
            pl.BlockSpec((2, own, 128), lambda p: (p, 0, 0)),
        ],
        out_shape=[
            far(own, 384),
            like(own, 384, dtype=BF),
            far(6, own, 128, dtype=BF),
        ],
        compiler_params=params(20 if keys <= 4096 else 60),
        cost_estimate=pl.CostEstimate(
            flops=4 * 6 * own * keys * 256,
            bytes_accessed=3 * keys * 1024,
            transcendentals=6 * own * keys,
        ),
        name="attend",
    )(*kept_far(q, k, v, ext))


def normalize(values):
    average = jnp.mean(values, axis=-1, keepdims=True)
    centred = values - average
    factor = lax.rsqrt(jnp.mean(centred * centred, axis=-1, keepdims=True) + EPS)
    return centred * factor, factor


def norm_back(gradient, normed, factor):
    return factor * (
        gradient
        - jnp.mean(gradient, axis=-1, keepdims=True)
        - normed * jnp.mean(gradient * normed, axis=-1, keepdims=True)
    )


def turned(a):
    half = a.shape[0] // 2
    return jnp.concatenate([a[half:], a[:half]], axis=0)


def silu_parts(gate):
    sigmoid = 1.0 / (1.0 + jnp.exp(-gate))
    return sigmoid, gate * sigmoid


def mid_kernel(me_ref, *refs, places, per, n, share_rows):
    pieces = refs[:n]
    ob_ref, got_ref, sib_ref, along_ref, beside_ref = refs[n : n + 5]
    n1_ref, f1_ref, h1_ref, up_ref, all_ref, out_ref, up_w_ref, norm_ref = refs[n + 5 :]
    local = along_ref.shape[1] - 8
    c = me_ref[3]
    ff = up_ref.shape[1]
    at = places(me_ref)
    done = 0
    norm = jnp.zeros(norm_ref.shape, F32)
    width = norm.shape[1]
    for piece in pieces:
        for i in range(piece.shape[0]):
            rows = pl.ds(pl.multiple_of(at[done] * per, 16), per)
            for d in range(per // share_rows):
                ext = piece[i, d * share_rows : d * share_rows + 4, ff + 384 : ff + 512].astype(F32)
                ext = jnp.concatenate([ext, jnp.zeros((4, width - 128), F32)], axis=1)
                ext = jnp.concatenate([ext, jnp.zeros((4, width), F32)], axis=0)
                norm = norm + pltpu.roll(ext, (at[done] * (per // share_rows) + d) * share_rows, 1)
            up_w_ref[rows, :] = piece[i, :, :ff]
            out_ref[c, rows, :] = piece[i, :, ff : ff + 384]
            out_ref[1 - c, rows, :] = sib_ref[done]
            done += 1
    norm_ref[...] = norm
    all_ref[c] = ob_ref[...]
    all_ref[1 - c] = turned(got_ref[...])
    halves = [dot(all_ref[0], out_ref[i, :384]) + dot(all_ref[1], out_ref[i, 384:]) for i in range(2)]
    n1, f1 = normalize(
        jnp.concatenate([along_ref[0, :local], beside_ref[0, :local]], axis=0).astype(F32)
        + jnp.concatenate(halves, axis=1)
    )
    low = (n1 * norm_ref[0:1] + norm_ref[2:3]).astype(BF)
    n1_ref[...] = n1
    f1_ref[...] = jnp.broadcast_to(f1, f1_ref.shape)
    h1_ref[...] = low
    up_ref[...] = dot(low, up_w_ref[...])


def mid(me, pieces, places, per, ob, got, sib, along, beside, ff, share_rows):
    own, width = ob.shape[0], along.shape[2]
    small = [ob, got, sib, along, beside]
    one = pl.BlockSpec((1, *along.shape[1:]), lambda *_: (0, 0, 0))
    return pl.pallas_call(
        functools.partial(mid_kernel, places=places, per=per, n=len(pieces), share_rows=share_rows),
        in_specs=[scalars()]
        + [whole(a.shape) for a in pieces + small[:3]]
        + [one, one],
        out_specs=[
            whole((own, width)), whole((own, 128)), whole((own, width)), whole((own, ff)),
            whole((2, own, 384)), whole((2, width, 384)), whole((width, ff)), whole((8, width)),
        ],
        out_shape=[
            like(own, width), like(own, 128), like(own, width, dtype=BF), like(own, ff),
            like(2, own, 384, dtype=BF), like(2, width, 384, dtype=BF), like(width, ff, dtype=BF), like(8, width),
        ],
        grid=(1,),
        compiler_params=params(22),
        cost_estimate=pl.CostEstimate(flops=2 * own * width * 2304, bytes_accessed=12 << 20, transcendentals=0),
        name="mid",
    )(me, *pieces, *small)


def gate_kernel(me_ref, *refs, places, per, n):
    pieces = refs[:n]
    h1_ref, up_ref, gate_ref, hidden_ref, w_ref = refs[n:]
    fill(w_ref, pieces, places(me_ref), per)
    gate = dot(h1_ref[...], w_ref[...])
    gate_ref[...] = gate
    hidden_ref[...] = (silu_parts(gate)[1] * up_ref[...]).astype(BF)


def gate_up(me, pieces, places, per, h1, up):
    own, ff = up.shape
    width = h1.shape[1]
    return pl.pallas_call(
        functools.partial(gate_kernel, places=places, per=per, n=len(pieces)),
        grid=(1,),
        in_specs=[scalars()] + [whole(a.shape) for a in [*pieces, h1, up]],
        out_specs=[whole((own, ff)), whole((own, ff)), whole((width, ff))],
        out_shape=[like(own, ff), like(own, ff, dtype=BF), like(width, ff, dtype=BF)],
        compiler_params=params(20),
        cost_estimate=pl.CostEstimate(flops=2 * own * width * ff, bytes_accessed=10 << 20, transcendentals=own * ff),
        name="gate_up",
    )(me, *pieces, h1, up)


def down_kernel(me_ref, *refs, places, per, n):
    pieces = refs[:n]
    hidden_ref, part_ref, w_ref = refs[n:]
    fill(w_ref, pieces, places(me_ref), per)
    part_ref[...] = dot(hidden_ref[...], w_ref[...])


def down(me, pieces, places, per, hidden):
    own, ff = hidden.shape
    width = pieces[0].shape[2]
    return pl.pallas_call(
        functools.partial(down_kernel, places=places, per=per, n=len(pieces)),
        grid=(1,),
        in_specs=[scalars()] + [whole(a.shape) for a in [*pieces, hidden]],
        out_specs=[whole((own, width)), whole((ff, width))],
        out_shape=[like(own, width), like(ff, width, dtype=BF)],
        compiler_params=params(14),
        cost_estimate=pl.CostEstimate(flops=2 * own * width * ff, bytes_accessed=8 << 20, transcendentals=0),
        name="down",
    )(me, *pieces, hidden)


def turn_kernel(
    part_ref, got_ref, n1_ref, norm_ref, cot_ref, cot_got_ref, keep_ref, gate_ref, up_ref, gate_w_ref, up_w_ref, down_w_ref,
    out_ref, dr2_ref, dm_ref, dgate_ref, dup_ref, back_ref, sums_ref,
):
    local = out_ref.shape[0]
    h1 = n1_ref[...] * norm_ref[0:1] + norm_ref[2:3]
    n2, f2 = normalize(h1 + part_ref[...] + turned(got_ref[...]))
    keep = keep_ref[:, :1]
    gain = norm_ref[1:2]
    out_ref[...] = ((n2[:local] * gain + norm_ref[3:4]) * keep[:local]).astype(BF)
    masked = jnp.concatenate([cot_ref[...], cot_got_ref[...]], axis=0).astype(F32) * keep
    sums_ref[0:1] = jnp.sum(masked * n2, axis=0, keepdims=True)
    sums_ref[1:2] = jnp.sum(masked, axis=0, keepdims=True)
    sums_ref[2:] = jnp.zeros((6, sums_ref.shape[1]), F32)
    dr2 = norm_back(masked * gain, n2, f2)
    dr2_ref[...] = dr2
    dm = dr2.astype(BF)
    dm_ref[...] = dm
    ff = gate_ref.shape[1]
    step = 512
    back = jnp.zeros(dr2.shape, F32)
    for j in range(0, ff, step):
        at = slice(j, j + step)
        dh = dot_t(dm, down_w_ref[at, :])
        gate = gate_ref[:, at]
        sigmoid, silu = silu_parts(gate)
        dgate = (dh * up_ref[:, at] * sigmoid * (1.0 + gate * (1.0 - sigmoid))).astype(BF)
        dup = (dh * silu).astype(BF)
        dgate_ref[:, at] = dgate
        dup_ref[:, at] = dup
        back = back + dot_t(dgate, gate_w_ref[:, at]) + dot_t(dup, up_w_ref[:, at])
    back_ref[...] = back


def turn(part, got, n1, norm, cot, cot_got, keep, gate, up, gate_w, up_w, down_w):
    own, width = part.shape
    ff = gate.shape[1]
    args = [part, got, n1, norm, cot, cot_got, keep, gate, up, gate_w, up_w, down_w]
    return pl.pallas_call(
        turn_kernel,
        grid=(1,),
        in_specs=[whole(a.shape) for a in args],
        out_specs=[
            whole((own // 2, width)), whole((own, width)), whole((own, width)), whole((own, ff)),
            whole((own, ff)), whole((own, width)), whole((8, width)),
        ],
        out_shape=[
            like(own // 2, width, dtype=BF), like(own, width), like(own, width, dtype=BF),
            like(own, ff, dtype=BF), like(own, ff, dtype=BF), like(own, width), like(8, width),
        ],
        compiler_params=params(34),
        cost_estimate=pl.CostEstimate(flops=6 * own * width * ff, bytes_accessed=20 << 20, transcendentals=own * ff),
        name="turn",
    )(*args)


def back_kernel(me_ref, dr2_ref, part_ref, got_ref, n1_ref, f1_ref, norm_ref, w_ref, dr1_ref, da_ref, dob_ref, sums_ref):
    dh1 = dr2_ref[...] + part_ref[...] + turned(got_ref[...])
    n1 = n1_ref[...]
    sums_ref[0:1] = jnp.sum(dh1 * n1, axis=0, keepdims=True)
    sums_ref[1:2] = jnp.sum(dh1, axis=0, keepdims=True)
    sums_ref[2:] = jnp.zeros((6, n1.shape[1]), F32)
    dr1 = norm_back(dh1 * norm_ref[0:1], n1, f1_ref[:, :1])
    dr1_ref[...] = dr1[: dr1_ref.shape[0]]
    da = dr1.astype(BF)
    da_ref[...] = da
    rows = pl.ds(pl.multiple_of(me_ref[3] * 384, 128), 384)
    dob_ref[...] = (dot_t(da[:, :384], w_ref[0, rows, :]) + dot_t(da[:, 384:], w_ref[1, rows, :])).astype(BF)


def back(me, dr2, part, got, n1, f1, norm, out_w):
    own, width = dr2.shape
    args = [dr2, part, got, n1, f1, norm, out_w]
    return pl.pallas_call(
        back_kernel,
        grid=(1,),
        in_specs=[scalars()] + [whole(a.shape) for a in args],
        out_specs=[whole((own // 2, width)), whole((own, width)), whole((own, 384)), whole((8, width))],
        out_shape=[like(own // 2, width), like(own, width, dtype=BF), like(own, 384, dtype=BF), like(8, width)],
        compiler_params=params(14),
        cost_estimate=pl.CostEstimate(flops=2 * own * width * 384, bytes_accessed=7 << 20, transcendentals=0),
        name="back",
    )(me, *args)


def share(whole_ref, at, per, mine_ref, theirs_ref):
    half = mine_ref.shape[0]
    for i in range(2 * half):
        block = whole_ref[pl.ds(pl.multiple_of(at[i] * per, 16), per), :]
        if i < half:
            mine_ref[i, :, : block.shape[1]] = block
        else:
            theirs_ref[i - half, :, : block.shape[1]] = block.astype(BF)


def grad_kernel(me_ref, left_ref, right_ref, mine_ref, theirs_ref, acc_ref, *, places, per):
    acc_ref[...] = t_dot(left_ref[...], right_ref[...])
    share(acc_ref, places(me_ref), per, mine_ref, theirs_ref)


def grad(me, places, per, left, right):
    own, rows = left.shape
    cols = right.shape[1]
    half = rows // per // 2
    step = 768 if cols % 768 == 0 else cols
    return pl.pallas_call(
        functools.partial(grad_kernel, places=places, per=per),
        grid=(cols // step,),
        in_specs=[scalars(), whole(left.shape), pl.BlockSpec((own, step), lambda j: (0, j))],
        out_specs=[pl.BlockSpec((half, per, step), lambda j: (0, 0, j))] * 2,
        out_shape=[like(half, per, cols), like(half, per, cols, dtype=BF)],
        scratch_shapes=[pltpu.VMEM((rows, step), F32)],
        compiler_params=params(18),
        cost_estimate=pl.CostEstimate(flops=2 * own * rows * cols, bytes_accessed=6 * rows * cols, transcendentals=0),
        name="grad",
    )(me, left, right)


def grad_up_kernel(
    me_ref, h1_ref, dup_ref, ob_ref, da_ref, one_ref, two_ref, mine_ref, theirs_ref, acc_ref, sums_s, *, places, per, share_rows
):
    width, ff = h1_ref.shape[1], dup_ref.shape[1]
    at = places(me_ref)
    acc_ref[:, :ff] = t_dot(h1_ref[...], dup_ref[...])
    columns = pl.ds(pl.multiple_of(me_ref[3] * 384, 128), 384)
    da = da_ref[:, columns]
    acc_ref[:384, ff:] = t_dot(ob_ref[0], da)
    acc_ref[384:, ff:] = t_dot(ob_ref[1], da)
    share(acc_ref, at, per, mine_ref, theirs_ref)
    for j in range(2):
        sums_s[2 * j : 2 * j + 1] = one_ref[j : j + 1]
        sums_s[2 * j + 1 : 2 * j + 2] = two_ref[j : j + 1]
    sums_s[4:] = jnp.zeros((4, width), F32)
    sums = sums_s[...]
    half = mine_ref.shape[0]
    lane = lanes((4, 128))
    for i in range(2 * half):
        ref, k = (mine_ref, i) if i < half else (theirs_ref, i - half)
        ref[k, :, ff + 384 :] = jnp.zeros((per, 128), ref.dtype)
        for d in range(per // share_rows):
            device = at[i] * (per // share_rows) + d
            turn = pltpu.roll(sums, width - device * share_rows, 1)[:4, :128]
            block = jnp.where(lane < share_rows, turn, 0.0)
            ref[k, d * share_rows : d * share_rows + 4, ff + 384 :] = block.astype(ref.dtype)


def grad_up(me, places, per, share_rows, h1, dup, ob_all, da, one, two):
    width, ff = h1.shape[1], dup.shape[1]
    cols = ff + 512
    half = width // per // 2
    args = [h1, dup, ob_all, da, one, two]
    return pl.pallas_call(
        functools.partial(grad_up_kernel, places=places, per=per, share_rows=share_rows),
        grid=(1,),
        in_specs=[scalars()] + [whole(a.shape) for a in args],
        out_specs=[whole((half, per, cols))] * 2,
        out_shape=[like(half, per, cols), like(half, per, cols, dtype=BF)],
        scratch_shapes=[pltpu.VMEM((width, ff + 384), F32), pltpu.VMEM((8, width), F32)],
        compiler_params=params(24),
        cost_estimate=pl.CostEstimate(flops=1, bytes_accessed=1, transcendentals=0),
        name="grad_up",
    )(me, *args)


def attend_back_kernel(
    me_ref, q_ref, lse_ref, d_ref, att_ref, k_ref, v_ref, ext_ref, cos_ref, sin_ref, cosq_ref, sinq_ref, t_ref, w_ref,
    dx_ref, dx_go_ref, dw_ref, dw_go_ref, qc_s, dc_s, dq_s, dkv_s, dw_s, *, places, per,
):
    j = pl.program_id(0)
    own = q_ref.shape[0]
    local = own // 2
    first = lanes((own, 128)) < 64

    @pl.when(j == 0)
    def _():
        for p in range(3):
            at = slice(p * 128, p * 128 + 128)
            q, d = q_ref[:, at], d_ref[:, at]
            prod = d.astype(F32) * att_ref[:, at]
            for h in range(2):
                keep = first if h == 0 else ~first
                rows = slice(h * own, (h + 1) * own)
                qc_s[p, rows, :128] = jnp.where(keep, q, jnp.zeros_like(q))
                qc_s[p, rows, 128:] = lse_ref[2 * p + h]
                dc_s[p, rows, :128] = jnp.where(keep, d, jnp.zeros_like(d))
                delta = jnp.sum(jnp.where(keep, prod, 0.0), axis=1, keepdims=True)
                dc_s[p, rows, 128:] = with_units(jnp.zeros((own, 128), F32), delta).astype(BF)
        dq_s[...] = jnp.zeros_like(dq_s)
        dw_s[...] = jnp.zeros_like(dw_s)

    ext = ext_ref[...]
    for p in range(3):
        k = k_ref[p]
        e = jnp.exp(dot_t(jnp.concatenate([k, ext], axis=1), qc_s[p]))
        ds = (e * dot_t(jnp.concatenate([v_ref[p], ext], axis=1), dc_s[p])).astype(BF)
        dkv_s[:, 384 + p * 128 : 512 + p * 128] = dot(e.astype(BF), dc_s[p, :, :128]).astype(BF)
        dk = dot(ds, qc_s[p, :, :128]).astype(BF).astype(F32)
        dk = dk * cos_ref[...] - swap_halves(dk) * sin_ref[...]
        dkv_s[:, p * 128 : p * 128 + 128] = dk.astype(BF)
        dq_s[p] += t_dot(k, ds)
    dkv = dkv_s[...]
    dw_s[:, 384:] += dot(t_ref[...], dkv)
    dx = dot_t(dkv, w_ref[:, 384:])

    def put(dx):
        for i in range(dx_ref.shape[0]):
            dx_ref[i] = dx[2 * i * local : (2 * i + 1) * local]
            dx_go_ref[i] = dx[(2 * i + 1) * local : (2 * i + 2) * local].astype(BF)

    last = j == pl.num_programs(0) - 1

    @pl.when(~last)
    def _():
        put(dx)

    @pl.when(last)
    def _():
        dqs = []
        for p in range(3):
            t = dq_s[p].T
            dq = jnp.where(first, t[:own], t[own:])
            dq = (dq * 0.125).astype(BF).astype(F32)
            dqs.append((dq * cosq_ref[...] - swap_halves(dq) * sinq_ref[...]).astype(BF))
        dq = jnp.concatenate(dqs, axis=1)
        dw_s[:, :384] = dot(t_ref[:, :own], dq)
        put(jnp.concatenate([dx[:own] + dot_t(dq, w_ref[:, :384]), dx[own:]], axis=0))
        share(dw_s, places(me_ref), per, dw_ref, dw_go_ref)


def attend_back(me, places, per, q, lse, d, att, k, v, ext, cos, sin, t, w):
    own = q.shape[0]
    keys = k.shape[1]
    width = w.shape[0]
    chunk = 2 * own
    steps = keys // chunk
    half = width // per // 2
    return pl.pallas_call(
        functools.partial(attend_back_kernel, places=places, per=per),
        grid=(steps,),
        in_specs=[
            scalars(),
            whole(q.shape),
            whole(lse.shape),
            whole(d.shape),
            whole(att.shape),
            pl.BlockSpec((3, chunk, 128), lambda j: (0, steps - 1 - j, 0)),
            pl.BlockSpec((3, chunk, 128), lambda j: (0, steps - 1 - j, 0)),
            pl.BlockSpec((chunk, 128), lambda j: (steps - 1 - j, 0)),
            pl.BlockSpec((chunk, 128), lambda j: (steps - 1 - j, 0)),
            pl.BlockSpec((chunk, 128), lambda j: (steps - 1 - j, 0)),
            pl.BlockSpec((own, 128), lambda j: (0, 0)),
            pl.BlockSpec((own, 128), lambda j: (0, 0)),
            pl.BlockSpec((width, chunk), lambda j: (0, steps - 1 - j)),
            whole(w.shape),
        ],
        out_specs=[
            pl.BlockSpec((2, own // 2, width), lambda j: (steps - 1 - j, 0, 0)),
            pl.BlockSpec((2, own // 2, width), lambda j: (steps - 1 - j, 0, 0)),
            whole((half, per, 1152)),
            whole((half, per, 1152)),
        ],
        out_shape=[
            like(keys // own, own // 2, width),
            like(keys // own, own // 2, width, dtype=BF),
            like(half, per, 1152),
            like(half, per, 1152, dtype=BF),
        ],
        scratch_shapes=[
            pltpu.VMEM((3, 2 * own, 256), BF),
            pltpu.VMEM((3, 2 * own, 256), BF),
            pltpu.VMEM((3, 128, 2 * own), F32),
            pltpu.VMEM((chunk, 768), BF),
            pltpu.VMEM((width, 1152), F32),
        ],
        compiler_params=params(40),
        cost_estimate=pl.CostEstimate(
            flops=16 * 6 * own * keys * 256,
            bytes_accessed=3 * keys * 1600,
            transcendentals=6 * own * keys,
        ),
        name="attend_back",
    )(me, *kept_far(q, lse), d, *kept_far(att, k, v, ext, cos, sin, cos, sin, t, w))


class Grid:
    def __init__(self, ndp, nseq):
        self.ny, self.nz = ndp, nseq // 4
        self.count = ndp * nseq
        self.ring = [0, 1, 3, 2] if self.nz == 4 else list(range(self.nz))
        self.place = [self.ring.index(z) for z in range(self.nz)]
        step = {z: self.ring[(self.place[z] + 1) % self.nz] for z in range(self.nz)}
        self.across = {
            "c": self.pairs(lambda y, z, x, c: (y, z, x, 1 - c)),
            "x": self.pairs(lambda y, z, x, c: (y, z, 1 - x, c)),
            "y": self.pairs(lambda y, z, x, c: (1 - y, z, x, c)),
            "up": self.pairs(lambda y, z, x, c: (y, step[z], x, c)),
        }
        self.across["down"] = [(b, a) for a, b in self.across["up"]]
        for k in range(1, self.nz):
            by = {z: self.ring[(self.place[z] + k) % self.nz] for z in range(self.nz)}
            self.across[f"up{k}"] = self.pairs(lambda y, z, x, c, by=by: (y, by[z], x, c))
            self.across[f"down{k}"] = [(b, a) for a, b in self.across[f"up{k}"]]
        self.bits = [1 << i for i in range(self.nz.bit_length() - 1)]
        for bit in self.bits:
            self.across[f"z{bit}"] = self.pairs(lambda y, z, x, c, bit=bit: (y, z ^ bit, x, c))
        self.across["spread"] = self.pairs(lambda y, z, x, c: (1 - y, z, x, c) if c == y else None)
        self.across["home"] = self.pairs(lambda y, z, x, c: (1 - y, z, x, c) if c != y else None)
        self.across["give"] = self.pairs(lambda y, z, x, c: (y, z, x, 1 - c) if c == y else None)

    def pairs(self, to):
        def index(y, z, x, c):
            return ((y * self.nz + z) * 2 + x) * 2 + c

        made = []
        for y in range(self.ny):
            for z in range(self.nz):
                for x in range(2):
                    for c in range(2):
                        there = to(y, z, x, c)
                        if there is not None:
                            made.append((index(y, z, x, c), index(*there)))
        return made

    def locate(self):
        s = lax.axis_index("seq")
        self.arrived, self.moved = [], {}
        self.latest, self.streams, self.waiting, self.results = [None, None], {}, {}, {}
        self.y = lax.axis_index("dp")
        self.z, self.x, self.c = s // 4, (s // 2) % 2, s % 2
        return jnp.stack([self.y, self.z, self.x, self.c]).astype(jnp.int32)

    def back_by(self, axis, z, d):
        if axis == "h":
            moved = sum(jnp.where(d & other != 0, bit, 0) for bit, other in zip(self.bits, reversed(self.bits)))
            return z ^ moved
        return self.place_of((self.place_of(z) + self.nz - d) & (self.nz - 1))

    def place_of(self, z):
        return z ^ (z >> 1) if self.nz == 4 else z

    def places(self, order, me):
        size = {"x": 2, "y": self.ny, "z": self.nz, "Z": self.nz, "h": self.nz}
        total = 1
        for axis in order:
            total *= size[axis]
        found = []
        for i in range(total):
            y, z, x = me[0], me[1], me[2]
            for axis in reversed(order):
                d, i = i % size[axis], i // size[axis]
                if d == 0:
                    continue
                if axis == "x":
                    x = 1 - x
                elif axis == "y":
                    y = 1 - y
                elif axis == "h":
                    z = z ^ sum(bit for bit, other in zip(self.bits, reversed(self.bits)) if d & other)
                else:
                    z = self.place_of((self.place_of(z) + self.nz - d) % self.nz)
            if "y" not in order:
                y = 0
            found.append((y * self.nz + z) * 2 + x)
        return found

    def tie(self, arrays):
        tokens = [t for t in self.latest if t is not None] + self.arrived
        self.arrived = []
        if not tokens:
            return list(arrays)
        return list(lax.optimization_barrier((*arrays, *tokens))[: len(arrays)])

    def move(self, way, a):
        a = self.tie([a])[0]
        self.latest[0] = a
        got = self.moved[self.label] = lax.ppermute(a, AXES, self.across[way])
        return got

    def work(self, f, *arrays):
        made = f(*self.tie(arrays))
        self.latest[1] = jax.tree.leaves(made)[0]
        return made

    def advance(self, name, whole_ring):
        while True:
            kind, *what = self.waiting[name]
            value = self.move(*what) if kind == "move" else self.work(*what)
            self.send(name, value)
            if not whole_ring or name not in self.waiting or self.waiting[name][1][0] not in "udz":
                return

    def send(self, name, value):
        try:
            self.waiting[name] = self.streams[name].send(value)
        except StopIteration as stop:
            self.waiting.pop(name, None)
            self.results[name] = stop.value

    def start(self, name, stream):
        self.streams[name] = stream
        self.send(name, None)

    def ways(self, axis):
        return [f"z{bit}" for bit in self.bits] if axis == "h" else [axis]

    def ordered(self, bit, mine, theirs, axis):
        return jnp.where(
            bit == 0,
            jnp.concatenate([mine, theirs], axis=axis),
            jnp.concatenate([theirs, mine], axis=axis),
        )

    def gather(self, shard, order):
        held = [shard[None]]
        for axis in order:
            a = held[0] if len(held) == 1 else jnp.concatenate(held, axis=0)
            if axis == "z":
                held = [a]
                for _ in range(self.nz - 1):
                    held.append((yield "move", "up", held[-1]))
            elif axis == "Z":
                held = [a]
                for k in range(1, self.nz):
                    held.append((yield "move", f"up{k}", a))
            elif axis == "h":
                held = [a]
                for bit in reversed(self.bits):
                    a = held[0] if len(held) == 1 else jnp.concatenate(held, axis=0)
                    held = [a, (yield "move", f"z{bit}", a)]
            else:
                held = [a, (yield "move", axis, a)]
        return held


def sum_blocks(grid, axis, blocks):
    if axis == "z":
        part = blocks[-1]
        for d in range(len(blocks) - 2, -1, -1):
            part = (yield "move", "down", part.astype(BF)).astype(F32) + blocks[d]
        return part
    arrived = []
    for d in range(1, len(blocks)):
        arrived.append((yield "move", f"down{d}", blocks[d].astype(BF)))
    return sum((piece.astype(F32) for piece in arrived), blocks[0])


def halve(grid, ways, part):
    for way in ways:
        n = part.shape[0]
        part = part[: n // 2] + (yield "move", way, part[n // 2 :].astype(BF)).astype(F32)
    return part


def reduce_axes(grid, part, axes):
    for axis in axes:
        if axis in "zZ":
            part = yield from sum_blocks(grid, axis, jnp.split(part, grid.nz))
        else:
            part = yield from halve(grid, grid.ways(axis), part)
    return part[0]


def reduce_shared(grid, mine, theirs, order):
    axis = order[0]
    if axis in "zZ":
        blocks = jnp.split(mine, grid.nz // 2) + jnp.split(theirs, grid.nz // 2)
        part = yield from sum_blocks(grid, axis, blocks)
    else:
        ways = grid.ways(axis)
        part = mine + (yield "move", ways[0], theirs).astype(F32)
        part = yield from halve(grid, ways[1:], part)
    return (yield from reduce_axes(grid, part, order[1:]))


def body(grid, tokens, segment_ids, pad_mask, w_qkv, w_out, w_gate, w_up, w_down, ln_gain, ln_bias, cotangent):
    me = grid.locate()
    y, c = grid.y, grid.c
    local, width = tokens.shape
    own = 2 * local
    chips = grid.nz * 2
    rows = w_qkv.shape[1]
    two = 2 * rows
    down_rows = w_down.shape[1]
    ff = w_gate.shape[2] // 2
    direct = two % 16 == 0

    def tokens_task():
        message = yield "work", make_message, tokens, segment_ids, pad_mask
        along = jnp.concatenate((yield from grid.gather(message, orders["X"])), axis=0)
        return along, (yield "move", "c", along)

    def columns_task():
        mine, theirs = yield "work", functools.partial(make_columns, me), w_qkv, w_up, w_out, w_gate, ln_gain, ln_bias
        return mine, (yield "move", "c", theirs)

    def shard(start, size):
        mine, theirs = grid.results["P"]
        return grid.ordered(c, mine[:, start : start + size], theirs[:, start : start + size], 0)

    def up_task(order):
        pieces = yield from grid.gather(shard(1152, ff + 512), order)
        outs = jnp.concatenate([p[:, :, ff : ff + 384] for p in pieces], axis=0)
        return pieces, (yield "move", "c", outs)

    def down_task(order):
        part = yield "work", lambda w: w.astype(BF), w_down[0]
        part = grid.ordered(c, part, (yield "move", "c", part), 0)
        part = jnp.where(c == y, part, (yield "move", "spread", part))
        return (yield from grid.gather(part, order))

    def cot_task():
        return (yield "move", "c", cotangent)

    def placed(pieces, order):
        per = pieces[0].shape[1]
        at = functools.partial(grid.places, order[::-1])
        if direct:
            return pieces, at, per
        blocks = jnp.concatenate(pieces, axis=0)
        table = jnp.stack(at(me))
        blocks = jnp.zeros_like(blocks).at[table].set(blocks)
        return [blocks.reshape(1, -1, blocks.shape[2])], lambda _: [0], blocks.shape[0] * per

    def numbers(index, me):
        chip, side = index >> 1, index & 1
        order = orders["X"][::-1]
        inner = grid.nz if order[1] != "x" else 2
        d = chip & (inner - 1), chip >> (inner.bit_length() - 1)
        dz, dx = d if order[1] != "x" else d[::-1]
        z = grid.back_by(order.replace("x", ""), me[1], dz)
        return ((z * 2 + (me[2] ^ dx)) << 1) + (me[3] ^ side)

    def shared(made, order, per):
        if direct:
            return made
        blocks = jnp.concatenate([made[0][0], made[1][0].astype(F32)], axis=0)
        blocks = blocks.reshape(-1, per, blocks.shape[1])[jnp.stack(grid.places(order, me))]
        half = blocks.shape[0] // 2
        return blocks[:half], blocks[half:].astype(BF)

    def places_of(order, per, total):
        if direct:
            return functools.partial(grid.places, order), per
        return (lambda _: [0, 1]), total // 2

    def down_grad(made, order):
        per = 2 * down_rows
        part = yield from reduce_shared(grid, *shared(made, order, per), order)
        part = part + (yield "move", "home", part.astype(BF)).astype(F32)
        sent = jnp.where(c == 0, part[down_rows:], part[:down_rows])
        kept = jnp.where(c == 0, part[:down_rows], part[down_rows:])
        return jnp.where(c == y, kept, (yield "move", "give", sent))

    def columns_grad(made, order, cuts):
        part = yield from reduce_shared(grid, *shared(made, order, two), order)
        sent = jnp.where(c == 0, part[rows:], part[:rows])
        kept = jnp.where(c == 0, part[:rows], part[rows:])
        got = yield "move", "c", sent[:, : cuts[-1]]
        return [
            grid.ordered(c, kept[:, i:j], got[:, i:j], 1) for i, j in zip(cuts, cuts[1:])
        ] + [kept[:4, cuts[-1] : cuts[-1] + rows]]

    def input_grad(dx, dx_go, dr1, order):
        part = dx + (yield "move", "c", dx_go).astype(F32)
        part = yield from reduce_axes(grid, part, order)
        return dr1 + part

    orders = ORDERS
    got, start = grid.results, grid.start

    def rank_():
        got["rank"] = grid.work(functools.partial(rank, me, numbers), *got["X"])

    def project_():
        pieces, at, per = placed(got["Q"], orders["Q"])
        got["project"] = grid.work(
            lambda *a: project(me, list(a[:-4]), at, per, *a[-4:]), *pieces, *got["X"], *got["rank"][1:3]
        )

    def attend_():
        q, k, v = got["project"][:3]
        got["attend"] = grid.work(attend, q, k, v, got["rank"][3])

    def ob_move():
        got["ob"] = grid.move("c", got["attend"][1])

    def mid_():
        pieces, out_sib = got["U"]
        if not direct:
            table = jnp.stack(grid.places(orders["U"][::-1], me))
            out_sib = jnp.zeros_like(out_sib).at[table].set(out_sib).reshape(1, width, 384)
        pieces, at, per = placed(pieces, orders["U"])
        args = [got["attend"][1], got["ob"], out_sib, *got["X"]]
        got["mid"] = grid.work(lambda *a: mid(me, list(a[:-5]), at, per, *a[-5:], ff, rows), *pieces, *args)
        got["norm"] = got["mid"][7]

    def gate_():
        pieces, at, per = placed(got["G"], orders["G"])
        h1, up = got["mid"][2:4]
        got["gate"] = grid.work(lambda *a: gate_up(me, list(a[:-2]), at, per, *a[-2:]), *pieces, h1, up)

    def down_():
        pieces, at, per = placed(got["D"], orders["D"])
        got["down"] = grid.work(lambda *a: down(me, list(a[:-1]), at, per, a[-1]), *pieces, got["gate"][1])

    def part_move():
        got["part"] = grid.move("c", got["down"][0])

    def turn_():
        n1, _, _, up, _, _, up_w, _ = got["mid"]
        gate, _, gate_w = got["gate"]
        part, down_w = got["down"]
        got["turn"] = grid.work(
            turn, part, got["part"], n1, got["norm"], cotangent, got["C"], got["rank"][4], gate, up, gate_w, up_w, down_w
        )

    def back_move():
        got["back_part"] = grid.move("c", got["turn"][5])

    def grad_d():
        order = orders["d"]
        at, per = places_of(order, 2 * down_rows, ff)
        made = grid.work(functools.partial(grad, me, at, per), got["gate"][1], got["turn"][2])
        start("d", down_grad(made, order))

    def grad_g():
        order = orders["g"]
        at, per = places_of(order, two, width)
        made = grid.work(functools.partial(grad, me, at, per), got["mid"][2], got["turn"][3])
        start("g", columns_grad(made, order, [0, ff]))

    def back_():
        n1, f1 = got["mid"][:2]
        got["back"] = grid.work(
            functools.partial(back, me), got["turn"][1], got["turn"][5], got["back_part"], n1, f1, got["norm"], got["mid"][5]
        )

    def grad_u():
        order = orders["u"]
        at, per = places_of(order, two, width)
        made = grid.work(
            functools.partial(grad_up, me, at, per, rows),
            got["mid"][2], got["turn"][4], got["mid"][4], got["back"][1], got["back"][3], got["turn"][6],
        )
        start("u", columns_grad(made, order, [0, ff, ff + 384]))

    def attend_back_():
        q, k, v, qkv_w = got["project"]
        x_t, cos, sin, ext = got["rank"][:4]
        att, _, lse = got["attend"]
        order = orders["q"]
        at, per = places_of(order, two, width)
        dx, dx_go, *made = grid.work(
            functools.partial(attend_back, me, at, per), q, lse, got["back"][2], att, k, v, ext, cos, sin, x_t, qkv_w
        )
        start("q", columns_grad(made, order, [0, 384, 768, 1152]))
        start("x", input_grad(dx, dx_go, got["back"][0], "x" + orders["x"][-1]))

    start("X", tokens_task())
    start("P", columns_task())
    later = {
        "Q": lambda: grid.gather(shard(0, 1152), orders["Q"]),
        "U": lambda: up_task(orders["U"]),
        "G": lambda: grid.gather(shard(1152 + ff + 512, ff), orders["G"]),
    }
    start("D", down_task(orders["D"]))
    start("C", cot_task())
    single = [
        rank_, project_, attend_, ob_move, mid_, gate_, down_, part_move, turn_, back_move, grad_d, grad_g,
        back_, grad_u, attend_back_,
    ]
    for code in SEQUENCE:
        if code < 0:
            grid.arrived.append(grid.moved[-code])
            continue
        grid.label = code if code >= 200 else code & ~8
        if code >= 200:
            single[code - 200]()
            continue
        name = STREAMS[code >> 4]
        if name in later:
            start(name, later.pop(name)())
        grid.advance(name, bool(code & 8))
    norms = got["u"][2].reshape(2, 2, rows)
    return (
        got["turn"][0],
        got["x"],
        jnp.concatenate(got["q"][:3], axis=1)[None],
        got["u"][1][None],
        got["g"][0][None],
        got["u"][0][None],
        got["d"][None],
        norms[0][None],
        norms[1][None],
    )


def solution(mesh):
    grid = Grid(mesh.shape["dp"], mesh.shape["seq"])
    rows = P(AXES, None)
    weight = P(None, AXES, None)
    norm = P(None, None, AXES)
    return jax.shard_map(
        functools.partial(body, grid),
        mesh=mesh,
        in_specs=(rows, P(AXES), P(AXES)) + (weight,) * 5 + (norm,) * 2 + (rows,),
        out_specs=(rows, rows) + (weight,) * 5 + (norm,) * 2,
        check_vma=False,
    )
```

```python
import functools

import jax
import jax.numpy as jnp
import numpy as np
from jax import lax
from jax.experimental import pallas as pl
from jax.experimental.pallas import tpu as pltpu
from jax.sharding import PartitionSpec as P

HEADS = 12
EPS = 1e-05
BASE = 10000.0
AXES = ("dp", "seq")
BF = jnp.bfloat16
F32 = jnp.float32
FAR = -1e30
NOTE = 16
ONES = 64


ORDERS = {"X": "hx", "Q": "Zyx", "U": "hyx", "G": "xzy", "D": "xz", "d": "xZ", "g": "yzx", "u": "yxz", "q": "yxh", "r": "xyZ", "x": "h"}
STREAMS = "XPQUGDCdguqx"
SEQUENCE = [
    1, 2, 81, 17, 18, 82, 83, -82, 49, 11, 33, -83, 65, 97, 34, -49, -97, 84,
    43, 4, 58, -50, -84, 66, 85, -34, -35, 51, 36, 37, 67, 5, -36, -4, 52, 86,
    -67, -5, 76, 200, 201, 95, 69, 202, 203, -203, -52, -203, -68, 53, 204, -85, -53, 205,
    206, -87, -69, 207, 208, -207, 209, -207, 212, 213, 145, 210, 211, 129, 113, 214, -145, 114,
    -113, 115, 146, 177, -177, 124, 178, -114, -115, 147, 161, -146, -116, -129, 130, 148, -147, 131,
    -178, 157, 162, 179, -162, -131, -149, 163, -130, 140, 117, 172, -179, 188, 133, -132, -163, 165,
    150, -133, 134, 118, -150, -134, -165, -117, -148,
]


def dot(a, b):
    return jnp.dot(a, b, preferred_element_type=F32)


def dot_t(a, b):
    return lax.dot_general(a, b, (((1,), (1,)), ((), ())), preferred_element_type=F32)


def t_dot(a, b):
    return lax.dot_general(a, b, (((0,), (0,)), ((), ())), preferred_element_type=F32)


def lanes(shape):
    return lax.broadcasted_iota(jnp.int32, shape, len(shape) - 1)


def swap_halves(u):
    width = u.shape[-1]
    low = lanes(u.shape) % 64 < 32
    return jnp.where(low, pltpu.roll(u, width - 32, 1), pltpu.roll(u, 32, 1))


def split3(v):
    hi = v.astype(BF).astype(F32)
    rest = v - hi
    mid = rest.astype(BF).astype(F32)
    return hi, mid, rest - mid


def with_units(base, v):
    at = lanes(base.shape)
    hi, mid, low = split3(v)
    return jnp.where(
        at == ONES,
        -hi,
        jnp.where(at == ONES + 1, -mid, jnp.where(at == ONES + 2, -low, base)),
    )


def fill(target, pieces, places, per):
    n = 0
    for piece in pieces:
        for i in range(piece.shape[0]):
            target[pl.ds(pl.multiple_of(places[n] * per, 16), per), :] = piece[i]
            n += 1


def whole(shape):
    return pl.BlockSpec(shape, lambda *_: (0,) * len(shape))


def scalars():
    return pl.BlockSpec(memory_space=pltpu.SMEM)


def params(mib):
    return pltpu.CompilerParams(vmem_limit_bytes=mib << 20)


def like(*shape, dtype=F32):
    return jax.ShapeDtypeStruct(shape, dtype)


def far(*shape, dtype=F32):
    return pltpu.HBM(shape, dtype)


def kept_far(*arrays):
    return [pltpu.with_memory_space_constraint(a, pltpu.HBM) for a in arrays]


def message_kernel(x_ref, ids_ref, mask_ref, down_ref, out_ref, low_ref, note_s):
    local = x_ref.shape[0]
    note_s[...] = jnp.zeros(note_s.shape, F32)
    note_s[0:1, :local] = ids_ref[...].astype(F32)
    note_s[1:2, :local] = mask_ref[...].astype(F32)
    out_ref[:local] = x_ref[...]
    out_ref[local:] = note_s[...].astype(BF)
    low_ref[...] = down_ref[0].astype(BF)


def make_message(tokens, ids, mask, down):
    local, width = tokens.shape
    args = [tokens, ids.reshape(1, local), mask.reshape(1, local), down]
    return pl.pallas_call(
        message_kernel,
        grid=(1,),
        in_specs=[whole(a.shape) for a in args],
        out_specs=[whole((local + NOTE, width)), whole(down.shape[1:])],
        out_shape=[like(local + NOTE, width, dtype=BF), like(*down.shape[1:], dtype=BF)],
        scratch_shapes=[pltpu.VMEM((NOTE, width), F32)],
        compiler_params=params(8),
        cost_estimate=pl.CostEstimate(flops=1, bytes_accessed=1, transcendentals=0),
        name="message",
    )(*kept_far(*args))


def columns_kernel(me_ref, qkv_ref, up_ref, out_w_ref, gate_ref, gain_ref, bias_ref, mine_ref, theirs_ref, ext_s):
    c = me_ref[3]
    rows = qkv_ref.shape[1]

    def halves(ref, start, size, to):
        for target, which in ((mine_ref, c), (theirs_ref, 1 - c)):
            at = pl.ds(pl.multiple_of(start + which * size, 128), size)
            target[:, to : to + size] = ref[0, :, at].astype(BF)

    for j in range(3):
        halves(qkv_ref, j * 768, 384, j * 384)
    ff = up_ref.shape[2] // 2
    to = 1152
    halves(up_ref, 0, ff, to)
    halves(out_w_ref, 0, 384, to + ff)
    halves(gate_ref, 0, ff, to + ff + 512)
    ext_s[...] = jnp.zeros(ext_s.shape, F32)
    ext_s[0:2, :rows] = gain_ref[0]
    ext_s[2:4, :rows] = bias_ref[0]
    for target in (mine_ref, theirs_ref):
        target[:, to + ff + 384 : to + ff + 512] = ext_s[...].astype(BF)


def make_columns(me, qkv, up, out_w, gate, gain, bias):
    rows = qkv.shape[1]
    shape = like(rows, 1152 + up.shape[2] + 512, dtype=BF)
    args = [qkv, up, out_w, gate, gain, bias]
    return pl.pallas_call(
        columns_kernel,
        grid=(1,),
        in_specs=[scalars()] + [whole(a.shape) for a in args],
        out_specs=[whole(shape.shape)] * 2,
        out_shape=[shape] * 2,
        scratch_shapes=[pltpu.VMEM((rows, 128), F32)],
        compiler_params=params(12),
        cost_estimate=pl.CostEstimate(flops=1, bytes_accessed=1, transcendentals=0),
        name="columns",
    )(me, *kept_far(*args))


def angle_table(count, stride):
    angle = np.arange(count)[:, None] * float(stride) * BASE ** (-2.0 * (np.arange(128) % 32) / 64)[None, :]
    rest = np.concatenate([np.cos(angle), np.sin(angle)], axis=1)
    parts = []
    for _ in range(3):
        part = rest.astype(jnp.bfloat16)
        parts.append(part)
        rest = rest - part.astype(np.float64)
    return np.concatenate(parts, axis=0)


def rank_kernel(
    me_ref, along_ref, beside_ref, note_a_ref, note_b_ref, fine_ref, coarse_ref,
    t_ref, cos_ref, sin_ref, ext_ref, keep_ref, ext_s, count_s, before_s, *, numbers, coarse,
):
    local = cos_ref.shape[0] // 4
    chips = note_a_ref.shape[0]
    step = pl.program_id(0)
    lane = lanes((local, 128))

    @pl.when(step == 0)
    def _():
        def one(i, _):
            for h, ref in enumerate((note_a_ref, note_b_ref)):
                note = ref[i].astype(F32)[:, :256].T
                own = jnp.where(note[:local, 0:1] == lane.astype(F32), 1.0, 0.0)
                ext = jnp.where(lane < 64, own, jnp.where(lane < ONES + 3, 1.0, 0.0))
                ext_s[2 * i + h] = ext.astype(BF)
                count_s[pl.ds(2 * i + h, 1), :] = jnp.sum(own, axis=0, keepdims=True)
            return 0

        lax.fori_loop(0, chips, one, 0)
        for h, ref in enumerate((note_a_ref, note_b_ref)):
            note = ref[0].astype(F32)[:, :256].T
            keep_ref[h * local : (h + 1) * local] = jnp.broadcast_to(note[:local, 1:2], (local, 128))
        blocks = 2 * chips
        mine = numbers(lax.broadcasted_iota(jnp.int32, (blocks, blocks), 0), me_ref)
        other = numbers(lax.broadcasted_iota(jnp.int32, (blocks, blocks), 1), me_ref)
        before_s[...] = dot(jnp.where(other < mine, 1.0, 0.0).astype(BF), count_s[...].astype(BF))

    x = jnp.concatenate([r[i, :local] for i in range(2) for r in (along_ref, beside_ref)], axis=0)
    t_ref[...] = x.T
    up = lax.broadcasted_iota(jnp.int32, (local, local), 0) > lax.broadcasted_iota(jnp.int32, (local, local), 1)
    up = jnp.where(up, 1.0, 0.0).astype(BF)
    for b in range(4):
        block = 4 * step + b
        ext = ext_s[block]
        rank = dot(up, ext) + before_s[pl.ds(block, 1), :]
        position = jnp.sum(jnp.where(lane < 64, ext.astype(F32) * rank, 0.0), axis=1, keepdims=True)
        high = jnp.floor(position * (1.0 / 64))

        def pick(value, size, table_ref):
            at = lanes((local, 3 * size)) & (size - 1)
            chosen = jnp.where(at.astype(F32) == value, 1.0, 0.0).astype(BF)
            return dot(chosen, table_ref[...])

        low = pick(position - 64 * high, 64, fine_ref)
        high = pick(high, coarse, coarse_ref)
        cos = low[:, :128] * high[:, :128] - low[:, 128:] * high[:, 128:]
        sin = low[:, 128:] * high[:, :128] + low[:, :128] * high[:, 128:]
        rows = slice(b * local, (b + 1) * local)
        cos_ref[rows] = cos
        sin_ref[rows] = jnp.where(lane % 64 < 32, -sin, sin)
        ext_ref[rows] = ext


def rank(me, numbers, along, beside):
    chips, padded, width = along.shape
    local = padded - NOTE
    count = chips * 2 * local
    step = 4 * local
    coarse = max(64, 1 << (-(-count // 64) - 1).bit_length())
    note = pl.BlockSpec((chips, NOTE, width), lambda i: (0, local // NOTE, 0))
    rows = pl.BlockSpec((step, 128), lambda i: (i, 0))
    return pl.pallas_call(
        functools.partial(rank_kernel, numbers=numbers, coarse=coarse),
        grid=(chips // 2,),
        in_specs=[scalars()]
        + [pl.BlockSpec((2, padded, width), lambda i: (i, 0, 0))] * 2
        + [note, note, whole((192, 256)), whole((3 * coarse, 256))],
        out_specs=[pl.BlockSpec((width, step), lambda i: (0, i)), rows, rows, rows, whole((2 * local, 128))],
        out_shape=[
            far(width, count, dtype=BF), far(count, 128), far(count, 128), far(count, 128, dtype=BF),
            like(2 * local, 128),
        ],
        scratch_shapes=[
            pltpu.VMEM((2 * chips, local, 128), BF),
            pltpu.VMEM((2 * chips, 128), F32),
            pltpu.VMEM((2 * chips, 128), F32),
        ],
        compiler_params=params(16),
        cost_estimate=pl.CostEstimate(flops=1, bytes_accessed=1, transcendentals=0),
        name="rank",
    )(
        me, along, beside, along, beside,
        jnp.asarray(angle_table(64, 1)), jnp.asarray(angle_table(coarse, 64)),
    )


def project_kernel(me_ref, *refs, places, per, n):
    pieces = refs[:n]
    along_ref, beside_ref, cos_ref, sin_ref, q_ref, k_ref, v_ref, w_ref = refs[n:]
    local = cos_ref.shape[0] // 4
    first = pl.program_id(0) == 0

    @pl.when(first)
    def _():
        fill(w_ref, pieces, places(me_ref), per)

    x = jnp.concatenate([r[i, :local] for i in range(2) for r in (along_ref, beside_ref)], axis=0)
    cos, sin = cos_ref[...], sin_ref[...]
    kv = dot(x, w_ref[:, 384:])
    for p in range(3):
        at = slice(p * 128, p * 128 + 128)
        u = kv[:, at]
        k_ref[p] = (u * cos + swap_halves(u) * sin).astype(BF)
        v_ref[p] = kv[:, 384 + p * 128 : 512 + p * 128].astype(BF)

    @pl.when(first)
    def _():
        q = dot(x[: 2 * local], w_ref[:, :384])
        for p in range(3):
            at = slice(p * 128, p * 128 + 128)
            u = q[:, at]
            r = (u * cos[: 2 * local] + swap_halves(u) * sin[: 2 * local]).astype(BF)
            q_ref[:, at] = r * jnp.asarray(0.125, BF)


def project(me, pieces, places, per, along, beside, cos, sin):
    chips, padded, width = along.shape
    count = cos.shape[0]
    step = 2 * (count // chips)
    rows = pl.BlockSpec((step, 128), lambda i: (i, 0))
    heads = pl.BlockSpec((3, step, 128), lambda i: (0, i, 0))
    return pl.pallas_call(
        functools.partial(project_kernel, places=places, per=per, n=len(pieces)),
        grid=(chips // 2,),
        in_specs=[scalars()]
        + [whole(p.shape) for p in pieces]
        + [pl.BlockSpec((2, padded, width), lambda i: (i, 0, 0))] * 2
        + [rows] * 2,
        out_specs=[whole((step // 2, 384)), heads, heads, whole((width, 1152))],
        out_shape=[
            far(step // 2, 384, dtype=BF), far(3, count, 128, dtype=BF), far(3, count, 128, dtype=BF),
            far(width, 1152, dtype=BF),
        ],
        compiler_params=params(24),
        cost_estimate=pl.CostEstimate(flops=1, bytes_accessed=1, transcendentals=0),
        name="project",
    )(me, *pieces, along, beside, *kept_far(cos, sin))


def attend_kernel(q_ref, k_ref, v_ref, ext_ref, att_ref, ob_ref, lse_ref, *, chunk):
    keys = k_ref.shape[1]
    q = q_ref[...]
    own = q.shape[0]
    first = lanes(q.shape) < 64
    ext = ext_ref[:own].astype(F32)
    ext = jnp.where(lanes(ext.shape) < 64, (1.0 - ext) * FAR, 0.0).astype(BF)
    parts = []
    for h in range(2):
        qh = jnp.where(first if h == 0 else ~first, q, jnp.zeros_like(q))
        qc = jnp.concatenate([qh, ext], axis=1)
        top = jnp.full((own, 1), FAR, F32)
        acc = jnp.zeros((own, 256), F32)
        for j in range(0, keys, chunk):
            rows = slice(j, j + chunk)
            s = dot_t(qc, jnp.concatenate([k_ref[0, rows], ext_ref[rows]], axis=1))
            above = jnp.maximum(top, jnp.max(s, axis=1, keepdims=True))
            e = jnp.exp(s - above).astype(BF)
            acc = acc * jnp.exp(top - above) + dot(e, jnp.concatenate([v_ref[0, rows], ext_ref[rows]], axis=1))
            top = above
        total = acc[:, 128 + ONES : 129 + ONES]
        parts.append(acc[:, :128] / total)
        lse_ref[h] = with_units(ext.astype(F32), top + jnp.log(total)).astype(BF)
    att = jnp.where(first, parts[0], parts[1])
    att_ref[...] = att
    ob_ref[...] = att.astype(BF)


def attend(q, k, v, ext):
    own = q.shape[0]
    keys = k.shape[1]
    return pl.pallas_call(
        functools.partial(attend_kernel, chunk=512),
        grid=(3,),
        in_specs=[
            pl.BlockSpec((own, 128), lambda p: (0, p)),
            pl.BlockSpec((1, keys, 128), lambda p: (p, 0, 0)),
            pl.BlockSpec((1, keys, 128), lambda p: (p, 0, 0)),
            whole(ext.shape),
        ],
        out_specs=[
            pl.BlockSpec((own, 128), lambda p: (0, p)),
            pl.BlockSpec((own, 128), lambda p: (0, p)),
            pl.BlockSpec((2, own, 128), lambda p: (p, 0, 0)),
        ],
        out_shape=[
            far(own, 384),
            like(own, 384, dtype=BF),
            far(6, own, 128, dtype=BF),
        ],
        compiler_params=params(20 if keys <= 4096 else 60),
        cost_estimate=pl.CostEstimate(
            flops=4 * 6 * own * keys * 256,
            bytes_accessed=3 * keys * 1024,
            transcendentals=6 * own * keys,
        ),
        name="attend",
    )(*kept_far(q, k, v, ext))


def normalize(values):
    average = jnp.mean(values, axis=-1, keepdims=True)
    centred = values - average
    factor = lax.rsqrt(jnp.mean(centred * centred, axis=-1, keepdims=True) + EPS)
    return centred * factor, factor


def norm_back(gradient, normed, factor):
    return factor * (
        gradient
        - jnp.mean(gradient, axis=-1, keepdims=True)
        - normed * jnp.mean(gradient * normed, axis=-1, keepdims=True)
    )


def turned(a):
    half = a.shape[0] // 2
    return jnp.concatenate([a[half:], a[:half]], axis=0)


def silu_parts(gate):
    sigmoid = 1.0 / (1.0 + jnp.exp(-gate))
    return sigmoid, gate * sigmoid


def mid_kernel(me_ref, *refs, places, per, n, share_rows):
    pieces = refs[:n]
    ob_ref, got_ref, sib_ref, along_ref, beside_ref = refs[n : n + 5]
    n1_ref, f1_ref, h1_ref, up_ref, all_ref, out_ref, up_w_ref, norm_ref = refs[n + 5 :]
    local = along_ref.shape[1] - NOTE
    c = me_ref[3]
    ff = up_ref.shape[1]
    at = places(me_ref)
    done = 0
    norm = jnp.zeros(norm_ref.shape, F32)
    width = norm.shape[1]
    for piece in pieces:
        for i in range(piece.shape[0]):
            rows = pl.ds(pl.multiple_of(at[done] * per, 16), per)
            block = piece[i, :, ff + 384 : ff + 512].astype(F32)
            for d in range(per // share_rows):
                ext = jnp.concatenate([block[d * share_rows :][:4], jnp.zeros((4, 128), F32)], axis=0)
                ext = jnp.concatenate([ext, jnp.zeros((8, width - 128), F32)], axis=1)
                norm = norm + pltpu.roll(ext, (at[done] * (per // share_rows) + d) * share_rows, 1)
            up_w_ref[rows, :] = piece[i, :, :ff]
            out_ref[c, rows, :] = piece[i, :, ff : ff + 384]
            out_ref[1 - c, rows, :] = sib_ref[done]
            done += 1
    norm_ref[...] = norm
    all_ref[c] = ob_ref[...]
    all_ref[1 - c] = turned(got_ref[...])
    halves = [dot(all_ref[0], out_ref[i, :384]) + dot(all_ref[1], out_ref[i, 384:]) for i in range(2)]
    n1, f1 = normalize(
        jnp.concatenate([along_ref[0, :local], beside_ref[0, :local]], axis=0).astype(F32)
        + jnp.concatenate(halves, axis=1)
    )
    low = (n1 * norm_ref[0:1] + norm_ref[2:3]).astype(BF)
    n1_ref[...] = n1
    f1_ref[...] = jnp.broadcast_to(f1, f1_ref.shape)
    h1_ref[...] = low
    up_ref[...] = dot(low, up_w_ref[...])


def mid(me, pieces, places, per, ob, got, sib, along, beside, ff, share_rows):
    own, width = ob.shape[0], along.shape[2]
    small = [ob, got, sib, along, beside]
    one = pl.BlockSpec((1, *along.shape[1:]), lambda *_: (0, 0, 0))
    return pl.pallas_call(
        functools.partial(mid_kernel, places=places, per=per, n=len(pieces), share_rows=share_rows),
        in_specs=[scalars()]
        + [whole(a.shape) for a in pieces + small[:3]]
        + [one, one],
        out_specs=[
            whole((own, width)), whole((own, 128)), whole((own, width)), whole((own, ff)),
            whole((2, own, 384)), whole((2, width, 384)), whole((width, ff)), whole((8, width)),
        ],
        out_shape=[
            like(own, width), like(own, 128), like(own, width, dtype=BF), like(own, ff),
            like(2, own, 384, dtype=BF), like(2, width, 384, dtype=BF), like(width, ff, dtype=BF), like(8, width),
        ],
        grid=(1,),
        compiler_params=params(22),
        cost_estimate=pl.CostEstimate(flops=2 * own * width * 2304, bytes_accessed=12 << 20, transcendentals=0),
        name="mid",
    )(me, *pieces, *small)


def gate_kernel(me_ref, *refs, places, per, n):
    pieces = refs[:n]
    h1_ref, up_ref, gate_ref, hidden_ref, w_ref = refs[n:]
    fill(w_ref, pieces, places(me_ref), per)
    gate = dot(h1_ref[...], w_ref[...])
    gate_ref[...] = gate
    hidden_ref[...] = (silu_parts(gate)[1] * up_ref[...]).astype(BF)


def gate_up(me, pieces, places, per, h1, up):
    own, ff = up.shape
    width = h1.shape[1]
    return pl.pallas_call(
        functools.partial(gate_kernel, places=places, per=per, n=len(pieces)),
        grid=(1,),
        in_specs=[scalars()] + [whole(a.shape) for a in [*pieces, h1, up]],
        out_specs=[whole((own, ff)), whole((own, ff)), whole((width, ff))],
        out_shape=[like(own, ff), like(own, ff, dtype=BF), like(width, ff, dtype=BF)],
        compiler_params=params(20),
        cost_estimate=pl.CostEstimate(flops=2 * own * width * ff, bytes_accessed=10 << 20, transcendentals=own * ff),
        name="gate_up",
    )(me, *pieces, h1, up)


def down_kernel(me_ref, *refs, places, per, n):
    pieces = refs[:n]
    hidden_ref, part_ref, w_ref = refs[n:]
    fill(w_ref, pieces, places(me_ref), per)
    part_ref[...] = dot(hidden_ref[...], w_ref[...])


def down(me, pieces, places, per, hidden):
    own, ff = hidden.shape
    width = pieces[0].shape[2]
    return pl.pallas_call(
        functools.partial(down_kernel, places=places, per=per, n=len(pieces)),
        grid=(1,),
        in_specs=[scalars()] + [whole(a.shape) for a in [*pieces, hidden]],
        out_specs=[whole((own, width)), whole((ff, width))],
        out_shape=[like(own, width), like(ff, width, dtype=BF)],
        compiler_params=params(14),
        cost_estimate=pl.CostEstimate(flops=2 * own * width * ff, bytes_accessed=8 << 20, transcendentals=0),
        name="down",
    )(me, *pieces, hidden)


def turn_kernel(
    part_ref, got_ref, n1_ref, norm_ref, cot_ref, cot_got_ref, keep_ref, gate_ref, up_ref, gate_w_ref, up_w_ref, down_w_ref,
    out_ref, dr2_ref, dm_ref, dgate_ref, dup_ref, back_ref, sums_ref,
):
    local = out_ref.shape[0]
    h1 = n1_ref[...] * norm_ref[0:1] + norm_ref[2:3]
    n2, f2 = normalize(h1 + part_ref[...] + turned(got_ref[...]))
    keep = keep_ref[:, :1]
    gain = norm_ref[1:2]
    out_ref[...] = ((n2[:local] * gain + norm_ref[3:4]) * keep[:local]).astype(BF)
    masked = jnp.concatenate([cot_ref[...], cot_got_ref[...]], axis=0).astype(F32) * keep
    sums_ref[0:1] = jnp.sum(masked * n2, axis=0, keepdims=True)
    sums_ref[1:2] = jnp.sum(masked, axis=0, keepdims=True)
    sums_ref[2:] = jnp.zeros((6, sums_ref.shape[1]), F32)
    dr2 = norm_back(masked * gain, n2, f2)
    dr2_ref[...] = dr2
    dm = dr2.astype(BF)
    dm_ref[...] = dm
    ff = gate_ref.shape[1]
    step = 512
    back = jnp.zeros(dr2.shape, F32)
    for j in range(0, ff, step):
        at = slice(j, j + step)
        dh = dot_t(dm, down_w_ref[at, :])
        gate = gate_ref[:, at]
        sigmoid, silu = silu_parts(gate)
        dgate = (dh * up_ref[:, at] * sigmoid * (1.0 + gate * (1.0 - sigmoid))).astype(BF)
        dup = (dh * silu).astype(BF)
        dgate_ref[:, at] = dgate
        dup_ref[:, at] = dup
        back = back + dot_t(dgate, gate_w_ref[:, at]) + dot_t(dup, up_w_ref[:, at])
    back_ref[...] = back


def turn(part, got, n1, norm, cot, cot_got, keep, gate, up, gate_w, up_w, down_w):
    own, width = part.shape
    ff = gate.shape[1]
    args = [part, got, n1, norm, cot, cot_got, keep, gate, up, gate_w, up_w, down_w]
    return pl.pallas_call(
        turn_kernel,
        grid=(1,),
        in_specs=[whole(a.shape) for a in args],
        out_specs=[
            whole((own // 2, width)), whole((own, width)), whole((own, width)), whole((own, ff)),
            whole((own, ff)), whole((own, width)), whole((8, width)),
        ],
        out_shape=[
            like(own // 2, width, dtype=BF), like(own, width), like(own, width, dtype=BF),
            like(own, ff, dtype=BF), like(own, ff, dtype=BF), like(own, width), like(8, width),
        ],
        compiler_params=params(34),
        cost_estimate=pl.CostEstimate(flops=6 * own * width * ff, bytes_accessed=20 << 20, transcendentals=own * ff),
        name="turn",
    )(*args)


def back_kernel(me_ref, dr2_ref, part_ref, got_ref, n1_ref, f1_ref, norm_ref, w_ref, dr1_ref, da_ref, dob_ref, sums_ref):
    dh1 = dr2_ref[...] + part_ref[...] + turned(got_ref[...])
    n1 = n1_ref[...]
    sums_ref[0:1] = jnp.sum(dh1 * n1, axis=0, keepdims=True)
    sums_ref[1:2] = jnp.sum(dh1, axis=0, keepdims=True)
    sums_ref[2:] = jnp.zeros((6, n1.shape[1]), F32)
    dr1 = norm_back(dh1 * norm_ref[0:1], n1, f1_ref[:, :1])
    dr1_ref[...] = dr1[: dr1_ref.shape[0]]
    da = dr1.astype(BF)
    da_ref[...] = da
    rows = pl.ds(pl.multiple_of(me_ref[3] * 384, 128), 384)
    dob_ref[...] = (dot_t(da[:, :384], w_ref[0, rows, :]) + dot_t(da[:, 384:], w_ref[1, rows, :])).astype(BF)


def back(me, dr2, part, got, n1, f1, norm, out_w):
    own, width = dr2.shape
    args = [dr2, part, got, n1, f1, norm, out_w]
    return pl.pallas_call(
        back_kernel,
        grid=(1,),
        in_specs=[scalars()] + [whole(a.shape) for a in args],
        out_specs=[whole((own // 2, width)), whole((own, width)), whole((own, 384)), whole((8, width))],
        out_shape=[like(own // 2, width), like(own, width, dtype=BF), like(own, 384, dtype=BF), like(8, width)],
        compiler_params=params(14),
        cost_estimate=pl.CostEstimate(flops=2 * own * width * 384, bytes_accessed=7 << 20, transcendentals=0),
        name="back",
    )(me, *args)


def share(whole_ref, at, per, mine_ref, theirs_ref):
    half = mine_ref.shape[0]
    for i in range(2 * half):
        block = whole_ref[pl.ds(pl.multiple_of(at[i] * per, 16), per), :]
        if i < half:
            mine_ref[i, :, : block.shape[1]] = block
        else:
            theirs_ref[i - half, :, : block.shape[1]] = block.astype(BF)


def grad_kernel(me_ref, left_ref, right_ref, mine_ref, theirs_ref, acc_ref, *, places, per):
    acc_ref[...] = t_dot(left_ref[...], right_ref[...])
    share(acc_ref, places(me_ref), per, mine_ref, theirs_ref)


def grad(me, places, per, left, right):
    own, rows = left.shape
    cols = right.shape[1]
    half = rows // per // 2
    step = 768 if cols % 768 == 0 else cols
    return pl.pallas_call(
        functools.partial(grad_kernel, places=places, per=per),
        grid=(cols // step,),
        in_specs=[scalars(), whole(left.shape), pl.BlockSpec((own, step), lambda j: (0, j))],
        out_specs=[pl.BlockSpec((half, per, step), lambda j: (0, 0, j))] * 2,
        out_shape=[like(half, per, cols), like(half, per, cols, dtype=BF)],
        scratch_shapes=[pltpu.VMEM((rows, step), F32)],
        compiler_params=params(18),
        cost_estimate=pl.CostEstimate(flops=2 * own * rows * cols, bytes_accessed=6 * rows * cols, transcendentals=0),
        name="grad",
    )(me, left, right)


def grad_up_kernel(
    me_ref, h1_ref, dup_ref, ob_ref, da_ref, one_ref, two_ref, mine_ref, theirs_ref, acc_ref, sums_s, *, places, per, share_rows
):
    width, ff = h1_ref.shape[1], dup_ref.shape[1]
    at = places(me_ref)
    acc_ref[:, :ff] = t_dot(h1_ref[...], dup_ref[...])
    columns = pl.ds(pl.multiple_of(me_ref[3] * 384, 128), 384)
    da = da_ref[:, columns]
    acc_ref[:384, ff:] = t_dot(ob_ref[0], da)
    acc_ref[384:, ff:] = t_dot(ob_ref[1], da)
    share(acc_ref, at, per, mine_ref, theirs_ref)
    for j in range(2):
        sums_s[2 * j : 2 * j + 1] = one_ref[j : j + 1]
        sums_s[2 * j + 1 : 2 * j + 2] = two_ref[j : j + 1]
    sums_s[4:] = jnp.zeros((4, width), F32)
    sums = sums_s[...]
    half = mine_ref.shape[0]
    lane = lanes((4, 128))
    for i in range(2 * half):
        ref, k = (mine_ref, i) if i < half else (theirs_ref, i - half)
        blocks = []
        for d in range(per // share_rows):
            device = at[i] * (per // share_rows) + d
            turn = pltpu.roll(sums, width - device * share_rows, 1)[:4, :128]
            blocks += [jnp.where(lane < share_rows, turn, 0.0), jnp.zeros((share_rows - 4, 128), F32)]
        ref[k, :, ff + 384 :] = jnp.concatenate(blocks, axis=0).astype(ref.dtype)


def grad_up(me, places, per, share_rows, h1, dup, ob_all, da, one, two):
    width, ff = h1.shape[1], dup.shape[1]
    cols = ff + 512
    half = width // per // 2
    args = [h1, dup, ob_all, da, one, two]
    return pl.pallas_call(
        functools.partial(grad_up_kernel, places=places, per=per, share_rows=share_rows),
        grid=(1,),
        in_specs=[scalars()] + [whole(a.shape) for a in args],
        out_specs=[whole((half, per, cols))] * 2,
        out_shape=[like(half, per, cols), like(half, per, cols, dtype=BF)],
        scratch_shapes=[pltpu.VMEM((width, ff + 384), F32), pltpu.VMEM((8, width), F32)],
        compiler_params=params(24),
        cost_estimate=pl.CostEstimate(flops=1, bytes_accessed=1, transcendentals=0),
        name="grad_up",
    )(me, *args)


def attend_back_kernel(
    me_ref, q_ref, lse_ref, d_ref, att_ref, k_ref, v_ref, ext_ref, cos_ref, sin_ref, cosq_ref, sinq_ref, t_ref, w_ref,
    dx_ref, dx_go_ref, dw_ref, dw_go_ref, qc_s, dc_s, dq_s, dkv_s, dw_s, *, places, per,
):
    j = pl.program_id(0)
    own = q_ref.shape[0]
    local = own // 2
    first = lanes((own, 128)) < 64

    @pl.when(j == 0)
    def _():
        for p in range(3):
            at = slice(p * 128, p * 128 + 128)
            q, d = q_ref[:, at], d_ref[:, at]
            prod = d.astype(F32) * att_ref[:, at]
            for h in range(2):
                keep = first if h == 0 else ~first
                rows = slice(h * own, (h + 1) * own)
                qc_s[p, rows, :128] = jnp.where(keep, q, jnp.zeros_like(q))
                qc_s[p, rows, 128:] = lse_ref[2 * p + h]
                dc_s[p, rows, :128] = jnp.where(keep, d, jnp.zeros_like(d))
                delta = jnp.sum(jnp.where(keep, prod, 0.0), axis=1, keepdims=True)
                dc_s[p, rows, 128:] = with_units(jnp.zeros((own, 128), F32), delta).astype(BF)
        dq_s[...] = jnp.zeros_like(dq_s)
        dw_s[...] = jnp.zeros_like(dw_s)

    ext = ext_ref[...]
    for p in range(3):
        k = k_ref[p]
        e = jnp.exp(dot_t(jnp.concatenate([k, ext], axis=1), qc_s[p]))
        ds = (e * dot_t(jnp.concatenate([v_ref[p], ext], axis=1), dc_s[p])).astype(BF)
        dkv_s[:, 384 + p * 128 : 512 + p * 128] = dot(e.astype(BF), dc_s[p, :, :128]).astype(BF)
        dk = dot(ds, qc_s[p, :, :128]).astype(BF).astype(F32)
        dk = dk * cos_ref[...] - swap_halves(dk) * sin_ref[...]
        dkv_s[:, p * 128 : p * 128 + 128] = dk.astype(BF)
        dq_s[p] += t_dot(k, ds)
    dkv = dkv_s[...]
    dw_s[:, 384:] += dot(t_ref[...], dkv)
    dx = dot_t(dkv, w_ref[:, 384:])

    def put(dx):
        for i in range(dx_ref.shape[0]):
            dx_ref[i] = dx[2 * i * local : (2 * i + 1) * local]
            dx_go_ref[i] = dx[(2 * i + 1) * local : (2 * i + 2) * local].astype(BF)

    last = j == pl.num_programs(0) - 1

    @pl.when(~last)
    def _():
        put(dx)

    @pl.when(last)
    def _():
        dqs = []
        for p in range(3):
            t = dq_s[p].T
            dq = jnp.where(first, t[:own], t[own:])
            dq = (dq * 0.125).astype(BF).astype(F32)
            dqs.append((dq * cosq_ref[...] - swap_halves(dq) * sinq_ref[...]).astype(BF))
        dq = jnp.concatenate(dqs, axis=1)
        dw_s[:, :384] = dot(t_ref[:, :own], dq)
        put(jnp.concatenate([dx[:own] + dot_t(dq, w_ref[:, :384]), dx[own:]], axis=0))
        share(dw_s, places(me_ref), per, dw_ref, dw_go_ref)


def attend_back(me, places, per, q, lse, d, att, k, v, ext, cos, sin, t, w):
    own = q.shape[0]
    keys = k.shape[1]
    width = w.shape[0]
    chunk = 2 * own
    steps = keys // chunk
    half = width // per // 2
    return pl.pallas_call(
        functools.partial(attend_back_kernel, places=places, per=per),
        grid=(steps,),
        in_specs=[
            scalars(),
            whole(q.shape),
            whole(lse.shape),
            whole(d.shape),
            whole(att.shape),
            pl.BlockSpec((3, chunk, 128), lambda j: (0, steps - 1 - j, 0)),
            pl.BlockSpec((3, chunk, 128), lambda j: (0, steps - 1 - j, 0)),
            pl.BlockSpec((chunk, 128), lambda j: (steps - 1 - j, 0)),
            pl.BlockSpec((chunk, 128), lambda j: (steps - 1 - j, 0)),
            pl.BlockSpec((chunk, 128), lambda j: (steps - 1 - j, 0)),
            pl.BlockSpec((own, 128), lambda j: (0, 0)),
            pl.BlockSpec((own, 128), lambda j: (0, 0)),
            pl.BlockSpec((width, chunk), lambda j: (0, steps - 1 - j)),
            whole(w.shape),
        ],
        out_specs=[
            pl.BlockSpec((2, own // 2, width), lambda j: (steps - 1 - j, 0, 0)),
            pl.BlockSpec((2, own // 2, width), lambda j: (steps - 1 - j, 0, 0)),
            whole((half, per, 1152)),
            whole((half, per, 1152)),
        ],
        out_shape=[
            like(keys // own, own // 2, width),
            like(keys // own, own // 2, width, dtype=BF),
            like(half, per, 1152),
            like(half, per, 1152, dtype=BF),
        ],
        scratch_shapes=[
            pltpu.VMEM((3, 2 * own, 256), BF),
            pltpu.VMEM((3, 2 * own, 256), BF),
            pltpu.VMEM((3, 128, 2 * own), F32),
            pltpu.VMEM((chunk, 768), BF),
            pltpu.VMEM((width, 1152), F32),
        ],
        compiler_params=params(40),
        cost_estimate=pl.CostEstimate(
            flops=16 * 6 * own * keys * 256,
            bytes_accessed=3 * keys * 1600,
            transcendentals=6 * own * keys,
        ),
        name="attend_back",
    )(me, *kept_far(q, lse), d, *kept_far(att, k, v, ext, cos, sin, cos, sin, t, w))


class Grid:
    def __init__(self, ndp, nseq):
        self.ny, self.nz = ndp, nseq // 4
        self.count = ndp * nseq
        self.ring = [0, 1, 3, 2] if self.nz == 4 else list(range(self.nz))
        self.place = [self.ring.index(z) for z in range(self.nz)]
        step = {z: self.ring[(self.place[z] + 1) % self.nz] for z in range(self.nz)}
        self.across = {
            "c": self.pairs(lambda y, z, x, c: (y, z, x, 1 - c)),
            "x": self.pairs(lambda y, z, x, c: (y, z, 1 - x, c)),
            "y": self.pairs(lambda y, z, x, c: (1 - y, z, x, c)),
            "up": self.pairs(lambda y, z, x, c: (y, step[z], x, c)),
        }
        self.across["down"] = [(b, a) for a, b in self.across["up"]]
        for k in range(1, self.nz):
            by = {z: self.ring[(self.place[z] + k) % self.nz] for z in range(self.nz)}
            self.across[f"up{k}"] = self.pairs(lambda y, z, x, c, by=by: (y, by[z], x, c))
            self.across[f"down{k}"] = [(b, a) for a, b in self.across[f"up{k}"]]
        self.bits = [1 << i for i in range(self.nz.bit_length() - 1)]
        for bit in self.bits:
            self.across[f"z{bit}"] = self.pairs(lambda y, z, x, c, bit=bit: (y, z ^ bit, x, c))
        self.across["spread"] = self.pairs(lambda y, z, x, c: (1 - y, z, x, c) if c == y else None)
        self.across["home"] = self.pairs(lambda y, z, x, c: (1 - y, z, x, c) if c != y else None)
        self.across["give"] = self.pairs(lambda y, z, x, c: (y, z, x, 1 - c) if c == y else None)

    def pairs(self, to):
        def index(y, z, x, c):
            return ((y * self.nz + z) * 2 + x) * 2 + c

        made = []
        for y in range(self.ny):
            for z in range(self.nz):
                for x in range(2):
                    for c in range(2):
                        there = to(y, z, x, c)
                        if there is not None:
                            made.append((index(y, z, x, c), index(*there)))
        return made

    def locate(self):
        s = lax.axis_index("seq")
        self.arrived, self.moved = [], {}
        self.latest, self.streams, self.waiting, self.results = [None, None], {}, {}, {}
        self.y = lax.axis_index("dp")
        self.z, self.x, self.c = s // 4, (s // 2) % 2, s % 2
        return jnp.stack([self.y, self.z, self.x, self.c]).astype(jnp.int32)

    def back_by(self, axis, z, d):
        if axis == "h":
            moved = sum(jnp.where(d & other != 0, bit, 0) for bit, other in zip(self.bits, reversed(self.bits)))
            return z ^ moved
        return self.place_of((self.place_of(z) + self.nz - d) & (self.nz - 1))

    def place_of(self, z):
        return z ^ (z >> 1) if self.nz == 4 else z

    def places(self, order, me):
        size = {"x": 2, "y": self.ny, "z": self.nz, "Z": self.nz, "h": self.nz}
        total = 1
        for axis in order:
            total *= size[axis]
        found = []
        for i in range(total):
            y, z, x = me[0], me[1], me[2]
            for axis in reversed(order):
                d, i = i % size[axis], i // size[axis]
                if d == 0:
                    continue
                if axis == "x":
                    x = 1 - x
                elif axis == "y":
                    y = 1 - y
                elif axis == "h":
                    z = z ^ sum(bit for bit, other in zip(self.bits, reversed(self.bits)) if d & other)
                else:
                    z = self.place_of((self.place_of(z) + self.nz - d) % self.nz)
            if "y" not in order:
                y = 0
            found.append((y * self.nz + z) * 2 + x)
        return found

    def tie(self, arrays):
        tokens = [t for t in self.latest if t is not None] + self.arrived
        self.arrived = []
        if not tokens:
            return list(arrays)
        return list(lax.optimization_barrier((*arrays, *tokens))[: len(arrays)])

    def move(self, way, a):
        a = self.tie([a])[0]
        self.latest[0] = a
        got = self.moved[self.label] = lax.ppermute(a, AXES, self.across[way])
        return got

    def work(self, f, *arrays):
        made = f(*self.tie(arrays))
        self.latest[1] = jax.tree.leaves(made)[0]
        return made

    def advance(self, name, whole_ring):
        while True:
            kind, *what = self.waiting[name]
            value = self.move(*what) if kind == "move" else self.work(*what)
            self.send(name, value)
            if not whole_ring or name not in self.waiting or self.waiting[name][1][0] not in "udz":
                return

    def send(self, name, value):
        try:
            self.waiting[name] = self.streams[name].send(value)
        except StopIteration as stop:
            self.waiting.pop(name, None)
            self.results[name] = stop.value

    def start(self, name, stream):
        self.streams[name] = stream
        self.send(name, None)

    def ways(self, axis):
        return [f"z{bit}" for bit in self.bits] if axis == "h" else [axis]

    def ordered(self, bit, mine, theirs, axis):
        return jnp.where(
            bit == 0,
            jnp.concatenate([mine, theirs], axis=axis),
            jnp.concatenate([theirs, mine], axis=axis),
        )

    def gather(self, shard, order):
        held = [shard[None]]
        for axis in order:
            a = held[0] if len(held) == 1 else jnp.concatenate(held, axis=0)
            if axis == "z":
                held = [a]
                for _ in range(self.nz - 1):
                    held.append((yield "move", "up", held[-1]))
            elif axis == "Z":
                held = [a]
                for k in range(1, self.nz):
                    held.append((yield "move", f"up{k}", a))
            elif axis == "h":
                held = [a]
                for bit in reversed(self.bits):
                    a = held[0] if len(held) == 1 else jnp.concatenate(held, axis=0)
                    held = [a, (yield "move", f"z{bit}", a)]
            else:
                held = [a, (yield "move", axis, a)]
        return held


def sum_blocks(grid, axis, blocks):
    if axis == "z":
        part = blocks[-1]
        for d in range(len(blocks) - 2, -1, -1):
            part = (yield "move", "down", part.astype(BF)).astype(F32) + blocks[d]
        return part
    arrived = []
    for d in range(1, len(blocks)):
        arrived.append((yield "move", f"down{d}", blocks[d].astype(BF)))
    return sum((piece.astype(F32) for piece in arrived), blocks[0])


def halve(grid, ways, part):
    for way in ways:
        n = part.shape[0]
        part = part[: n // 2] + (yield "move", way, part[n // 2 :].astype(BF)).astype(F32)
    return part


def reduce_axes(grid, part, axes):
    for axis in axes:
        if axis in "zZ":
            part = yield from sum_blocks(grid, axis, jnp.split(part, grid.nz))
        else:
            part = yield from halve(grid, grid.ways(axis), part)
    return part[0]


def reduce_shared(grid, mine, theirs, order):
    axis = order[0]
    if axis in "zZ":
        blocks = jnp.split(mine, grid.nz // 2) + jnp.split(theirs, grid.nz // 2)
        part = yield from sum_blocks(grid, axis, blocks)
    else:
        ways = grid.ways(axis)
        part = mine + (yield "move", ways[0], theirs).astype(F32)
        part = yield from halve(grid, ways[1:], part)
    return (yield from reduce_axes(grid, part, order[1:]))


def body(grid, tokens, segment_ids, pad_mask, w_qkv, w_out, w_gate, w_up, w_down, ln_gain, ln_bias, cotangent):
    me = grid.locate()
    y, c = grid.y, grid.c
    local, width = tokens.shape
    own = 2 * local
    chips = grid.nz * 2
    rows = w_qkv.shape[1]
    two = 2 * rows
    down_rows = w_down.shape[1]
    ff = w_gate.shape[2] // 2
    direct = two % 16 == 0

    def tokens_task():
        message, grid.results["down"] = yield "work", make_message, tokens, segment_ids, pad_mask, w_down
        along = jnp.concatenate((yield from grid.gather(message, orders["X"])), axis=0)
        return along, (yield "move", "c", along)

    def columns_task():
        mine, theirs = yield "work", functools.partial(make_columns, me), w_qkv, w_up, w_out, w_gate, ln_gain, ln_bias
        return mine, (yield "move", "c", theirs)

    def shard(start, size):
        mine, theirs = grid.results["P"]
        return grid.ordered(c, mine[:, start : start + size], theirs[:, start : start + size], 0)

    def up_task(order):
        pieces = yield from grid.gather(shard(1152, ff + 512), order)
        outs = jnp.concatenate([p[:, :, ff : ff + 384] for p in pieces], axis=0)
        return pieces, (yield "move", "c", outs)

    def down_task(order):
        part = yield "work", lambda w: w, grid.results["down"]
        part = grid.ordered(c, part, (yield "move", "c", part), 0)
        part = jnp.where(c == y, part, (yield "move", "spread", part))
        return (yield from grid.gather(part, order))

    def cot_task():
        return (yield "move", "c", cotangent)

    def placed(pieces, order):
        per = pieces[0].shape[1]
        at = functools.partial(grid.places, order[::-1])
        if direct:
            return pieces, at, per
        blocks = jnp.concatenate(pieces, axis=0)
        table = jnp.stack(at(me))
        blocks = jnp.zeros_like(blocks).at[table].set(blocks)
        return [blocks.reshape(1, -1, blocks.shape[2])], lambda _: [0], blocks.shape[0] * per

    def numbers(index, me):
        chip, side = index >> 1, index & 1
        order = orders["X"][::-1]
        inner = grid.nz if order[1] != "x" else 2
        d = chip & (inner - 1), chip >> (inner.bit_length() - 1)
        dz, dx = d if order[1] != "x" else d[::-1]
        z = grid.back_by(order.replace("x", ""), me[1], dz)
        return ((z * 2 + (me[2] ^ dx)) << 1) + (me[3] ^ side)

    def shared(made, order, per):
        if direct:
            return made
        blocks = jnp.concatenate([made[0][0], made[1][0].astype(F32)], axis=0)
        blocks = blocks.reshape(-1, per, blocks.shape[1])[jnp.stack(grid.places(order, me))]
        half = blocks.shape[0] // 2
        return blocks[:half], blocks[half:].astype(BF)

    def places_of(order, per, total):
        if direct:
            return functools.partial(grid.places, order), per
        return (lambda _: [0, 1]), total // 2

    def down_grad(made, order):
        per = 2 * down_rows
        part = yield from reduce_shared(grid, *shared(made, order, per), order)
        part = part + (yield "move", "home", part.astype(BF)).astype(F32)
        sent = jnp.where(c == 0, part[down_rows:], part[:down_rows])
        kept = jnp.where(c == 0, part[:down_rows], part[down_rows:])
        return jnp.where(c == y, kept, (yield "move", "give", sent))

    def columns_grad(made, order, cuts):
        part = yield from reduce_shared(grid, *shared(made, order, two), order)
        sent = jnp.where(c == 0, part[rows:], part[:rows])
        kept = jnp.where(c == 0, part[:rows], part[rows:])
        got = yield "move", "c", sent[:, : cuts[-1]]
        return [
            grid.ordered(c, kept[:, i:j], got[:, i:j], 1) for i, j in zip(cuts, cuts[1:])
        ] + [kept[:4, cuts[-1] : cuts[-1] + rows]]

    def input_grad(dx, dx_go, dr1, order):
        part = dx + (yield "move", "c", dx_go).astype(F32)
        part = yield from reduce_axes(grid, part, order)
        return dr1 + part

    orders = ORDERS
    got, start = grid.results, grid.start

    def rank_():
        got["rank"] = grid.work(functools.partial(rank, me, numbers), *got["X"])

    def project_():
        pieces, at, per = placed(got["Q"], orders["Q"])
        got["project"] = grid.work(
            lambda *a: project(me, list(a[:-4]), at, per, *a[-4:]), *pieces, *got["X"], *got["rank"][1:3]
        )

    def attend_():
        q, k, v = got["project"][:3]
        got["attend"] = grid.work(attend, q, k, v, got["rank"][3])

    def ob_move():
        got["ob"] = grid.move("c", got["attend"][1])

    def mid_():
        pieces, out_sib = got["U"]
        if not direct:
            table = jnp.stack(grid.places(orders["U"][::-1], me))
            out_sib = jnp.zeros_like(out_sib).at[table].set(out_sib).reshape(1, width, 384)
        pieces, at, per = placed(pieces, orders["U"])
        args = [got["attend"][1], got["ob"], out_sib, *got["X"]]
        got["mid"] = grid.work(lambda *a: mid(me, list(a[:-5]), at, per, *a[-5:], ff, rows), *pieces, *args)
        got["norm"] = got["mid"][7]

    def gate_():
        pieces, at, per = placed(got["G"], orders["G"])
        h1, up = got["mid"][2:4]
        got["gate"] = grid.work(lambda *a: gate_up(me, list(a[:-2]), at, per, *a[-2:]), *pieces, h1, up)

    def down_():
        pieces, at, per = placed(got["D"], orders["D"])
        got["down"] = grid.work(lambda *a: down(me, list(a[:-1]), at, per, a[-1]), *pieces, got["gate"][1])

    def part_move():
        got["part"] = grid.move("c", got["down"][0])

    def turn_():
        n1, _, _, up, _, _, up_w, _ = got["mid"]
        gate, _, gate_w = got["gate"]
        part, down_w = got["down"]
        got["turn"] = grid.work(
            turn, part, got["part"], n1, got["norm"], cotangent, got["C"], got["rank"][4], gate, up, gate_w, up_w, down_w
        )

    def back_move():
        got["back_part"] = grid.move("c", got["turn"][5])

    def grad_d():
        order = orders["d"]
        at, per = places_of(order, 2 * down_rows, ff)
        made = grid.work(functools.partial(grad, me, at, per), got["gate"][1], got["turn"][2])
        start("d", down_grad(made, order))

    def grad_g():
        order = orders["g"]
        at, per = places_of(order, two, width)
        made = grid.work(functools.partial(grad, me, at, per), got["mid"][2], got["turn"][3])
        start("g", columns_grad(made, order, [0, ff]))

    def back_():
        n1, f1 = got["mid"][:2]
        got["back"] = grid.work(
            functools.partial(back, me), got["turn"][1], got["turn"][5], got["back_part"], n1, f1, got["norm"], got["mid"][5]
        )

    def grad_u():
        order = orders["u"]
        at, per = places_of(order, two, width)
        made = grid.work(
            functools.partial(grad_up, me, at, per, rows),
            got["mid"][2], got["turn"][4], got["mid"][4], got["back"][1], got["back"][3], got["turn"][6],
        )
        start("u", columns_grad(made, order, [0, ff, ff + 384]))

    def attend_back_():
        q, k, v, qkv_w = got["project"]
        x_t, cos, sin, ext = got["rank"][:4]
        att, _, lse = got["attend"]
        order = orders["q"]
        at, per = places_of(order, two, width)
        dx, dx_go, *made = grid.work(
            functools.partial(attend_back, me, at, per), q, lse, got["back"][2], att, k, v, ext, cos, sin, x_t, qkv_w
        )
        start("q", columns_grad(made, order, [0, 384, 768, 1152]))
        start("x", input_grad(dx, dx_go, got["back"][0], "x" + orders["x"][-1]))

    start("X", tokens_task())
    start("P", columns_task())
    later = {
        "D": lambda: down_task(orders["D"]),
        "Q": lambda: grid.gather(shard(0, 1152), orders["Q"]),
        "U": lambda: up_task(orders["U"]),
        "G": lambda: grid.gather(shard(1152 + ff + 512, ff), orders["G"]),
    }
    start("C", cot_task())
    single = [
        rank_, project_, attend_, ob_move, mid_, gate_, down_, part_move, turn_, back_move, grad_d, grad_g,
        back_, grad_u, attend_back_,
    ]
    for code in SEQUENCE:
        if code < 0:
            grid.arrived.append(grid.moved[-code])
            continue
        grid.label = code if code >= 200 else code & ~8
        if code >= 200:
            single[code - 200]()
            continue
        name = STREAMS[code >> 4]
        if name in later:
            start(name, later.pop(name)())
        grid.advance(name, bool(code & 8))
    norms = got["u"][2].reshape(2, 2, rows)
    return (
        got["turn"][0],
        got["x"],
        jnp.concatenate(got["q"][:3], axis=1)[None],
        got["u"][1][None],
        got["g"][0][None],
        got["u"][0][None],
        got["d"][None],
        norms[0][None],
        norms[1][None],
    )


def solution(mesh):
    grid = Grid(mesh.shape["dp"], mesh.shape["seq"])
    rows = P(AXES, None)
    weight = P(None, AXES, None)
    norm = P(None, None, AXES)
    return jax.shard_map(
        functools.partial(body, grid),
        mesh=mesh,
        in_specs=(rows, P(AXES), P(AXES)) + (weight,) * 5 + (norm,) * 2 + (rows,),
        out_specs=(rows, rows) + (weight,) * 5 + (norm,) * 2,
        check_vma=False,
    )
```

```python
import functools

import jax
import jax.numpy as jnp
import numpy as np
from jax import lax
from jax.experimental import pallas as pl
from jax.experimental.pallas import tpu as pltpu
from jax.sharding import PartitionSpec as P

HEADS = 12
EPS = 1e-05
BASE = 10000.0
AXES = ("dp", "seq")
BF = jnp.bfloat16
F32 = jnp.float32
FAR = -1e30
NOTE = 16
ONES = 64


ORDERS = {"X": "zx", "x": "Z", "Q": "zxy", "U": "xzy", "G": "hyx", "D": "zx", "d": "zx", "g": "yxZ", "u": "xyz", "q": "yxz"}
STREAMS = "XPQUGDCdguqx"
SEQUENCE = [
    1, 17, 18, -18, 33, 65, 81, 49, 34, 82, 2, -49, 43, 74, -33, -34, 83, -2,
    3, -65, -35, 36, 50, 67, -36, 12, -66, -83, 37, -50, 51, -4, 5, -3, -67, 68,
    84, -51, 60, -37, -84, 97, 85, -97, -52, 53, -5, 6, -85, -6, 94, 200, -68, -86,
    87, 201, 202, 203, -203, -53, 54, 204, 205, 206, 207, -207, 208, 209, 211, 212, 129, 213,
    145, -54, 210, 113, 214, -113, 161, -209, 130, -145, 114, 146, -130, 131, 177, -129, -114, 123,
    -161, 162, -177, 132, -131, 178, -162, 163, -115, 147, -163, 141, -132, -146, 148, 164, 116, -133,
    -178, -164, 179, -148, 173, 157, -116, 180, 117, 166, -166, 189, 150, -149, -117, 118, 134, -118,
    -134, -180, -150,
]


def dot(a, b):
    return jnp.dot(a, b, preferred_element_type=F32)


def dot_t(a, b):
    return lax.dot_general(a, b, (((1,), (1,)), ((), ())), preferred_element_type=F32)


def t_dot(a, b):
    return lax.dot_general(a, b, (((0,), (0,)), ((), ())), preferred_element_type=F32)


def lanes(shape):
    return lax.broadcasted_iota(jnp.int32, shape, len(shape) - 1)


def swap_halves(u):
    width = u.shape[-1]
    low = lanes(u.shape) % 64 < 32
    return jnp.where(low, pltpu.roll(u, width - 32, 1), pltpu.roll(u, 32, 1))


def split3(v):
    hi = v.astype(BF).astype(F32)
    rest = v - hi
    mid = rest.astype(BF).astype(F32)
    return hi, mid, rest - mid


def with_units(base, v):
    at = lanes(base.shape)
    hi, mid, low = split3(v)
    return jnp.where(
        at == ONES,
        -hi,
        jnp.where(at == ONES + 1, -mid, jnp.where(at == ONES + 2, -low, base)),
    )


def fill(target, pieces, places, per):
    n = 0
    for piece in pieces:
        for i in range(piece.shape[0]):
            target[pl.ds(pl.multiple_of(places[n] * per, 16), per), :] = piece[i]
            n += 1


def whole(shape):
    return pl.BlockSpec(shape, lambda *_: (0,) * len(shape))


def scalars():
    return pl.BlockSpec(memory_space=pltpu.SMEM)


def params(mib):
    return pltpu.CompilerParams(vmem_limit_bytes=mib << 20)


def like(*shape, dtype=F32):
    return jax.ShapeDtypeStruct(shape, dtype)


def far(*shape, dtype=F32):
    return pltpu.HBM(shape, dtype)


def kept_far(*arrays):
    return [pltpu.with_memory_space_constraint(a, pltpu.HBM) for a in arrays]


def message_kernel(x_ref, ids_ref, mask_ref, down_ref, out_ref, low_ref, note_s):
    local = x_ref.shape[0]
    note_s[...] = jnp.zeros(note_s.shape, F32)
    note_s[0:1, :local] = ids_ref[...].astype(F32)
    note_s[1:2, :local] = mask_ref[...].astype(F32)
    out_ref[:local] = x_ref[...]
    out_ref[local:] = note_s[...].astype(BF)
    low_ref[...] = down_ref[0].astype(BF)


def make_message(tokens, ids, mask, down):
    local, width = tokens.shape
    args = [tokens, ids.reshape(1, local), mask.reshape(1, local), down]
    return pl.pallas_call(
        message_kernel,
        grid=(1,),
        in_specs=[whole(a.shape) for a in args],
        out_specs=[whole((local + NOTE, width)), whole(down.shape[1:])],
        out_shape=[like(local + NOTE, width, dtype=BF), like(*down.shape[1:], dtype=BF)],
        scratch_shapes=[pltpu.VMEM((NOTE, width), F32)],
        compiler_params=params(8),
        cost_estimate=pl.CostEstimate(flops=1, bytes_accessed=1, transcendentals=0),
        name="message",
    )(*kept_far(*args))


def columns_kernel(me_ref, qkv_ref, up_ref, out_w_ref, gate_ref, gain_ref, bias_ref, mine_ref, theirs_ref, ext_s):
    c = me_ref[3]
    rows = qkv_ref.shape[1]

    def halves(ref, start, size, to):
        for target, which in ((mine_ref, c), (theirs_ref, 1 - c)):
            at = pl.ds(pl.multiple_of(start + which * size, 128), size)
            target[:, to : to + size] = ref[0, :, at].astype(BF)

    for j in range(3):
        halves(qkv_ref, j * 768, 384, j * 384)
    ff = up_ref.shape[2] // 2
    to = 1152
    halves(up_ref, 0, ff, to)
    halves(out_w_ref, 0, 384, to + ff)
    halves(gate_ref, 0, ff, to + ff + 512)
    ext_s[...] = jnp.zeros(ext_s.shape, F32)
    ext_s[0:2, :rows] = gain_ref[0]
    ext_s[2:4, :rows] = bias_ref[0]
    for target in (mine_ref, theirs_ref):
        target[:, to + ff + 384 : to + ff + 512] = ext_s[...].astype(BF)


def make_columns(me, qkv, up, out_w, gate, gain, bias):
    rows = qkv.shape[1]
    shape = like(rows, 1152 + up.shape[2] + 512, dtype=BF)
    args = [qkv, up, out_w, gate, gain, bias]
    return pl.pallas_call(
        columns_kernel,
        grid=(1,),
        in_specs=[scalars()] + [whole(a.shape) for a in args],
        out_specs=[whole(shape.shape)] * 2,
        out_shape=[shape] * 2,
        scratch_shapes=[pltpu.VMEM((rows, 128), F32)],
        compiler_params=params(12),
        cost_estimate=pl.CostEstimate(flops=1, bytes_accessed=1, transcendentals=0),
        name="columns",
    )(me, *kept_far(*args))


def angle_table(count, stride):
    angle = np.arange(count)[:, None] * float(stride) * BASE ** (-2.0 * (np.arange(128) % 32) / 64)[None, :]
    rest = np.concatenate([np.cos(angle), np.sin(angle)], axis=1)
    parts = []
    for _ in range(3):
        part = rest.astype(jnp.bfloat16)
        parts.append(part)
        rest = rest - part.astype(np.float64)
    return np.concatenate(parts, axis=0)


def rank_kernel(
    me_ref, along_ref, beside_ref, note_a_ref, note_b_ref, fine_ref, coarse_ref,
    t_ref, cos_ref, sin_ref, ext_ref, keep_ref, ext_s, count_s, before_s, *, numbers, coarse,
):
    local = cos_ref.shape[0] // 4
    chips = note_a_ref.shape[0]
    step = pl.program_id(0)
    lane = lanes((local, 128))

    @pl.when(step == 0)
    def _():
        def one(i, _):
            for h, ref in enumerate((note_a_ref, note_b_ref)):
                note = ref[i].astype(F32)[:, :256].T
                own = jnp.where(note[:local, 0:1] == lane.astype(F32), 1.0, 0.0)
                ext = jnp.where(lane < 64, own, jnp.where(lane < ONES + 3, 1.0, 0.0))
                ext_s[2 * i + h] = ext.astype(BF)
                count_s[pl.ds(2 * i + h, 1), :] = jnp.sum(own, axis=0, keepdims=True)
            return 0

        lax.fori_loop(0, chips, one, 0)
        for h, ref in enumerate((note_a_ref, note_b_ref)):
            note = ref[0].astype(F32)[:, :256].T
            keep_ref[h * local : (h + 1) * local] = jnp.broadcast_to(note[:local, 1:2], (local, 128))
        blocks = 2 * chips
        mine = numbers(lax.broadcasted_iota(jnp.int32, (blocks, blocks), 0), me_ref)
        other = numbers(lax.broadcasted_iota(jnp.int32, (blocks, blocks), 1), me_ref)
        before_s[...] = dot(jnp.where(other < mine, 1.0, 0.0).astype(BF), count_s[...].astype(BF))

    x = jnp.concatenate([r[i, :local] for i in range(2) for r in (along_ref, beside_ref)], axis=0)
    t_ref[...] = x.T
    up = lax.broadcasted_iota(jnp.int32, (local, local), 0) > lax.broadcasted_iota(jnp.int32, (local, local), 1)
    up = jnp.where(up, 1.0, 0.0).astype(BF)
    for b in range(4):
        block = 4 * step + b
        ext = ext_s[block]
        rank = dot(up, ext) + before_s[pl.ds(block, 1), :]
        position = jnp.sum(jnp.where(lane < 64, ext.astype(F32) * rank, 0.0), axis=1, keepdims=True)
        high = jnp.floor(position * (1.0 / 64))

        def pick(value, size, table_ref):
            at = lanes((local, 3 * size)) & (size - 1)
            chosen = jnp.where(at.astype(F32) == value, 1.0, 0.0).astype(BF)
            return dot(chosen, table_ref[...])

        low = pick(position - 64 * high, 64, fine_ref)
        high = pick(high, coarse, coarse_ref)
        cos = low[:, :128] * high[:, :128] - low[:, 128:] * high[:, 128:]
        sin = low[:, 128:] * high[:, :128] + low[:, :128] * high[:, 128:]
        rows = slice(b * local, (b + 1) * local)
        cos_ref[rows] = cos
        sin_ref[rows] = jnp.where(lane % 64 < 32, -sin, sin)
        ext_ref[rows] = ext


def rank(me, numbers, along, beside):
    chips, padded, width = along.shape
    local = padded - NOTE
    count = chips * 2 * local
    step = 4 * local
    coarse = max(64, 1 << (-(-count // 64) - 1).bit_length())
    note = pl.BlockSpec((chips, NOTE, width), lambda i: (0, local // NOTE, 0))
    rows = pl.BlockSpec((step, 128), lambda i: (i, 0))
    return pl.pallas_call(
        functools.partial(rank_kernel, numbers=numbers, coarse=coarse),
        grid=(chips // 2,),
        in_specs=[scalars()]
        + [pl.BlockSpec((2, padded, width), lambda i: (i, 0, 0))] * 2
        + [note, note, whole((192, 256)), whole((3 * coarse, 256))],
        out_specs=[pl.BlockSpec((width, step), lambda i: (0, i)), rows, rows, rows, whole((2 * local, 128))],
        out_shape=[
            far(width, count, dtype=BF), far(count, 128), far(count, 128), far(count, 128, dtype=BF),
            like(2 * local, 128),
        ],
        scratch_shapes=[
            pltpu.VMEM((2 * chips, local, 128), BF),
            pltpu.VMEM((2 * chips, 128), F32),
            pltpu.VMEM((2 * chips, 128), F32),
        ],
        compiler_params=params(16),
        cost_estimate=pl.CostEstimate(flops=1, bytes_accessed=1, transcendentals=0),
        name="rank",
    )(
        me, along, beside, along, beside,
        jnp.asarray(angle_table(64, 1)), jnp.asarray(angle_table(coarse, 64)),
    )


def project_kernel(me_ref, *refs, places, per, n):
    pieces = refs[:n]
    along_ref, beside_ref, cos_ref, sin_ref, q_ref, k_ref, v_ref, w_ref = refs[n:]
    local = cos_ref.shape[0] // 4
    first = pl.program_id(0) == 0

    @pl.when(first)
    def _():
        fill(w_ref, pieces, places(me_ref), per)

    x = jnp.concatenate([r[i, :local] for i in range(2) for r in (along_ref, beside_ref)], axis=0)
    cos, sin = cos_ref[...], sin_ref[...]
    kv = dot(x, w_ref[:, 384:])
    for p in range(3):
        at = slice(p * 128, p * 128 + 128)
        u = kv[:, at]
        k_ref[p] = (u * cos + swap_halves(u) * sin).astype(BF)
        v_ref[p] = kv[:, 384 + p * 128 : 512 + p * 128].astype(BF)

    @pl.when(first)
    def _():
        q = dot(x[: 2 * local], w_ref[:, :384])
        for p in range(3):
            at = slice(p * 128, p * 128 + 128)
            u = q[:, at]
            r = (u * cos[: 2 * local] + swap_halves(u) * sin[: 2 * local]).astype(BF)
            q_ref[:, at] = r * jnp.asarray(0.125, BF)


def project(me, pieces, places, per, along, beside, cos, sin):
    chips, padded, width = along.shape
    count = cos.shape[0]
    step = 2 * (count // chips)
    rows = pl.BlockSpec((step, 128), lambda i: (i, 0))
    heads = pl.BlockSpec((3, step, 128), lambda i: (0, i, 0))
    return pl.pallas_call(
        functools.partial(project_kernel, places=places, per=per, n=len(pieces)),
        grid=(chips // 2,),
        in_specs=[scalars()]
        + [whole(p.shape) for p in pieces]
        + [pl.BlockSpec((2, padded, width), lambda i: (i, 0, 0))] * 2
        + [rows] * 2,
        out_specs=[whole((step // 2, 384)), heads, heads, whole((width, 1152))],
        out_shape=[
            far(step // 2, 384, dtype=BF), far(3, count, 128, dtype=BF), far(3, count, 128, dtype=BF),
            far(width, 1152, dtype=BF),
        ],
        compiler_params=params(24),
        cost_estimate=pl.CostEstimate(flops=1, bytes_accessed=1, transcendentals=0),
        name="project",
    )(me, *pieces, along, beside, *kept_far(cos, sin))


def attend_kernel(q_ref, k_ref, v_ref, ext_ref, att_ref, ob_ref, lse_ref, *, chunk):
    keys = k_ref.shape[1]
    q = q_ref[...]
    own = q.shape[0]
    first = lanes(q.shape) < 64
    ext = ext_ref[:own].astype(F32)
    ext = jnp.where(lanes(ext.shape) < 64, (1.0 - ext) * FAR, 0.0).astype(BF)
    parts = []
    for h in range(2):
        qh = jnp.where(first if h == 0 else ~first, q, jnp.zeros_like(q))
        qc = jnp.concatenate([qh, ext], axis=1)
        top = jnp.full((own, 1), FAR, F32)
        acc = jnp.zeros((own, 256), F32)
        for j in range(0, keys, chunk):
            rows = slice(j, j + chunk)
            s = dot_t(qc, jnp.concatenate([k_ref[0, rows], ext_ref[rows]], axis=1))
            above = jnp.maximum(top, jnp.max(s, axis=1, keepdims=True))
            e = jnp.exp(s - above).astype(BF)
            acc = acc * jnp.exp(top - above) + dot(e, jnp.concatenate([v_ref[0, rows], ext_ref[rows]], axis=1))
            top = above
        total = acc[:, 128 + ONES : 129 + ONES]
        parts.append(acc[:, :128] / total)
        lse_ref[h] = with_units(ext.astype(F32), top + jnp.log(total)).astype(BF)
    att = jnp.where(first, parts[0], parts[1])
    att_ref[...] = att
    ob_ref[...] = att.astype(BF)


def attend(q, k, v, ext):
    own = q.shape[0]
    keys = k.shape[1]
    return pl.pallas_call(
        functools.partial(attend_kernel, chunk=512),
        grid=(3,),
        in_specs=[
            pl.BlockSpec((own, 128), lambda p: (0, p)),
            pl.BlockSpec((1, keys, 128), lambda p: (p, 0, 0)),
            pl.BlockSpec((1, keys, 128), lambda p: (p, 0, 0)),
            whole(ext.shape),
        ],
        out_specs=[
            pl.BlockSpec((own, 128), lambda p: (0, p)),
            pl.BlockSpec((own, 128), lambda p: (0, p)),
            pl.BlockSpec((2, own, 128), lambda p: (p, 0, 0)),
        ],
        out_shape=[
            far(own, 384),
            like(own, 384, dtype=BF),
            far(6, own, 128, dtype=BF),
        ],
        compiler_params=params(20 if keys <= 4096 else 60),
        cost_estimate=pl.CostEstimate(
            flops=4 * 6 * own * keys * 256,
            bytes_accessed=3 * keys * 1024,
            transcendentals=6 * own * keys,
        ),
        name="attend",
    )(*kept_far(q, k, v, ext))


def normalize(values):
    average = jnp.mean(values, axis=-1, keepdims=True)
    centred = values - average
    factor = lax.rsqrt(jnp.mean(centred * centred, axis=-1, keepdims=True) + EPS)
    return centred * factor, factor


def norm_back(gradient, normed, factor):
    return factor * (
        gradient
        - jnp.mean(gradient, axis=-1, keepdims=True)
        - normed * jnp.mean(gradient * normed, axis=-1, keepdims=True)
    )


def turned(a):
    half = a.shape[0] // 2
    return jnp.concatenate([a[half:], a[:half]], axis=0)


def silu_parts(gate):
    sigmoid = 1.0 / (1.0 + jnp.exp(-gate))
    return sigmoid, gate * sigmoid


def mid_kernel(me_ref, *refs, places, per, n, share_rows):
    pieces = refs[:n]
    ob_ref, got_ref, sib_ref, along_ref, beside_ref = refs[n : n + 5]
    n1_ref, f1_ref, h1_ref, up_ref, all_ref, out_ref, up_w_ref, norm_ref = refs[n + 5 :]
    local = along_ref.shape[1] - NOTE
    c = me_ref[3]
    ff = up_ref.shape[1]
    at = places(me_ref)
    done = 0
    norm = jnp.zeros(norm_ref.shape, F32)
    width = norm.shape[1]
    for piece in pieces:
        for i in range(piece.shape[0]):
            rows = pl.ds(pl.multiple_of(at[done] * per, 16), per)
            block = piece[i, :, ff + 384 : ff + 512].astype(F32)
            for d in range(per // share_rows):
                ext = jnp.concatenate([block[d * share_rows :][:4], jnp.zeros((4, 128), F32)], axis=0)
                ext = jnp.concatenate([ext, jnp.zeros((8, width - 128), F32)], axis=1)
                norm = norm + pltpu.roll(ext, (at[done] * (per // share_rows) + d) * share_rows, 1)
            up_w_ref[rows, :] = piece[i, :, :ff]
            out_ref[c, rows, :] = piece[i, :, ff : ff + 384]
            out_ref[1 - c, rows, :] = sib_ref[done]
            done += 1
    norm_ref[...] = norm
    all_ref[c] = ob_ref[...]
    all_ref[1 - c] = turned(got_ref[...])
    halves = [dot(all_ref[0], out_ref[i, :384]) + dot(all_ref[1], out_ref[i, 384:]) for i in range(2)]
    n1, f1 = normalize(
        jnp.concatenate([along_ref[0, :local], beside_ref[0, :local]], axis=0).astype(F32)
        + jnp.concatenate(halves, axis=1)
    )
    low = (n1 * norm_ref[0:1] + norm_ref[2:3]).astype(BF)
    n1_ref[...] = n1
    f1_ref[...] = jnp.broadcast_to(f1, f1_ref.shape)
    h1_ref[...] = low
    up_ref[...] = dot(low, up_w_ref[...])


def mid(me, pieces, places, per, ob, got, sib, along, beside, ff, share_rows):
    own, width = ob.shape[0], along.shape[2]
    small = [ob, got, sib, along, beside]
    one = pl.BlockSpec((1, *along.shape[1:]), lambda *_: (0, 0, 0))
    return pl.pallas_call(
        functools.partial(mid_kernel, places=places, per=per, n=len(pieces), share_rows=share_rows),
        in_specs=[scalars()]
        + [whole(a.shape) for a in pieces + small[:3]]
        + [one, one],
        out_specs=[
            whole((own, width)), whole((own, 128)), whole((own, width)), whole((own, ff)),
            whole((2, own, 384)), whole((2, width, 384)), whole((width, ff)), whole((8, width)),
        ],
        out_shape=[
            like(own, width), like(own, 128), like(own, width, dtype=BF), like(own, ff),
            like(2, own, 384, dtype=BF), like(2, width, 384, dtype=BF), like(width, ff, dtype=BF), like(8, width),
        ],
        grid=(1,),
        compiler_params=params(22),
        cost_estimate=pl.CostEstimate(flops=2 * own * width * 2304, bytes_accessed=12 << 20, transcendentals=0),
        name="mid",
    )(me, *pieces, *small)


def gate_kernel(me_ref, *refs, places, per, n):
    pieces = refs[:n]
    h1_ref, up_ref, gate_ref, hidden_ref, w_ref = refs[n:]
    fill(w_ref, pieces, places(me_ref), per)
    gate = dot(h1_ref[...], w_ref[...])
    gate_ref[...] = gate
    hidden_ref[...] = (silu_parts(gate)[1] * up_ref[...]).astype(BF)


def gate_up(me, pieces, places, per, h1, up):
    own, ff = up.shape
    width = h1.shape[1]
    return pl.pallas_call(
        functools.partial(gate_kernel, places=places, per=per, n=len(pieces)),
        grid=(1,),
        in_specs=[scalars()] + [whole(a.shape) for a in [*pieces, h1, up]],
        out_specs=[whole((own, ff)), whole((own, ff)), whole((width, ff))],
        out_shape=[like(own, ff), like(own, ff, dtype=BF), like(width, ff, dtype=BF)],
        compiler_params=params(20),
        cost_estimate=pl.CostEstimate(flops=2 * own * width * ff, bytes_accessed=10 << 20, transcendentals=own * ff),
        name="gate_up",
    )(me, *pieces, h1, up)


def down_kernel(me_ref, *refs, places, per, n):
    pieces = refs[:n]
    hidden_ref, part_ref, w_ref = refs[n:]
    fill(w_ref, pieces, places(me_ref), per)
    part_ref[...] = dot(hidden_ref[...], w_ref[...])


def down(me, pieces, places, per, hidden):
    own, ff = hidden.shape
    width = pieces[0].shape[2]
    return pl.pallas_call(
        functools.partial(down_kernel, places=places, per=per, n=len(pieces)),
        grid=(1,),
        in_specs=[scalars()] + [whole(a.shape) for a in [*pieces, hidden]],
        out_specs=[whole((own, width)), whole((ff, width))],
        out_shape=[like(own, width), like(ff, width, dtype=BF)],
        compiler_params=params(14),
        cost_estimate=pl.CostEstimate(flops=2 * own * width * ff, bytes_accessed=8 << 20, transcendentals=0),
        name="down",
    )(me, *pieces, hidden)


def turn_kernel(
    part_ref, got_ref, n1_ref, norm_ref, cot_ref, cot_got_ref, keep_ref, gate_ref, up_ref, gate_w_ref, up_w_ref, down_w_ref,
    out_ref, dr2_ref, dm_ref, dgate_ref, dup_ref, back_ref, sums_ref,
):
    local = out_ref.shape[0]
    h1 = n1_ref[...] * norm_ref[0:1] + norm_ref[2:3]
    n2, f2 = normalize(h1 + part_ref[...] + turned(got_ref[...]))
    keep = keep_ref[:, :1]
    gain = norm_ref[1:2]
    out_ref[...] = ((n2[:local] * gain + norm_ref[3:4]) * keep[:local]).astype(BF)
    masked = jnp.concatenate([cot_ref[...], cot_got_ref[...]], axis=0).astype(F32) * keep
    sums_ref[0:1] = jnp.sum(masked * n2, axis=0, keepdims=True)
    sums_ref[1:2] = jnp.sum(masked, axis=0, keepdims=True)
    sums_ref[2:] = jnp.zeros((6, sums_ref.shape[1]), F32)
    dr2 = norm_back(masked * gain, n2, f2)
    dr2_ref[...] = dr2
    dm = dr2.astype(BF)
    dm_ref[...] = dm
    ff = gate_ref.shape[1]
    step = 512
    back = jnp.zeros(dr2.shape, F32)
    for j in range(0, ff, step):
        at = slice(j, j + step)
        dh = dot_t(dm, down_w_ref[at, :])
        gate = gate_ref[:, at]
        sigmoid, silu = silu_parts(gate)
        dgate = (dh * up_ref[:, at] * sigmoid * (1.0 + gate * (1.0 - sigmoid))).astype(BF)
        dup = (dh * silu).astype(BF)
        dgate_ref[:, at] = dgate
        dup_ref[:, at] = dup
        back = back + dot_t(dgate, gate_w_ref[:, at]) + dot_t(dup, up_w_ref[:, at])
    back_ref[...] = back


def turn(part, got, n1, norm, cot, cot_got, keep, gate, up, gate_w, up_w, down_w):
    own, width = part.shape
    ff = gate.shape[1]
    args = [part, got, n1, norm, cot, cot_got, keep, gate, up, gate_w, up_w, down_w]
    return pl.pallas_call(
        turn_kernel,
        grid=(1,),
        in_specs=[whole(a.shape) for a in args],
        out_specs=[
            whole((own // 2, width)), whole((own, width)), whole((own, width)), whole((own, ff)),
            whole((own, ff)), whole((own, width)), whole((8, width)),
        ],
        out_shape=[
            like(own // 2, width, dtype=BF), like(own, width), like(own, width, dtype=BF),
            like(own, ff, dtype=BF), like(own, ff, dtype=BF), like(own, width), like(8, width),
        ],
        compiler_params=params(34),
        cost_estimate=pl.CostEstimate(flops=6 * own * width * ff, bytes_accessed=20 << 20, transcendentals=own * ff),
        name="turn",
    )(*args)


def back_kernel(me_ref, dr2_ref, part_ref, got_ref, n1_ref, f1_ref, norm_ref, w_ref, dr1_ref, da_ref, dob_ref, sums_ref):
    dh1 = dr2_ref[...] + part_ref[...] + turned(got_ref[...])
    n1 = n1_ref[...]
    sums_ref[0:1] = jnp.sum(dh1 * n1, axis=0, keepdims=True)
    sums_ref[1:2] = jnp.sum(dh1, axis=0, keepdims=True)
    sums_ref[2:] = jnp.zeros((6, n1.shape[1]), F32)
    dr1 = norm_back(dh1 * norm_ref[0:1], n1, f1_ref[:, :1])
    dr1_ref[...] = dr1[: dr1_ref.shape[0]]
    da = dr1.astype(BF)
    da_ref[...] = da
    rows = pl.ds(pl.multiple_of(me_ref[3] * 384, 128), 384)
    dob_ref[...] = (dot_t(da[:, :384], w_ref[0, rows, :]) + dot_t(da[:, 384:], w_ref[1, rows, :])).astype(BF)


def back(me, dr2, part, got, n1, f1, norm, out_w):
    own, width = dr2.shape
    args = [dr2, part, got, n1, f1, norm, out_w]
    return pl.pallas_call(
        back_kernel,
        grid=(1,),
        in_specs=[scalars()] + [whole(a.shape) for a in args],
        out_specs=[whole((own // 2, width)), whole((own, width)), whole((own, 384)), whole((8, width))],
        out_shape=[like(own // 2, width), like(own, width, dtype=BF), like(own, 384, dtype=BF), like(8, width)],
        compiler_params=params(14),
        cost_estimate=pl.CostEstimate(flops=2 * own * width * 384, bytes_accessed=7 << 20, transcendentals=0),
        name="back",
    )(me, *args)


def share(whole_ref, at, per, mine_ref, theirs_ref):
    half = mine_ref.shape[0]
    for i in range(2 * half):
        block = whole_ref[pl.ds(pl.multiple_of(at[i] * per, 16), per), :]
        if i < half:
            mine_ref[i, :, : block.shape[1]] = block
        else:
            theirs_ref[i - half, :, : block.shape[1]] = block.astype(BF)


def grad_kernel(me_ref, left_ref, right_ref, mine_ref, theirs_ref, acc_ref, *, places, per):
    acc_ref[...] = t_dot(left_ref[...], right_ref[...])
    share(acc_ref, places(me_ref), per, mine_ref, theirs_ref)


def grad(me, places, per, left, right):
    own, rows = left.shape
    cols = right.shape[1]
    half = rows // per // 2
    step = 768 if cols % 768 == 0 else cols
    return pl.pallas_call(
        functools.partial(grad_kernel, places=places, per=per),
        grid=(cols // step,),
        in_specs=[scalars(), whole(left.shape), pl.BlockSpec((own, step), lambda j: (0, j))],
        out_specs=[pl.BlockSpec((half, per, step), lambda j: (0, 0, j))] * 2,
        out_shape=[like(half, per, cols), like(half, per, cols, dtype=BF)],
        scratch_shapes=[pltpu.VMEM((rows, step), F32)],
        compiler_params=params(18),
        cost_estimate=pl.CostEstimate(flops=2 * own * rows * cols, bytes_accessed=6 * rows * cols, transcendentals=0),
        name="grad",
    )(me, left, right)


def grad_up_kernel(
    me_ref, h1_ref, dup_ref, ob_ref, da_ref, one_ref, two_ref, mine_ref, theirs_ref, acc_ref, sums_s, *, places, per, share_rows
):
    width, ff = h1_ref.shape[1], dup_ref.shape[1]
    at = places(me_ref)
    acc_ref[:, :ff] = t_dot(h1_ref[...], dup_ref[...])
    columns = pl.ds(pl.multiple_of(me_ref[3] * 384, 128), 384)
    da = da_ref[:, columns]
    acc_ref[:384, ff:] = t_dot(ob_ref[0], da)
    acc_ref[384:, ff:] = t_dot(ob_ref[1], da)
    share(acc_ref, at, per, mine_ref, theirs_ref)
    for j in range(2):
        sums_s[2 * j : 2 * j + 1] = one_ref[j : j + 1]
        sums_s[2 * j + 1 : 2 * j + 2] = two_ref[j : j + 1]
    sums_s[4:] = jnp.zeros((4, width), F32)
    sums = sums_s[...]
    half = mine_ref.shape[0]
    lane = lanes((4, 128))
    for i in range(2 * half):
        ref, k = (mine_ref, i) if i < half else (theirs_ref, i - half)
        blocks = []
        for d in range(per // share_rows):
            device = at[i] * (per // share_rows) + d
            turn = pltpu.roll(sums, width - device * share_rows, 1)[:4, :128]
            blocks += [jnp.where(lane < share_rows, turn, 0.0), jnp.zeros((share_rows - 4, 128), F32)]
        ref[k, :, ff + 384 :] = jnp.concatenate(blocks, axis=0).astype(ref.dtype)


def grad_up(me, places, per, share_rows, h1, dup, ob_all, da, one, two):
    width, ff = h1.shape[1], dup.shape[1]
    cols = ff + 512
    half = width // per // 2
    args = [h1, dup, ob_all, da, one, two]
    return pl.pallas_call(
        functools.partial(grad_up_kernel, places=places, per=per, share_rows=share_rows),
        grid=(1,),
        in_specs=[scalars()] + [whole(a.shape) for a in args],
        out_specs=[whole((half, per, cols))] * 2,
        out_shape=[like(half, per, cols), like(half, per, cols, dtype=BF)],
        scratch_shapes=[pltpu.VMEM((width, ff + 384), F32), pltpu.VMEM((8, width), F32)],
        compiler_params=params(24),
        cost_estimate=pl.CostEstimate(flops=1, bytes_accessed=1, transcendentals=0),
        name="grad_up",
    )(me, *args)


def attend_back_kernel(
    me_ref, q_ref, lse_ref, d_ref, att_ref, k_ref, v_ref, ext_ref, cos_ref, sin_ref, cosq_ref, sinq_ref, t_ref, w_ref,
    dx_ref, dx_go_ref, dw_ref, dw_go_ref, qc_s, dc_s, dq_s, dkv_s, dw_s, *, places, per,
):
    j = pl.program_id(0)
    own = q_ref.shape[0]
    local = own // 2
    first = lanes((own, 128)) < 64

    @pl.when(j == 0)
    def _():
        for p in range(3):
            at = slice(p * 128, p * 128 + 128)
            q, d = q_ref[:, at], d_ref[:, at]
            prod = d.astype(F32) * att_ref[:, at]
            for h in range(2):
                keep = first if h == 0 else ~first
                rows = slice(h * own, (h + 1) * own)
                qc_s[p, rows, :128] = jnp.where(keep, q, jnp.zeros_like(q))
                qc_s[p, rows, 128:] = lse_ref[2 * p + h]
                dc_s[p, rows, :128] = jnp.where(keep, d, jnp.zeros_like(d))
                delta = jnp.sum(jnp.where(keep, prod, 0.0), axis=1, keepdims=True)
                dc_s[p, rows, 128:] = with_units(jnp.zeros((own, 128), F32), delta).astype(BF)
        dq_s[...] = jnp.zeros_like(dq_s)
        dw_s[...] = jnp.zeros_like(dw_s)

    ext = ext_ref[...]
    for p in range(3):
        k = k_ref[p]
        e = jnp.exp(dot_t(jnp.concatenate([k, ext], axis=1), qc_s[p]))
        ds = (e * dot_t(jnp.concatenate([v_ref[p], ext], axis=1), dc_s[p])).astype(BF)
        dkv_s[:, 384 + p * 128 : 512 + p * 128] = dot(e.astype(BF), dc_s[p, :, :128]).astype(BF)
        dk = dot(ds, qc_s[p, :, :128]).astype(BF).astype(F32)
        dk = dk * cos_ref[...] - swap_halves(dk) * sin_ref[...]
        dkv_s[:, p * 128 : p * 128 + 128] = dk.astype(BF)
        dq_s[p] += t_dot(k, ds)
    dkv = dkv_s[...]
    dw_s[:, 384:] += dot(t_ref[...], dkv)
    dx = dot_t(dkv, w_ref[:, 384:])

    def put(dx):
        for i in range(dx_ref.shape[0]):
            dx_ref[i] = dx[2 * i * local : (2 * i + 1) * local]
            dx_go_ref[i] = dx[(2 * i + 1) * local : (2 * i + 2) * local].astype(BF)

    last = j == pl.num_programs(0) - 1

    @pl.when(~last)
    def _():
        put(dx)

    @pl.when(last)
    def _():
        dqs = []
        for p in range(3):
            t = dq_s[p].T
            dq = jnp.where(first, t[:own], t[own:])
            dq = (dq * 0.125).astype(BF).astype(F32)
            dqs.append((dq * cosq_ref[...] - swap_halves(dq) * sinq_ref[...]).astype(BF))
        dq = jnp.concatenate(dqs, axis=1)
        dw_s[:, :384] = dot(t_ref[:, :own], dq)
        put(jnp.concatenate([dx[:own] + dot_t(dq, w_ref[:, :384]), dx[own:]], axis=0))
        share(dw_s, places(me_ref), per, dw_ref, dw_go_ref)


def attend_back(me, places, per, q, lse, d, att, k, v, ext, cos, sin, t, w):
    own = q.shape[0]
    keys = k.shape[1]
    width = w.shape[0]
    chunk = 2 * own
    steps = keys // chunk
    half = width // per // 2
    return pl.pallas_call(
        functools.partial(attend_back_kernel, places=places, per=per),
        grid=(steps,),
        in_specs=[
            scalars(),
            whole(q.shape),
            whole(lse.shape),
            whole(d.shape),
            whole(att.shape),
            pl.BlockSpec((3, chunk, 128), lambda j: (0, steps - 1 - j, 0)),
            pl.BlockSpec((3, chunk, 128), lambda j: (0, steps - 1 - j, 0)),
            pl.BlockSpec((chunk, 128), lambda j: (steps - 1 - j, 0)),
            pl.BlockSpec((chunk, 128), lambda j: (steps - 1 - j, 0)),
            pl.BlockSpec((chunk, 128), lambda j: (steps - 1 - j, 0)),
            pl.BlockSpec((own, 128), lambda j: (0, 0)),
            pl.BlockSpec((own, 128), lambda j: (0, 0)),
            pl.BlockSpec((width, chunk), lambda j: (0, steps - 1 - j)),
            whole(w.shape),
        ],
        out_specs=[
            pl.BlockSpec((2, own // 2, width), lambda j: (steps - 1 - j, 0, 0)),
            pl.BlockSpec((2, own // 2, width), lambda j: (steps - 1 - j, 0, 0)),
            whole((half, per, 1152)),
            whole((half, per, 1152)),
        ],
        out_shape=[
            like(keys // own, own // 2, width),
            like(keys // own, own // 2, width, dtype=BF),
            like(half, per, 1152),
            like(half, per, 1152, dtype=BF),
        ],
        scratch_shapes=[
            pltpu.VMEM((3, 2 * own, 256), BF),
            pltpu.VMEM((3, 2 * own, 256), BF),
            pltpu.VMEM((3, 128, 2 * own), F32),
            pltpu.VMEM((chunk, 768), BF),
            pltpu.VMEM((width, 1152), F32),
        ],
        compiler_params=params(40),
        cost_estimate=pl.CostEstimate(
            flops=16 * 6 * own * keys * 256,
            bytes_accessed=3 * keys * 1600,
            transcendentals=6 * own * keys,
        ),
        name="attend_back",
    )(me, *kept_far(q, lse), d, *kept_far(att, k, v, ext, cos, sin, cos, sin, t, w))


class Grid:
    def __init__(self, ndp, nseq):
        self.ny, self.nz = ndp, nseq // 4
        self.count = ndp * nseq
        self.ring = [0, 1, 3, 2] if self.nz == 4 else list(range(self.nz))
        self.place = [self.ring.index(z) for z in range(self.nz)]
        step = {z: self.ring[(self.place[z] + 1) % self.nz] for z in range(self.nz)}
        self.across = {
            "c": self.pairs(lambda y, z, x, c: (y, z, x, 1 - c)),
            "x": self.pairs(lambda y, z, x, c: (y, z, 1 - x, c)),
            "y": self.pairs(lambda y, z, x, c: (1 - y, z, x, c)),
            "up": self.pairs(lambda y, z, x, c: (y, step[z], x, c)),
        }
        self.across["down"] = [(b, a) for a, b in self.across["up"]]
        for k in range(1, self.nz):
            by = {z: self.ring[(self.place[z] + k) % self.nz] for z in range(self.nz)}
            self.across[f"up{k}"] = self.pairs(lambda y, z, x, c, by=by: (y, by[z], x, c))
            self.across[f"down{k}"] = [(b, a) for a, b in self.across[f"up{k}"]]
        self.bits = [1 << i for i in range(self.nz.bit_length() - 1)]
        for bit in self.bits:
            self.across[f"z{bit}"] = self.pairs(lambda y, z, x, c, bit=bit: (y, z ^ bit, x, c))
        self.across["spread"] = self.pairs(lambda y, z, x, c: (1 - y, z, x, c) if c == y else None)
        self.across["home"] = self.pairs(lambda y, z, x, c: (1 - y, z, x, c) if c != y else None)
        self.across["give"] = self.pairs(lambda y, z, x, c: (y, z, x, 1 - c) if c == y else None)

    def pairs(self, to):
        def index(y, z, x, c):
            return ((y * self.nz + z) * 2 + x) * 2 + c

        made = []
        for y in range(self.ny):
            for z in range(self.nz):
                for x in range(2):
                    for c in range(2):
                        there = to(y, z, x, c)
                        if there is not None:
                            made.append((index(y, z, x, c), index(*there)))
        return made

    def locate(self):
        s = lax.axis_index("seq")
        self.arrived, self.moved = [], {}
        self.latest, self.streams, self.waiting, self.results = [None, None], {}, {}, {}
        self.y = lax.axis_index("dp")
        self.z, self.x, self.c = s // 4, (s // 2) % 2, s % 2
        return jnp.stack([self.y, self.z, self.x, self.c]).astype(jnp.int32)

    def back_by(self, axis, z, d):
        if axis == "h":
            moved = sum(jnp.where(d & other != 0, bit, 0) for bit, other in zip(self.bits, reversed(self.bits)))
            return z ^ moved
        return self.place_of((self.place_of(z) + self.nz - d) & (self.nz - 1))

    def place_of(self, z):
        return z ^ (z >> 1) if self.nz == 4 else z

    def places(self, order, me):
        size = {"x": 2, "y": self.ny, "z": self.nz, "Z": self.nz, "h": self.nz}
        total = 1
        for axis in order:
            total *= size[axis]
        found = []
        for i in range(total):
            y, z, x = me[0], me[1], me[2]
            for axis in reversed(order):
                d, i = i % size[axis], i // size[axis]
                if d == 0:
                    continue
                if axis == "x":
                    x = 1 - x
                elif axis == "y":
                    y = 1 - y
                elif axis == "h":
                    z = z ^ sum(bit for bit, other in zip(self.bits, reversed(self.bits)) if d & other)
                else:
                    z = self.place_of((self.place_of(z) + self.nz - d) % self.nz)
            if "y" not in order:
                y = 0
            found.append((y * self.nz + z) * 2 + x)
        return found

    def tie(self, arrays):
        tokens = [t for t in self.latest if t is not None] + self.arrived
        self.arrived = []
        if not tokens:
            return list(arrays)
        return list(lax.optimization_barrier((*arrays, *tokens))[: len(arrays)])

    def move(self, way, a):
        a = self.tie([a])[0]
        self.latest[0] = a
        got = self.moved[self.label] = lax.ppermute(a, AXES, self.across[way])
        return got

    def work(self, f, *arrays):
        made = f(*self.tie(arrays))
        self.latest[1] = jax.tree.leaves(made)[0]
        return made

    def advance(self, name, whole_ring):
        while True:
            kind, *what = self.waiting[name]
            value = self.move(*what) if kind == "move" else self.work(*what)
            self.send(name, value)
            if not whole_ring or name not in self.waiting or self.waiting[name][1][0] not in "udz":
                return

    def send(self, name, value):
        try:
            self.waiting[name] = self.streams[name].send(value)
        except StopIteration as stop:
            self.waiting.pop(name, None)
            self.results[name] = stop.value

    def start(self, name, stream):
        self.streams[name] = stream
        self.send(name, None)

    def ways(self, axis):
        return [f"z{bit}" for bit in self.bits] if axis == "h" else [axis]

    def ordered(self, bit, mine, theirs, axis):
        return jnp.where(
            bit == 0,
            jnp.concatenate([mine, theirs], axis=axis),
            jnp.concatenate([theirs, mine], axis=axis),
        )

    def gather(self, shard, order):
        held = [shard[None]]
        for axis in order:
            a = held[0] if len(held) == 1 else jnp.concatenate(held, axis=0)
            if axis == "z":
                held = [a]
                for _ in range(self.nz - 1):
                    held.append((yield "move", "up", held[-1]))
            elif axis == "Z":
                held = [a]
                for k in range(1, self.nz):
                    held.append((yield "move", f"up{k}", a))
            elif axis == "h":
                held = [a]
                for bit in reversed(self.bits):
                    a = held[0] if len(held) == 1 else jnp.concatenate(held, axis=0)
                    held = [a, (yield "move", f"z{bit}", a)]
            else:
                held = [a, (yield "move", axis, a)]
        return held


def sum_blocks(grid, axis, blocks):
    if axis == "z":
        part = blocks[-1]
        for d in range(len(blocks) - 2, -1, -1):
            part = (yield "move", "down", part.astype(BF)).astype(F32) + blocks[d]
        return part
    arrived = []
    for d in range(1, len(blocks)):
        arrived.append((yield "move", f"down{d}", blocks[d].astype(BF)))
    return sum((piece.astype(F32) for piece in arrived), blocks[0])


def halve(grid, ways, part):
    for way in ways:
        n = part.shape[0]
        part = part[: n // 2] + (yield "move", way, part[n // 2 :].astype(BF)).astype(F32)
    return part


def reduce_axes(grid, part, axes):
    for axis in axes:
        if axis in "zZ":
            part = yield from sum_blocks(grid, axis, jnp.split(part, grid.nz))
        else:
            part = yield from halve(grid, grid.ways(axis), part)
    return part[0]


def reduce_shared(grid, mine, theirs, order):
    axis = order[0]
    if axis in "zZ":
        blocks = jnp.split(mine, grid.nz // 2) + jnp.split(theirs, grid.nz // 2)
        part = yield from sum_blocks(grid, axis, blocks)
    else:
        ways = grid.ways(axis)
        part = mine + (yield "move", ways[0], theirs).astype(F32)
        part = yield from halve(grid, ways[1:], part)
    return (yield from reduce_axes(grid, part, order[1:]))


def body(grid, tokens, segment_ids, pad_mask, w_qkv, w_out, w_gate, w_up, w_down, ln_gain, ln_bias, cotangent):
    me = grid.locate()
    y, c = grid.y, grid.c
    local, width = tokens.shape
    own = 2 * local
    chips = grid.nz * 2
    rows = w_qkv.shape[1]
    two = 2 * rows
    down_rows = w_down.shape[1]
    ff = w_gate.shape[2] // 2
    direct = two % 16 == 0

    def tokens_task():
        message, grid.results["low_down"] = yield "work", make_message, tokens, segment_ids, pad_mask, w_down
        along = jnp.concatenate((yield from grid.gather(message, orders["X"])), axis=0)
        return along, (yield "move", "c", along)

    def columns_task():
        mine, theirs = yield "work", functools.partial(make_columns, me), w_qkv, w_up, w_out, w_gate, ln_gain, ln_bias
        return mine, (yield "move", "c", theirs)

    def shard(start, size):
        mine, theirs = grid.results["P"]
        return grid.ordered(c, mine[:, start : start + size], theirs[:, start : start + size], 0)

    def up_task(order):
        pieces = yield from grid.gather(shard(1152, ff + 512), order)
        outs = jnp.concatenate([p[:, :, ff : ff + 384] for p in pieces], axis=0)
        return pieces, (yield "move", "c", outs)

    def down_task(order):
        part = yield "work", lambda w: w, grid.results["low_down"]
        part = grid.ordered(c, part, (yield "move", "c", part), 0)
        part = jnp.where(c == y, part, (yield "move", "spread", part))
        return (yield from grid.gather(part, order))

    def cot_task():
        return (yield "move", "c", cotangent)

    def placed(pieces, order):
        per = pieces[0].shape[1]
        at = functools.partial(grid.places, order[::-1])
        if direct:
            return pieces, at, per
        blocks = jnp.concatenate(pieces, axis=0)
        table = jnp.stack(at(me))
        blocks = jnp.zeros_like(blocks).at[table].set(blocks)
        return [blocks.reshape(1, -1, blocks.shape[2])], lambda _: [0], blocks.shape[0] * per

    def numbers(index, me):
        chip, side = index >> 1, index & 1
        order = orders["X"][::-1]
        inner = grid.nz if order[1] != "x" else 2
        d = chip & (inner - 1), chip >> (inner.bit_length() - 1)
        dz, dx = d if order[1] != "x" else d[::-1]
        z = grid.back_by(order.replace("x", ""), me[1], dz)
        return ((z * 2 + (me[2] ^ dx)) << 1) + (me[3] ^ side)

    def shared(made, order, per):
        if direct:
            return made
        blocks = jnp.concatenate([made[0][0], made[1][0].astype(F32)], axis=0)
        blocks = blocks.reshape(-1, per, blocks.shape[1])[jnp.stack(grid.places(order, me))]
        half = blocks.shape[0] // 2
        return blocks[:half], blocks[half:].astype(BF)

    def places_of(order, per, total):
        if direct:
            return functools.partial(grid.places, order), per
        return (lambda _: [0, 1]), total // 2

    def down_grad(made, order):
        per = 2 * down_rows
        part = yield from reduce_shared(grid, *shared(made, order, per), order)
        part = part + (yield "move", "home", part.astype(BF)).astype(F32)
        sent = jnp.where(c == 0, part[down_rows:], part[:down_rows])
        kept = jnp.where(c == 0, part[:down_rows], part[down_rows:])
        return jnp.where(c == y, kept, (yield "move", "give", sent))

    def columns_grad(made, order, cuts):
        part = yield from reduce_shared(grid, *shared(made, order, two), order)
        sent = jnp.where(c == 0, part[rows:], part[:rows])
        kept = jnp.where(c == 0, part[:rows], part[rows:])
        got = yield "move", "c", sent[:, : cuts[-1]]
        return [
            grid.ordered(c, kept[:, i:j], got[:, i:j], 1) for i, j in zip(cuts, cuts[1:])
        ] + [kept[:4, cuts[-1] : cuts[-1] + rows]]

    def input_grad(dx, dx_go, dr1, order):
        part = dx + (yield "move", "c", dx_go).astype(F32)
        part = yield from reduce_axes(grid, part, order)
        return dr1 + part

    orders = ORDERS
    got, start = grid.results, grid.start

    def rank_():
        got["rank"] = grid.work(functools.partial(rank, me, numbers), *got["X"])

    def project_():
        pieces, at, per = placed(got["Q"], orders["Q"])
        got["project"] = grid.work(
            lambda *a: project(me, list(a[:-4]), at, per, *a[-4:]), *pieces, *got["X"], *got["rank"][1:3]
        )

    def attend_():
        q, k, v = got["project"][:3]
        got["attend"] = grid.work(attend, q, k, v, got["rank"][3])

    def ob_move():
        got["ob"] = grid.move("c", got["attend"][1])

    def mid_():
        pieces, out_sib = got["U"]
        if not direct:
            table = jnp.stack(grid.places(orders["U"][::-1], me))
            out_sib = jnp.zeros_like(out_sib).at[table].set(out_sib).reshape(1, width, 384)
        pieces, at, per = placed(pieces, orders["U"])
        args = [got["attend"][1], got["ob"], out_sib, *got["X"]]
        got["mid"] = grid.work(lambda *a: mid(me, list(a[:-5]), at, per, *a[-5:], ff, rows), *pieces, *args)
        got["norm"] = got["mid"][7]

    def gate_():
        pieces, at, per = placed(got["G"], orders["G"])
        h1, up = got["mid"][2:4]
        got["gate"] = grid.work(lambda *a: gate_up(me, list(a[:-2]), at, per, *a[-2:]), *pieces, h1, up)

    def down_():
        pieces, at, per = placed(got["D"], orders["D"])
        got["down"] = grid.work(lambda *a: down(me, list(a[:-1]), at, per, a[-1]), *pieces, got["gate"][1])

    def part_move():
        got["part"] = grid.move("c", got["down"][0])

    def turn_():
        n1, _, _, up, _, _, up_w, _ = got["mid"]
        gate, _, gate_w = got["gate"]
        part, down_w = got["down"]
        got["turn"] = grid.work(
            turn, part, got["part"], n1, got["norm"], cotangent, got["C"], got["rank"][4], gate, up, gate_w, up_w, down_w
        )

    def back_move():
        got["back_part"] = grid.move("c", got["turn"][5])

    def grad_d():
        order = orders["d"]
        at, per = places_of(order, 2 * down_rows, ff)
        made = grid.work(functools.partial(grad, me, at, per), got["gate"][1], got["turn"][2])
        start("d", down_grad(made, order))

    def grad_g():
        order = orders["g"]
        at, per = places_of(order, two, width)
        made = grid.work(functools.partial(grad, me, at, per), got["mid"][2], got["turn"][3])
        start("g", columns_grad(made, order, [0, ff]))

    def back_():
        n1, f1 = got["mid"][:2]
        got["back"] = grid.work(
            functools.partial(back, me), got["turn"][1], got["turn"][5], got["back_part"], n1, f1, got["norm"], got["mid"][5]
        )

    def grad_u():
        order = orders["u"]
        at, per = places_of(order, two, width)
        made = grid.work(
            functools.partial(grad_up, me, at, per, rows),
            got["mid"][2], got["turn"][4], got["mid"][4], got["back"][1], got["back"][3], got["turn"][6],
        )
        start("u", columns_grad(made, order, [0, ff, ff + 384]))

    def attend_back_():
        q, k, v, qkv_w = got["project"]
        x_t, cos, sin, ext = got["rank"][:4]
        att, _, lse = got["attend"]
        order = orders["q"]
        at, per = places_of(order, two, width)
        dx, dx_go, *made = grid.work(
            functools.partial(attend_back, me, at, per), q, lse, got["back"][2], att, k, v, ext, cos, sin, x_t, qkv_w
        )
        start("q", columns_grad(made, order, [0, 384, 768, 1152]))
        start("x", input_grad(dx, dx_go, got["back"][0], "x" + orders["x"][-1]))

    start("X", tokens_task())
    start("P", columns_task())
    later = {
        "D": lambda: down_task(orders["D"]),
        "Q": lambda: grid.gather(shard(0, 1152), orders["Q"]),
        "U": lambda: up_task(orders["U"]),
        "G": lambda: grid.gather(shard(1152 + ff + 512, ff), orders["G"]),
    }
    start("C", cot_task())
    single = [
        rank_, project_, attend_, ob_move, mid_, gate_, down_, part_move, turn_, back_move, grad_d, grad_g,
        back_, grad_u, attend_back_,
    ]
    for code in SEQUENCE:
        if code < 0:
            grid.arrived.append(grid.moved[-code])
            continue
        grid.label = code if code >= 200 else code & ~8
        if code >= 200:
            single[code - 200]()
            continue
        name = STREAMS[code >> 4]
        if name in later:
            start(name, later.pop(name)())
        grid.advance(name, bool(code & 8))
    norms = got["u"][2].reshape(2, 2, rows)
    return (
        got["turn"][0],
        got["x"],
        jnp.concatenate(got["q"][:3], axis=1)[None],
        got["u"][1][None],
        got["g"][0][None],
        got["u"][0][None],
        got["d"][None],
        norms[0][None],
        norms[1][None],
    )


def solution(mesh):
    grid = Grid(mesh.shape["dp"], mesh.shape["seq"])
    rows = P(AXES, None)
    weight = P(None, AXES, None)
    norm = P(None, None, AXES)
    return jax.shard_map(
        functools.partial(body, grid),
        mesh=mesh,
        in_specs=(rows, P(AXES), P(AXES)) + (weight,) * 5 + (norm,) * 2 + (rows,),
        out_specs=(rows, rows) + (weight,) * 5 + (norm,) * 2,
        check_vma=False,
    )
```

```python
import functools

import jax
import jax.numpy as jnp
import numpy as np
from jax import lax
from jax.experimental import pallas as pl
from jax.experimental.pallas import tpu as pltpu
from jax.sharding import PartitionSpec as P

HEADS = 12
EPS = 1e-05
BASE = 10000.0
AXES = ("dp", "seq")
BF = jnp.bfloat16
F32 = jnp.float32
FAR = -1e30
NOTE = 16
ONES = 64


ORDERS = {"X": "zx", "x": "Z", "Q": "zxy", "U": "xzy", "G": "hyx", "D": "zx", "d": "zx", "g": "yxZ", "u": "xyz", "q": "yxz"}
STREAMS = "XPQUGDCdguqx"
SEQUENCE = [
    17, 1, 18, -18, 33, 65, 81, 34, 49, 2, -49, 43, 82, 74, -33, 3, -34, 83,
    -2, -65, -35, 36, 50, 67, 37, 12, -66, 51, -50, -4, 5, -3, -67, -36, 68, 84,
    60, -37, -84, 97, 85, -97, -5, 53, 6, -85, -52, -6, 94, 200, -68, 87, 201, 202,
    203, -203, -86, 54, -53, 204, 205, -87, 206, 207, 208, 209, 210, 211, 212, 129, 213, 113,
    145, -54, -209, 214, -113, 161, 130, -145, 114, 146, -130, 131, 177, -129, -114, 123, -161, 162,
    -177, 178, 163, 147, -162, -163, 132, 141, -147, -132, 148, 164, 116, -115, -178, -164, 179, -148,
    173, 157, 117, -116, 180, 118, 166, -166, 189, 150, -149, 134, -118, -134, -180, -150,
]


def dot(a, b):
    return jnp.dot(a, b, preferred_element_type=F32)


def dot_t(a, b):
    return lax.dot_general(a, b, (((1,), (1,)), ((), ())), preferred_element_type=F32)


def t_dot(a, b):
    return lax.dot_general(a, b, (((0,), (0,)), ((), ())), preferred_element_type=F32)


def lanes(shape):
    return lax.broadcasted_iota(jnp.int32, shape, len(shape) - 1)


def swap_halves(u):
    width = u.shape[-1]
    low = lanes(u.shape) % 64 < 32
    return jnp.where(low, pltpu.roll(u, width - 32, 1), pltpu.roll(u, 32, 1))


def split3(v):
    hi = v.astype(BF).astype(F32)
    rest = v - hi
    mid = rest.astype(BF).astype(F32)
    return hi, mid, rest - mid


def with_units(base, v):
    at = lanes(base.shape)
    hi, mid, low = split3(v)
    return jnp.where(
        at == ONES,
        -hi,
        jnp.where(at == ONES + 1, -mid, jnp.where(at == ONES + 2, -low, base)),
    )


def fill(target, pieces, places, per):
    n = 0
    for piece in pieces:
        for i in range(piece.shape[0]):
            target[pl.ds(pl.multiple_of(places[n] * per, 16), per), :] = piece[i]
            n += 1


def whole(shape):
    return pl.BlockSpec(shape, lambda *_: (0,) * len(shape))


def scalars():
    return pl.BlockSpec(memory_space=pltpu.SMEM)


def params(mib):
    return pltpu.CompilerParams(vmem_limit_bytes=mib << 20)


def like(*shape, dtype=F32):
    return jax.ShapeDtypeStruct(shape, dtype)


def far(*shape, dtype=F32):
    return pltpu.HBM(shape, dtype)


def kept_far(*arrays):
    return [pltpu.with_memory_space_constraint(a, pltpu.HBM) for a in arrays]


def message_kernel(x_ref, ids_ref, mask_ref, down_ref, out_ref, low_ref, note_s):
    local = x_ref.shape[0]
    note_s[...] = jnp.zeros(note_s.shape, F32)
    note_s[0:1, :local] = ids_ref[...].astype(F32)
    note_s[1:2, :local] = mask_ref[...].astype(F32)
    out_ref[:local] = x_ref[...]
    out_ref[local:] = note_s[...].astype(BF)
    low_ref[...] = down_ref[0].astype(BF)


def make_message(tokens, ids, mask, down):
    local, width = tokens.shape
    args = [tokens, ids.reshape(1, local), mask.reshape(1, local), down]
    return pl.pallas_call(
        message_kernel,
        grid=(1,),
        in_specs=[whole(a.shape) for a in args],
        out_specs=[whole((local + NOTE, width)), whole(down.shape[1:])],
        out_shape=[like(local + NOTE, width, dtype=BF), like(*down.shape[1:], dtype=BF)],
        scratch_shapes=[pltpu.VMEM((NOTE, width), F32)],
        compiler_params=params(8),
        cost_estimate=pl.CostEstimate(flops=1, bytes_accessed=1, transcendentals=0),
        name="message",
    )(*kept_far(*args))


def columns_kernel(me_ref, qkv_ref, up_ref, out_w_ref, gate_ref, gain_ref, bias_ref, mine_ref, theirs_ref, ext_s):
    c = me_ref[3]
    rows = qkv_ref.shape[1]

    def halves(ref, start, size, to):
        for target, which in ((mine_ref, c), (theirs_ref, 1 - c)):
            at = pl.ds(pl.multiple_of(start + which * size, 128), size)
            target[:, to : to + size] = ref[0, :, at].astype(BF)

    for j in range(3):
        halves(qkv_ref, j * 768, 384, j * 384)
    ff = up_ref.shape[2] // 2
    to = 1152
    halves(up_ref, 0, ff, to)
    halves(out_w_ref, 0, 384, to + ff)
    halves(gate_ref, 0, ff, to + ff + 512)
    ext_s[...] = jnp.zeros(ext_s.shape, F32)
    ext_s[0:2, :rows] = gain_ref[0]
    ext_s[2:4, :rows] = bias_ref[0]
    for target in (mine_ref, theirs_ref):
        target[:, to + ff + 384 : to + ff + 512] = ext_s[...].astype(BF)


def make_columns(me, qkv, up, out_w, gate, gain, bias):
    rows = qkv.shape[1]
    shape = like(rows, 1152 + up.shape[2] + 512, dtype=BF)
    args = [qkv, up, out_w, gate, gain, bias]
    return pl.pallas_call(
        columns_kernel,
        grid=(1,),
        in_specs=[scalars()] + [whole(a.shape) for a in args],
        out_specs=[whole(shape.shape)] * 2,
        out_shape=[shape] * 2,
        scratch_shapes=[pltpu.VMEM((rows, 128), F32)],
        compiler_params=params(12),
        cost_estimate=pl.CostEstimate(flops=1, bytes_accessed=1, transcendentals=0),
        name="columns",
    )(me, *kept_far(*args))


def angle_table(count, stride):
    angle = np.arange(count)[:, None] * float(stride) * BASE ** (-2.0 * (np.arange(128) % 32) / 64)[None, :]
    rest = np.concatenate([np.cos(angle), np.sin(angle)], axis=1)
    parts = []
    for _ in range(3):
        part = rest.astype(jnp.bfloat16)
        parts.append(part)
        rest = rest - part.astype(np.float64)
    return np.concatenate(parts, axis=0)


def rank_kernel(
    me_ref, along_ref, beside_ref, note_a_ref, note_b_ref, fine_ref, coarse_ref,
    t_ref, cos_ref, sin_ref, ext_ref, keep_ref, ext_s, count_s, before_s, *, numbers, coarse,
):
    local = cos_ref.shape[0] // 4
    chips = note_a_ref.shape[0]
    step = pl.program_id(0)
    lane = lanes((local, 128))

    @pl.when(step == 0)
    def _():
        def one(i, _):
            for h, ref in enumerate((note_a_ref, note_b_ref)):
                note = ref[i].astype(F32)[:, :256].T
                own = jnp.where(note[:local, 0:1] == lane.astype(F32), 1.0, 0.0)
                ext = jnp.where(lane < 64, own, jnp.where(lane < ONES + 3, 1.0, 0.0))
                ext_s[2 * i + h] = ext.astype(BF)
                count_s[pl.ds(2 * i + h, 1), :] = jnp.sum(own, axis=0, keepdims=True)
            return 0

        lax.fori_loop(0, chips, one, 0)
        for h, ref in enumerate((note_a_ref, note_b_ref)):
            note = ref[0].astype(F32)[:, :256].T
            keep_ref[h * local : (h + 1) * local] = jnp.broadcast_to(note[:local, 1:2], (local, 128))
        blocks = 2 * chips
        mine = numbers(lax.broadcasted_iota(jnp.int32, (blocks, blocks), 0), me_ref)
        other = numbers(lax.broadcasted_iota(jnp.int32, (blocks, blocks), 1), me_ref)
        before_s[...] = dot(jnp.where(other < mine, 1.0, 0.0).astype(BF), count_s[...].astype(BF))

    x = jnp.concatenate([r[i, :local] for i in range(2) for r in (along_ref, beside_ref)], axis=0)
    t_ref[...] = x.T
    up = lax.broadcasted_iota(jnp.int32, (local, local), 0) > lax.broadcasted_iota(jnp.int32, (local, local), 1)
    up = jnp.where(up, 1.0, 0.0).astype(BF)
    for b in range(4):
        block = 4 * step + b
        ext = ext_s[block]
        rank = dot(up, ext) + before_s[pl.ds(block, 1), :]
        position = jnp.sum(jnp.where(lane < 64, ext.astype(F32) * rank, 0.0), axis=1, keepdims=True)
        high = jnp.floor(position * (1.0 / 64))

        def pick(value, size, table_ref):
            at = lanes((local, 3 * size)) & (size - 1)
            chosen = jnp.where(at.astype(F32) == value, 1.0, 0.0).astype(BF)
            return dot(chosen, table_ref[...])

        low = pick(position - 64 * high, 64, fine_ref)
        high = pick(high, coarse, coarse_ref)
        cos = low[:, :128] * high[:, :128] - low[:, 128:] * high[:, 128:]
        sin = low[:, 128:] * high[:, :128] + low[:, :128] * high[:, 128:]
        rows = slice(b * local, (b + 1) * local)
        cos_ref[rows] = cos
        sin_ref[rows] = jnp.where(lane % 64 < 32, -sin, sin)
        ext_ref[rows] = ext


def rank(me, numbers, along, beside):
    chips, padded, width = along.shape
    local = padded - NOTE
    count = chips * 2 * local
    step = 4 * local
    coarse = max(64, 1 << (-(-count // 64) - 1).bit_length())
    note = pl.BlockSpec((chips, NOTE, width), lambda i: (0, local // NOTE, 0))
    rows = pl.BlockSpec((step, 128), lambda i: (i, 0))
    return pl.pallas_call(
        functools.partial(rank_kernel, numbers=numbers, coarse=coarse),
        grid=(chips // 2,),
        in_specs=[scalars()]
        + [pl.BlockSpec((2, padded, width), lambda i: (i, 0, 0))] * 2
        + [note, note, whole((192, 256)), whole((3 * coarse, 256))],
        out_specs=[pl.BlockSpec((width, step), lambda i: (0, i)), rows, rows, rows, whole((2 * local, 128))],
        out_shape=[
            far(width, count, dtype=BF), far(count, 128), far(count, 128), far(count, 128, dtype=BF),
            like(2 * local, 128),
        ],
        scratch_shapes=[
            pltpu.VMEM((2 * chips, local, 128), BF),
            pltpu.VMEM((2 * chips, 128), F32),
            pltpu.VMEM((2 * chips, 128), F32),
        ],
        compiler_params=params(16),
        cost_estimate=pl.CostEstimate(flops=1, bytes_accessed=1, transcendentals=0),
        name="rank",
    )(
        me, along, beside, along, beside,
        jnp.asarray(angle_table(64, 1)), jnp.asarray(angle_table(coarse, 64)),
    )


def project_kernel(me_ref, *refs, places, per, n):
    pieces = refs[:n]
    along_ref, beside_ref, cos_ref, sin_ref, q_ref, k_ref, v_ref, w_ref = refs[n:]
    local = cos_ref.shape[0] // 4
    first = pl.program_id(0) == 0

    @pl.when(first)
    def _():
        fill(w_ref, pieces, places(me_ref), per)

    x = jnp.concatenate([r[i, :local] for i in range(2) for r in (along_ref, beside_ref)], axis=0)
    cos, sin = cos_ref[...], sin_ref[...]
    kv = dot(x, w_ref[:, 384:])
    for p in range(3):
        at = slice(p * 128, p * 128 + 128)
        u = kv[:, at]
        k_ref[p] = (u * cos + swap_halves(u) * sin).astype(BF)
        v_ref[p] = kv[:, 384 + p * 128 : 512 + p * 128].astype(BF)

    @pl.when(first)
    def _():
        q = dot(x[: 2 * local], w_ref[:, :384])
        for p in range(3):
            at = slice(p * 128, p * 128 + 128)
            u = q[:, at]
            r = (u * cos[: 2 * local] + swap_halves(u) * sin[: 2 * local]).astype(BF)
            q_ref[:, at] = r * jnp.asarray(0.125, BF)


def project(me, pieces, places, per, along, beside, cos, sin):
    chips, padded, width = along.shape
    count = cos.shape[0]
    step = 2 * (count // chips)
    rows = pl.BlockSpec((step, 128), lambda i: (i, 0))
    heads = pl.BlockSpec((3, step, 128), lambda i: (0, i, 0))
    return pl.pallas_call(
        functools.partial(project_kernel, places=places, per=per, n=len(pieces)),
        grid=(chips // 2,),
        in_specs=[scalars()]
        + [whole(p.shape) for p in pieces]
        + [pl.BlockSpec((2, padded, width), lambda i: (i, 0, 0))] * 2
        + [rows] * 2,
        out_specs=[whole((step // 2, 384)), heads, heads, whole((width, 1152))],
        out_shape=[
            far(step // 2, 384, dtype=BF), far(3, count, 128, dtype=BF), far(3, count, 128, dtype=BF),
            far(width, 1152, dtype=BF),
        ],
        compiler_params=params(24),
        cost_estimate=pl.CostEstimate(flops=1, bytes_accessed=1, transcendentals=0),
        name="project",
    )(me, *pieces, along, beside, *kept_far(cos, sin))


def attend_kernel(q_ref, k_ref, v_ref, ext_ref, att_ref, ob_ref, lse_ref, *, chunk):
    keys = k_ref.shape[1]
    q = q_ref[...]
    own = q.shape[0]
    first = lanes(q.shape) < 64
    ext = ext_ref[:own].astype(F32)
    ext = jnp.where(lanes(ext.shape) < 64, (1.0 - ext) * FAR, 0.0).astype(BF)
    parts = []
    for h in range(2):
        qh = jnp.where(first if h == 0 else ~first, q, jnp.zeros_like(q))
        qc = jnp.concatenate([qh, ext], axis=1)
        top = jnp.full((own, 1), FAR, F32)
        acc = jnp.zeros((own, 256), F32)
        for j in range(0, keys, chunk):
            rows = slice(j, j + chunk)
            s = dot_t(qc, jnp.concatenate([k_ref[0, rows], ext_ref[rows]], axis=1))
            above = jnp.maximum(top, jnp.max(s, axis=1, keepdims=True))
            e = jnp.exp(s - above).astype(BF)
            acc = acc * jnp.exp(top - above) + dot(e, jnp.concatenate([v_ref[0, rows], ext_ref[rows]], axis=1))
            top = above
        total = acc[:, 128 + ONES : 129 + ONES]
        parts.append(acc[:, :128] / total)
        lse_ref[h] = with_units(ext.astype(F32), top + jnp.log(total)).astype(BF)
    att = jnp.where(first, parts[0], parts[1])
    att_ref[...] = att
    ob_ref[...] = att.astype(BF)


def attend(q, k, v, ext):
    own = q.shape[0]
    keys = k.shape[1]
    return pl.pallas_call(
        functools.partial(attend_kernel, chunk=512),
        grid=(3,),
        in_specs=[
            pl.BlockSpec((own, 128), lambda p: (0, p)),
            pl.BlockSpec((1, keys, 128), lambda p: (p, 0, 0)),
            pl.BlockSpec((1, keys, 128), lambda p: (p, 0, 0)),
            whole(ext.shape),
        ],
        out_specs=[
            pl.BlockSpec((own, 128), lambda p: (0, p)),
            pl.BlockSpec((own, 128), lambda p: (0, p)),
            pl.BlockSpec((2, own, 128), lambda p: (p, 0, 0)),
        ],
        out_shape=[
            far(own, 384),
            like(own, 384, dtype=BF),
            far(6, own, 128, dtype=BF),
        ],
        compiler_params=params(20 if keys <= 4096 else 60),
        cost_estimate=pl.CostEstimate(
            flops=4 * 6 * own * keys * 256,
            bytes_accessed=3 * keys * 1024,
            transcendentals=6 * own * keys,
        ),
        name="attend",
    )(*kept_far(q, k, v, ext))


def normalize(values):
    average = jnp.mean(values, axis=-1, keepdims=True)
    centred = values - average
    factor = lax.rsqrt(jnp.mean(centred * centred, axis=-1, keepdims=True) + EPS)
    return centred * factor, factor


def norm_back(gradient, normed, factor):
    return factor * (
        gradient
        - jnp.mean(gradient, axis=-1, keepdims=True)
        - normed * jnp.mean(gradient * normed, axis=-1, keepdims=True)
    )


def turned(a):
    half = a.shape[0] // 2
    return jnp.concatenate([a[half:], a[:half]], axis=0)


def silu_parts(gate):
    sigmoid = 1.0 / (1.0 + jnp.exp(-gate))
    return sigmoid, gate * sigmoid


def mid_kernel(me_ref, *refs, places, per, n, share_rows):
    pieces = refs[:n]
    ob_ref, got_ref, sib_ref, along_ref, beside_ref = refs[n : n + 5]
    n1_ref, f1_ref, h1_ref, up_ref, all_ref, out_ref, up_w_ref, norm_ref = refs[n + 5 :]
    local = along_ref.shape[1] - NOTE
    c = me_ref[3]
    ff = up_ref.shape[1]
    at = places(me_ref)
    done = 0
    norm = jnp.zeros(norm_ref.shape, F32)
    width = norm.shape[1]
    for piece in pieces:
        for i in range(piece.shape[0]):
            rows = pl.ds(pl.multiple_of(at[done] * per, 16), per)
            block = piece[i, :, ff + 384 : ff + 512].astype(F32)
            for d in range(per // share_rows):
                ext = jnp.concatenate([block[d * share_rows :][:4], jnp.zeros((4, 128), F32)], axis=0)
                ext = jnp.concatenate([ext, jnp.zeros((8, width - 128), F32)], axis=1)
                norm = norm + pltpu.roll(ext, (at[done] * (per // share_rows) + d) * share_rows, 1)
            up_w_ref[rows, :] = piece[i, :, :ff]
            out_ref[c, rows, :] = piece[i, :, ff : ff + 384]
            out_ref[1 - c, rows, :] = sib_ref[done]
            done += 1
    norm_ref[...] = norm
    all_ref[c] = ob_ref[...]
    all_ref[1 - c] = turned(got_ref[...])
    halves = [dot(all_ref[0], out_ref[i, :384]) + dot(all_ref[1], out_ref[i, 384:]) for i in range(2)]
    n1, f1 = normalize(
        jnp.concatenate([along_ref[0, :local], beside_ref[0, :local]], axis=0).astype(F32)
        + jnp.concatenate(halves, axis=1)
    )
    low = (n1 * norm_ref[0:1] + norm_ref[2:3]).astype(BF)
    n1_ref[...] = n1
    f1_ref[...] = jnp.broadcast_to(f1, f1_ref.shape)
    h1_ref[...] = low
    up_ref[...] = dot(low, up_w_ref[...])


def mid(me, pieces, places, per, ob, got, sib, along, beside, ff, share_rows):
    own, width = ob.shape[0], along.shape[2]
    small = [ob, got, sib, along, beside]
    one = pl.BlockSpec((1, *along.shape[1:]), lambda *_: (0, 0, 0))
    return pl.pallas_call(
        functools.partial(mid_kernel, places=places, per=per, n=len(pieces), share_rows=share_rows),
        in_specs=[scalars()]
        + [whole(a.shape) for a in pieces + small[:3]]
        + [one, one],
        out_specs=[
            whole((own, width)), whole((own, 128)), whole((own, width)), whole((own, ff)),
            whole((2, own, 384)), whole((2, width, 384)), whole((width, ff)), whole((8, width)),
        ],
        out_shape=[
            like(own, width), like(own, 128), like(own, width, dtype=BF), like(own, ff),
            like(2, own, 384, dtype=BF), like(2, width, 384, dtype=BF), like(width, ff, dtype=BF), like(8, width),
        ],
        grid=(1,),
        compiler_params=params(22),
        cost_estimate=pl.CostEstimate(flops=2 * own * width * 2304, bytes_accessed=12 << 20, transcendentals=0),
        name="mid",
    )(me, *pieces, *small)


def gate_kernel(me_ref, *refs, places, per, n):
    pieces = refs[:n]
    h1_ref, up_ref, gate_ref, hidden_ref, w_ref = refs[n:]
    fill(w_ref, pieces, places(me_ref), per)
    gate = dot(h1_ref[...], w_ref[...])
    gate_ref[...] = gate
    hidden_ref[...] = (silu_parts(gate)[1] * up_ref[...]).astype(BF)


def gate_up(me, pieces, places, per, h1, up):
    own, ff = up.shape
    width = h1.shape[1]
    return pl.pallas_call(
        functools.partial(gate_kernel, places=places, per=per, n=len(pieces)),
        grid=(1,),
        in_specs=[scalars()] + [whole(a.shape) for a in [*pieces, h1, up]],
        out_specs=[whole((own, ff)), whole((own, ff)), whole((width, ff))],
        out_shape=[like(own, ff), like(own, ff, dtype=BF), like(width, ff, dtype=BF)],
        compiler_params=params(20),
        cost_estimate=pl.CostEstimate(flops=2 * own * width * ff, bytes_accessed=10 << 20, transcendentals=own * ff),
        name="gate_up",
    )(me, *pieces, h1, up)


def down_kernel(me_ref, *refs, places, per, n):
    pieces = refs[:n]
    hidden_ref, part_ref, w_ref = refs[n:]
    fill(w_ref, pieces, places(me_ref), per)
    part_ref[...] = dot(hidden_ref[...], w_ref[...])


def down(me, pieces, places, per, hidden):
    own, ff = hidden.shape
    width = pieces[0].shape[2]
    return pl.pallas_call(
        functools.partial(down_kernel, places=places, per=per, n=len(pieces)),
        grid=(1,),
        in_specs=[scalars()] + [whole(a.shape) for a in [*pieces, hidden]],
        out_specs=[whole((own, width)), whole((ff, width))],
        out_shape=[like(own, width), like(ff, width, dtype=BF)],
        compiler_params=params(14),
        cost_estimate=pl.CostEstimate(flops=2 * own * width * ff, bytes_accessed=8 << 20, transcendentals=0),
        name="down",
    )(me, *pieces, hidden)


def turn_kernel(
    part_ref, got_ref, n1_ref, norm_ref, cot_ref, cot_got_ref, keep_ref, gate_ref, up_ref, gate_w_ref, up_w_ref, down_w_ref,
    out_ref, dr2_ref, dm_ref, dgate_ref, dup_ref, back_ref, sums_ref,
):
    local = out_ref.shape[0]
    h1 = n1_ref[...] * norm_ref[0:1] + norm_ref[2:3]
    n2, f2 = normalize(h1 + part_ref[...] + turned(got_ref[...]))
    keep = keep_ref[:, :1]
    gain = norm_ref[1:2]
    out_ref[...] = ((n2[:local] * gain + norm_ref[3:4]) * keep[:local]).astype(BF)
    masked = jnp.concatenate([cot_ref[...], cot_got_ref[...]], axis=0).astype(F32) * keep
    sums_ref[0:1] = jnp.sum(masked * n2, axis=0, keepdims=True)
    sums_ref[1:2] = jnp.sum(masked, axis=0, keepdims=True)
    sums_ref[2:] = jnp.zeros((6, sums_ref.shape[1]), F32)
    dr2 = norm_back(masked * gain, n2, f2)
    dr2_ref[...] = dr2
    dm = dr2.astype(BF)
    dm_ref[...] = dm
    ff = gate_ref.shape[1]
    step = 512
    back = jnp.zeros(dr2.shape, F32)
    for j in range(0, ff, step):
        at = slice(j, j + step)
        dh = dot_t(dm, down_w_ref[at, :])
        gate = gate_ref[:, at]
        sigmoid, silu = silu_parts(gate)
        dgate = (dh * up_ref[:, at] * sigmoid * (1.0 + gate * (1.0 - sigmoid))).astype(BF)
        dup = (dh * silu).astype(BF)
        dgate_ref[:, at] = dgate
        dup_ref[:, at] = dup
        back = back + dot_t(dgate, gate_w_ref[:, at]) + dot_t(dup, up_w_ref[:, at])
    back_ref[...] = back


def turn(part, got, n1, norm, cot, cot_got, keep, gate, up, gate_w, up_w, down_w):
    own, width = part.shape
    ff = gate.shape[1]
    args = [part, got, n1, norm, cot, cot_got, keep, gate, up, gate_w, up_w, down_w]
    return pl.pallas_call(
        turn_kernel,
        grid=(1,),
        in_specs=[whole(a.shape) for a in args],
        out_specs=[
            whole((own // 2, width)), whole((own, width)), whole((own, width)), whole((own, ff)),
            whole((own, ff)), whole((own, width)), whole((8, width)),
        ],
        out_shape=[
            like(own // 2, width, dtype=BF), like(own, width), like(own, width, dtype=BF),
            like(own, ff, dtype=BF), like(own, ff, dtype=BF), like(own, width), like(8, width),
        ],
        compiler_params=params(34),
        cost_estimate=pl.CostEstimate(flops=6 * own * width * ff, bytes_accessed=20 << 20, transcendentals=own * ff),
        name="turn",
    )(*args)


def back_kernel(me_ref, dr2_ref, part_ref, got_ref, n1_ref, f1_ref, norm_ref, w_ref, dr1_ref, da_ref, dob_ref, sums_ref):
    dh1 = dr2_ref[...] + part_ref[...] + turned(got_ref[...])
    n1 = n1_ref[...]
    sums_ref[0:1] = jnp.sum(dh1 * n1, axis=0, keepdims=True)
    sums_ref[1:2] = jnp.sum(dh1, axis=0, keepdims=True)
    sums_ref[2:] = jnp.zeros((6, n1.shape[1]), F32)
    dr1 = norm_back(dh1 * norm_ref[0:1], n1, f1_ref[:, :1])
    dr1_ref[...] = dr1[: dr1_ref.shape[0]]
    da = dr1.astype(BF)
    da_ref[...] = da
    rows = pl.ds(pl.multiple_of(me_ref[3] * 384, 128), 384)
    dob_ref[...] = (dot_t(da[:, :384], w_ref[0, rows, :]) + dot_t(da[:, 384:], w_ref[1, rows, :])).astype(BF)


def back(me, dr2, part, got, n1, f1, norm, out_w):
    own, width = dr2.shape
    args = [dr2, part, got, n1, f1, norm, out_w]
    return pl.pallas_call(
        back_kernel,
        grid=(1,),
        in_specs=[scalars()] + [whole(a.shape) for a in args],
        out_specs=[whole((own // 2, width)), whole((own, width)), whole((own, 384)), whole((8, width))],
        out_shape=[like(own // 2, width), like(own, width, dtype=BF), like(own, 384, dtype=BF), like(8, width)],
        compiler_params=params(14),
        cost_estimate=pl.CostEstimate(flops=2 * own * width * 384, bytes_accessed=7 << 20, transcendentals=0),
        name="back",
    )(me, *args)


def share(whole_ref, at, per, mine_ref, theirs_ref):
    half = mine_ref.shape[0]
    for i in range(2 * half):
        block = whole_ref[pl.ds(pl.multiple_of(at[i] * per, 16), per), :]
        if i < half:
            mine_ref[i, :, : block.shape[1]] = block
        else:
            theirs_ref[i - half, :, : block.shape[1]] = block.astype(BF)


def grad_kernel(me_ref, left_ref, right_ref, mine_ref, theirs_ref, acc_ref, *, places, per):
    acc_ref[...] = t_dot(left_ref[...], right_ref[...])
    share(acc_ref, places(me_ref), per, mine_ref, theirs_ref)


def grad(me, places, per, left, right):
    own, rows = left.shape
    cols = right.shape[1]
    half = rows // per // 2
    step = 768 if cols % 768 == 0 else cols
    return pl.pallas_call(
        functools.partial(grad_kernel, places=places, per=per),
        grid=(cols // step,),
        in_specs=[scalars(), whole(left.shape), pl.BlockSpec((own, step), lambda j: (0, j))],
        out_specs=[pl.BlockSpec((half, per, step), lambda j: (0, 0, j))] * 2,
        out_shape=[like(half, per, cols), like(half, per, cols, dtype=BF)],
        scratch_shapes=[pltpu.VMEM((rows, step), F32)],
        compiler_params=params(18),
        cost_estimate=pl.CostEstimate(flops=2 * own * rows * cols, bytes_accessed=6 * rows * cols, transcendentals=0),
        name="grad",
    )(me, left, right)


def grad_up_kernel(
    me_ref, h1_ref, dup_ref, ob_ref, da_ref, one_ref, two_ref, mine_ref, theirs_ref, acc_ref, sums_s, *, places, per, share_rows
):
    width, ff = h1_ref.shape[1], dup_ref.shape[1]
    at = places(me_ref)
    acc_ref[:, :ff] = t_dot(h1_ref[...], dup_ref[...])
    columns = pl.ds(pl.multiple_of(me_ref[3] * 384, 128), 384)
    da = da_ref[:, columns]
    acc_ref[:384, ff:] = t_dot(ob_ref[0], da)
    acc_ref[384:, ff:] = t_dot(ob_ref[1], da)
    share(acc_ref, at, per, mine_ref, theirs_ref)
    for j in range(2):
        sums_s[2 * j : 2 * j + 1] = one_ref[j : j + 1]
        sums_s[2 * j + 1 : 2 * j + 2] = two_ref[j : j + 1]
    sums_s[4:] = jnp.zeros((4, width), F32)
    sums = sums_s[...]
    half = mine_ref.shape[0]
    lane = lanes((4, 128))
    for i in range(2 * half):
        ref, k = (mine_ref, i) if i < half else (theirs_ref, i - half)
        blocks = []
        for d in range(per // share_rows):
            device = at[i] * (per // share_rows) + d
            turn = pltpu.roll(sums, width - device * share_rows, 1)[:4, :128]
            blocks += [jnp.where(lane < share_rows, turn, 0.0), jnp.zeros((share_rows - 4, 128), F32)]
        ref[k, :, ff + 384 :] = jnp.concatenate(blocks, axis=0).astype(ref.dtype)


def grad_up(me, places, per, share_rows, h1, dup, ob_all, da, one, two):
    width, ff = h1.shape[1], dup.shape[1]
    cols = ff + 512
    half = width // per // 2
    args = [h1, dup, ob_all, da, one, two]
    return pl.pallas_call(
        functools.partial(grad_up_kernel, places=places, per=per, share_rows=share_rows),
        grid=(1,),
        in_specs=[scalars()] + [whole(a.shape) for a in args],
        out_specs=[whole((half, per, cols))] * 2,
        out_shape=[like(half, per, cols), like(half, per, cols, dtype=BF)],
        scratch_shapes=[pltpu.VMEM((width, ff + 384), F32), pltpu.VMEM((8, width), F32)],
        compiler_params=params(24),
        cost_estimate=pl.CostEstimate(flops=1, bytes_accessed=1, transcendentals=0),
        name="grad_up",
    )(me, *args)


def attend_back_kernel(
    me_ref, q_ref, lse_ref, d_ref, att_ref, k_ref, v_ref, ext_ref, cos_ref, sin_ref, cosq_ref, sinq_ref, t_ref, w_ref,
    dx_ref, dx_go_ref, dw_ref, dw_go_ref, qc_s, dc_s, dq_s, dkv_s, dw_s, *, places, per,
):
    j = pl.program_id(0)
    own = q_ref.shape[0]
    local = own // 2
    first = lanes((own, 128)) < 64

    @pl.when(j == 0)
    def _():
        for p in range(3):
            at = slice(p * 128, p * 128 + 128)
            q, d = q_ref[:, at], d_ref[:, at]
            prod = d.astype(F32) * att_ref[:, at]
            for h in range(2):
                keep = first if h == 0 else ~first
                rows = slice(h * own, (h + 1) * own)
                qc_s[p, rows, :128] = jnp.where(keep, q, jnp.zeros_like(q))
                qc_s[p, rows, 128:] = lse_ref[2 * p + h]
                dc_s[p, rows, :128] = jnp.where(keep, d, jnp.zeros_like(d))
                delta = jnp.sum(jnp.where(keep, prod, 0.0), axis=1, keepdims=True)
                dc_s[p, rows, 128:] = with_units(jnp.zeros((own, 128), F32), delta).astype(BF)
        dq_s[...] = jnp.zeros_like(dq_s)
        dw_s[...] = jnp.zeros_like(dw_s)

    ext = ext_ref[...]
    for p in range(3):
        k = k_ref[p]
        e = jnp.exp(dot_t(jnp.concatenate([k, ext], axis=1), qc_s[p]))
        ds = (e * dot_t(jnp.concatenate([v_ref[p], ext], axis=1), dc_s[p])).astype(BF)
        dkv_s[:, 384 + p * 128 : 512 + p * 128] = dot(e.astype(BF), dc_s[p, :, :128]).astype(BF)
        dk = dot(ds, qc_s[p, :, :128]).astype(BF).astype(F32)
        dk = dk * cos_ref[...] - swap_halves(dk) * sin_ref[...]
        dkv_s[:, p * 128 : p * 128 + 128] = dk.astype(BF)
        dq_s[p] += t_dot(k, ds)
    dkv = dkv_s[...]
    dw_s[:, 384:] += dot(t_ref[...], dkv)
    dx = dot_t(dkv, w_ref[:, 384:])

    def put(dx):
        for i in range(dx_ref.shape[0]):
            dx_ref[i] = dx[2 * i * local : (2 * i + 1) * local]
            dx_go_ref[i] = dx[(2 * i + 1) * local : (2 * i + 2) * local].astype(BF)

    last = j == pl.num_programs(0) - 1

    @pl.when(~last)
    def _():
        put(dx)

    @pl.when(last)
    def _():
        dqs = []
        for p in range(3):
            t = dq_s[p].T
            dq = jnp.where(first, t[:own], t[own:])
            dq = (dq * 0.125).astype(BF).astype(F32)
            dqs.append((dq * cosq_ref[...] - swap_halves(dq) * sinq_ref[...]).astype(BF))
        dq = jnp.concatenate(dqs, axis=1)
        dw_s[:, :384] = dot(t_ref[:, :own], dq)
        put(jnp.concatenate([dx[:own] + dot_t(dq, w_ref[:, :384]), dx[own:]], axis=0))
        share(dw_s, places(me_ref), per, dw_ref, dw_go_ref)


def attend_back(me, places, per, q, lse, d, att, k, v, ext, cos, sin, t, w):
    own = q.shape[0]
    keys = k.shape[1]
    width = w.shape[0]
    chunk = 2 * own
    steps = keys // chunk
    half = width // per // 2
    return pl.pallas_call(
        functools.partial(attend_back_kernel, places=places, per=per),
        grid=(steps,),
        in_specs=[
            scalars(),
            whole(q.shape),
            whole(lse.shape),
            whole(d.shape),
            whole(att.shape),
            pl.BlockSpec((3, chunk, 128), lambda j: (0, steps - 1 - j, 0)),
            pl.BlockSpec((3, chunk, 128), lambda j: (0, steps - 1 - j, 0)),
            pl.BlockSpec((chunk, 128), lambda j: (steps - 1 - j, 0)),
            pl.BlockSpec((chunk, 128), lambda j: (steps - 1 - j, 0)),
            pl.BlockSpec((chunk, 128), lambda j: (steps - 1 - j, 0)),
            pl.BlockSpec((own, 128), lambda j: (0, 0)),
            pl.BlockSpec((own, 128), lambda j: (0, 0)),
            pl.BlockSpec((width, chunk), lambda j: (0, steps - 1 - j)),
            whole(w.shape),
        ],
        out_specs=[
            pl.BlockSpec((2, own // 2, width), lambda j: (steps - 1 - j, 0, 0)),
            pl.BlockSpec((2, own // 2, width), lambda j: (steps - 1 - j, 0, 0)),
            whole((half, per, 1152)),
            whole((half, per, 1152)),
        ],
        out_shape=[
            like(keys // own, own // 2, width),
            like(keys // own, own // 2, width, dtype=BF),
            like(half, per, 1152),
            like(half, per, 1152, dtype=BF),
        ],
        scratch_shapes=[
            pltpu.VMEM((3, 2 * own, 256), BF),
            pltpu.VMEM((3, 2 * own, 256), BF),
            pltpu.VMEM((3, 128, 2 * own), F32),
            pltpu.VMEM((chunk, 768), BF),
            pltpu.VMEM((width, 1152), F32),
        ],
        compiler_params=params(40),
        cost_estimate=pl.CostEstimate(
            flops=16 * 6 * own * keys * 256,
            bytes_accessed=3 * keys * 1600,
            transcendentals=6 * own * keys,
        ),
        name="attend_back",
    )(me, *kept_far(q, lse), d, *kept_far(att, k, v, ext, cos, sin, cos, sin, t, w))


class Grid:
    def __init__(self, ndp, nseq):
        self.ny, self.nz = ndp, nseq // 4
        self.count = ndp * nseq
        self.ring = [0, 1, 3, 2] if self.nz == 4 else list(range(self.nz))
        self.place = [self.ring.index(z) for z in range(self.nz)]
        step = {z: self.ring[(self.place[z] + 1) % self.nz] for z in range(self.nz)}
        self.across = {
            "c": self.pairs(lambda y, z, x, c: (y, z, x, 1 - c)),
            "x": self.pairs(lambda y, z, x, c: (y, z, 1 - x, c)),
            "y": self.pairs(lambda y, z, x, c: (1 - y, z, x, c)),
            "up": self.pairs(lambda y, z, x, c: (y, step[z], x, c)),
        }
        self.across["down"] = [(b, a) for a, b in self.across["up"]]
        for k in range(1, self.nz):
            by = {z: self.ring[(self.place[z] + k) % self.nz] for z in range(self.nz)}
            self.across[f"up{k}"] = self.pairs(lambda y, z, x, c, by=by: (y, by[z], x, c))
            self.across[f"down{k}"] = [(b, a) for a, b in self.across[f"up{k}"]]
        self.bits = [1 << i for i in range(self.nz.bit_length() - 1)]
        for bit in self.bits:
            self.across[f"z{bit}"] = self.pairs(lambda y, z, x, c, bit=bit: (y, z ^ bit, x, c))
        self.across["spread"] = self.pairs(lambda y, z, x, c: (1 - y, z, x, c) if c == y else None)
        self.across["home"] = self.pairs(lambda y, z, x, c: (1 - y, z, x, c) if c != y else None)
        self.across["give"] = self.pairs(lambda y, z, x, c: (y, z, x, 1 - c) if c == y else None)

    def pairs(self, to):
        def index(y, z, x, c):
            return ((y * self.nz + z) * 2 + x) * 2 + c

        made = []
        for y in range(self.ny):
            for z in range(self.nz):
                for x in range(2):
                    for c in range(2):
                        there = to(y, z, x, c)
                        if there is not None:
                            made.append((index(y, z, x, c), index(*there)))
        return made

    def locate(self):
        s = lax.axis_index("seq")
        self.arrived, self.moved = [], {}
        self.latest, self.streams, self.waiting, self.results = [None, None], {}, {}, {}
        self.y = lax.axis_index("dp")
        self.z, self.x, self.c = s // 4, (s // 2) % 2, s % 2
        return jnp.stack([self.y, self.z, self.x, self.c]).astype(jnp.int32)

    def back_by(self, axis, z, d):
        if axis == "h":
            moved = sum(jnp.where(d & other != 0, bit, 0) for bit, other in zip(self.bits, reversed(self.bits)))
            return z ^ moved
        return self.place_of((self.place_of(z) + self.nz - d) & (self.nz - 1))

    def place_of(self, z):
        return z ^ (z >> 1) if self.nz == 4 else z

    def places(self, order, me):
        size = {"x": 2, "y": self.ny, "z": self.nz, "Z": self.nz, "h": self.nz}
        total = 1
        for axis in order:
            total *= size[axis]
        found = []
        for i in range(total):
            y, z, x = me[0], me[1], me[2]
            for axis in reversed(order):
                d, i = i % size[axis], i // size[axis]
                if d == 0:
                    continue
                if axis == "x":
                    x = 1 - x
                elif axis == "y":
                    y = 1 - y
                elif axis == "h":
                    z = z ^ sum(bit for bit, other in zip(self.bits, reversed(self.bits)) if d & other)
                else:
                    z = self.place_of((self.place_of(z) + self.nz - d) % self.nz)
            if "y" not in order:
                y = 0
            found.append((y * self.nz + z) * 2 + x)
        return found

    def tie(self, arrays):
        tokens = [t for t in self.latest if t is not None] + self.arrived
        self.arrived = []
        if not tokens:
            return list(arrays)
        return list(lax.optimization_barrier((*arrays, *tokens))[: len(arrays)])

    def move(self, way, a):
        a = self.tie([a])[0]
        self.latest[0] = a
        got = self.moved[self.label] = lax.ppermute(a, AXES, self.across[way])
        return got

    def work(self, f, *arrays):
        made = f(*self.tie(arrays))
        self.latest[1] = jax.tree.leaves(made)[0]
        return made

    def advance(self, name, whole_ring):
        while True:
            kind, *what = self.waiting[name]
            value = self.move(*what) if kind == "move" else self.work(*what)
            self.send(name, value)
            if not whole_ring or name not in self.waiting or self.waiting[name][1][0] not in "udz":
                return

    def send(self, name, value):
        try:
            self.waiting[name] = self.streams[name].send(value)
        except StopIteration as stop:
            self.waiting.pop(name, None)
            self.results[name] = stop.value

    def start(self, name, stream):
        self.streams[name] = stream
        self.send(name, None)

    def ways(self, axis):
        return [f"z{bit}" for bit in self.bits] if axis == "h" else [axis]

    def ordered(self, bit, mine, theirs, axis):
        return jnp.where(
            bit == 0,
            jnp.concatenate([mine, theirs], axis=axis),
            jnp.concatenate([theirs, mine], axis=axis),
        )

    def gather(self, shard, order):
        held = [shard[None]]
        for axis in order:
            a = held[0] if len(held) == 1 else jnp.concatenate(held, axis=0)
            if axis == "z":
                held = [a]
                for _ in range(self.nz - 1):
                    held.append((yield "move", "up", held[-1]))
            elif axis == "Z":
                held = [a]
                for k in range(1, self.nz):
                    held.append((yield "move", f"up{k}", a))
            elif axis == "h":
                held = [a]
                for bit in reversed(self.bits):
                    a = held[0] if len(held) == 1 else jnp.concatenate(held, axis=0)
                    held = [a, (yield "move", f"z{bit}", a)]
            else:
                held = [a, (yield "move", axis, a)]
        return held


def sum_blocks(grid, axis, blocks):
    if axis == "z":
        part = blocks[-1]
        for d in range(len(blocks) - 2, -1, -1):
            part = (yield "move", "down", part.astype(BF)).astype(F32) + blocks[d]
        return part
    arrived = []
    for d in range(1, len(blocks)):
        arrived.append((yield "move", f"down{d}", blocks[d].astype(BF)))
    return sum((piece.astype(F32) for piece in arrived), blocks[0])


def halve(grid, ways, part):
    for way in ways:
        n = part.shape[0]
        part = part[: n // 2] + (yield "move", way, part[n // 2 :].astype(BF)).astype(F32)
    return part


def reduce_axes(grid, part, axes):
    for axis in axes:
        if axis in "zZ":
            part = yield from sum_blocks(grid, axis, jnp.split(part, grid.nz))
        else:
            part = yield from halve(grid, grid.ways(axis), part)
    return part[0]


def reduce_shared(grid, mine, theirs, order):
    axis = order[0]
    if axis in "zZ":
        blocks = jnp.split(mine, grid.nz // 2) + jnp.split(theirs, grid.nz // 2)
        part = yield from sum_blocks(grid, axis, blocks)
    else:
        ways = grid.ways(axis)
        part = mine + (yield "move", ways[0], theirs).astype(F32)
        part = yield from halve(grid, ways[1:], part)
    return (yield from reduce_axes(grid, part, order[1:]))


def body(grid, tokens, segment_ids, pad_mask, w_qkv, w_out, w_gate, w_up, w_down, ln_gain, ln_bias, cotangent):
    me = grid.locate()
    y, c = grid.y, grid.c
    local, width = tokens.shape
    own = 2 * local
    chips = grid.nz * 2
    rows = w_qkv.shape[1]
    two = 2 * rows
    down_rows = w_down.shape[1]
    ff = w_gate.shape[2] // 2
    direct = two % 16 == 0

    def tokens_task():
        message, grid.results["low_down"] = yield "work", make_message, tokens, segment_ids, pad_mask, w_down
        along = jnp.concatenate((yield from grid.gather(message, orders["X"])), axis=0)
        return along, (yield "move", "c", along)

    def columns_task():
        mine, theirs = yield "work", functools.partial(make_columns, me), w_qkv, w_up, w_out, w_gate, ln_gain, ln_bias
        return mine, (yield "move", "c", theirs)

    def shard(start, size):
        mine, theirs = grid.results["P"]
        return grid.ordered(c, mine[:, start : start + size], theirs[:, start : start + size], 0)

    def up_task(order):
        pieces = yield from grid.gather(shard(1152, ff + 512), order)
        outs = jnp.concatenate([p[:, :, ff : ff + 384] for p in pieces], axis=0)
        return pieces, (yield "move", "c", outs)

    def down_task(order):
        part = yield "work", lambda w: w, grid.results["low_down"]
        part = grid.ordered(c, part, (yield "move", "c", part), 0)
        part = jnp.where(c == y, part, (yield "move", "spread", part))
        return (yield from grid.gather(part, order))

    def cot_task():
        return (yield "move", "c", cotangent)

    def placed(pieces, order):
        per = pieces[0].shape[1]
        at = functools.partial(grid.places, order[::-1])
        if direct:
            return pieces, at, per
        blocks = jnp.concatenate(pieces, axis=0)
        table = jnp.stack(at(me))
        blocks = jnp.zeros_like(blocks).at[table].set(blocks)
        return [blocks.reshape(1, -1, blocks.shape[2])], lambda _: [0], blocks.shape[0] * per

    def numbers(index, me):
        chip, side = index >> 1, index & 1
        order = orders["X"][::-1]
        inner = grid.nz if order[1] != "x" else 2
        d = chip & (inner - 1), chip >> (inner.bit_length() - 1)
        dz, dx = d if order[1] != "x" else d[::-1]
        z = grid.back_by(order.replace("x", ""), me[1], dz)
        return ((z * 2 + (me[2] ^ dx)) << 1) + (me[3] ^ side)

    def shared(made, order, per):
        if direct:
            return made
        blocks = jnp.concatenate([made[0][0], made[1][0].astype(F32)], axis=0)
        blocks = blocks.reshape(-1, per, blocks.shape[1])[jnp.stack(grid.places(order, me))]
        half = blocks.shape[0] // 2
        return blocks[:half], blocks[half:].astype(BF)

    def places_of(order, per, total):
        if direct:
            return functools.partial(grid.places, order), per
        return (lambda _: [0, 1]), total // 2

    def down_grad(made, order):
        per = 2 * down_rows
        part = yield from reduce_shared(grid, *shared(made, order, per), order)
        part = part + (yield "move", "home", part.astype(BF)).astype(F32)
        sent = jnp.where(c == 0, part[down_rows:], part[:down_rows])
        kept = jnp.where(c == 0, part[:down_rows], part[down_rows:])
        return jnp.where(c == y, kept, (yield "move", "give", sent))

    def columns_grad(made, order, cuts):
        part = yield from reduce_shared(grid, *shared(made, order, two), order)
        sent = jnp.where(c == 0, part[rows:], part[:rows])
        kept = jnp.where(c == 0, part[:rows], part[rows:])
        got = yield "move", "c", sent[:, : cuts[-1]]
        return [
            grid.ordered(c, kept[:, i:j], got[:, i:j], 1) for i, j in zip(cuts, cuts[1:])
        ] + [kept[:4, cuts[-1] : cuts[-1] + rows]]

    def input_grad(dx, dx_go, dr1, order):
        part = dx + (yield "move", "c", dx_go).astype(F32)
        part = yield from reduce_axes(grid, part, order)
        return dr1 + part

    orders = ORDERS
    got, start = grid.results, grid.start

    def rank_():
        got["rank"] = grid.work(functools.partial(rank, me, numbers), *got["X"])

    def project_():
        pieces, at, per = placed(got["Q"], orders["Q"])
        got["project"] = grid.work(
            lambda *a: project(me, list(a[:-4]), at, per, *a[-4:]), *pieces, *got["X"], *got["rank"][1:3]
        )

    def attend_():
        q, k, v = got["project"][:3]
        got["attend"] = grid.work(attend, q, k, v, got["rank"][3])

    def ob_move():
        got["ob"] = grid.move("c", got["attend"][1])

    def mid_():
        pieces, out_sib = got["U"]
        if not direct:
            table = jnp.stack(grid.places(orders["U"][::-1], me))
            out_sib = jnp.zeros_like(out_sib).at[table].set(out_sib).reshape(1, width, 384)
        pieces, at, per = placed(pieces, orders["U"])
        args = [got["attend"][1], got["ob"], out_sib, *got["X"]]
        got["mid"] = grid.work(lambda *a: mid(me, list(a[:-5]), at, per, *a[-5:], ff, rows), *pieces, *args)
        got["norm"] = got["mid"][7]

    def gate_():
        pieces, at, per = placed(got["G"], orders["G"])
        h1, up = got["mid"][2:4]
        got["gate"] = grid.work(lambda *a: gate_up(me, list(a[:-2]), at, per, *a[-2:]), *pieces, h1, up)

    def down_():
        pieces, at, per = placed(got["D"], orders["D"])
        got["down"] = grid.work(lambda *a: down(me, list(a[:-1]), at, per, a[-1]), *pieces, got["gate"][1])

    def part_move():
        got["part"] = grid.move("c", got["down"][0])

    def turn_():
        n1, _, _, up, _, _, up_w, _ = got["mid"]
        gate, _, gate_w = got["gate"]
        part, down_w = got["down"]
        got["turn"] = grid.work(
            turn, part, got["part"], n1, got["norm"], cotangent, got["C"], got["rank"][4], gate, up, gate_w, up_w, down_w
        )

    def back_move():
        got["back_part"] = grid.move("c", got["turn"][5])

    def grad_d():
        order = orders["d"]
        at, per = places_of(order, 2 * down_rows, ff)
        made = grid.work(functools.partial(grad, me, at, per), got["gate"][1], got["turn"][2])
        start("d", down_grad(made, order))

    def grad_g():
        order = orders["g"]
        at, per = places_of(order, two, width)
        made = grid.work(functools.partial(grad, me, at, per), got["mid"][2], got["turn"][3])
        start("g", columns_grad(made, order, [0, ff]))

    def back_():
        n1, f1 = got["mid"][:2]
        got["back"] = grid.work(
            functools.partial(back, me), got["turn"][1], got["turn"][5], got["back_part"], n1, f1, got["norm"], got["mid"][5]
        )

    def grad_u():
        order = orders["u"]
        at, per = places_of(order, two, width)
        made = grid.work(
            functools.partial(grad_up, me, at, per, rows),
            got["mid"][2], got["turn"][4], got["mid"][4], got["back"][1], got["back"][3], got["turn"][6],
        )
        start("u", columns_grad(made, order, [0, ff, ff + 384]))

    def attend_back_():
        q, k, v, qkv_w = got["project"]
        x_t, cos, sin, ext = got["rank"][:4]
        att, _, lse = got["attend"]
        order = orders["q"]
        at, per = places_of(order, two, width)
        dx, dx_go, *made = grid.work(
            functools.partial(attend_back, me, at, per), q, lse, got["back"][2], att, k, v, ext, cos, sin, x_t, qkv_w
        )
        start("q", columns_grad(made, order, [0, 384, 768, 1152]))
        start("x", input_grad(dx, dx_go, got["back"][0], "x" + orders["x"][-1]))

    start("X", tokens_task())
    start("P", columns_task())
    later = {
        "D": lambda: down_task(orders["D"]),
        "Q": lambda: grid.gather(shard(0, 1152), orders["Q"]),
        "U": lambda: up_task(orders["U"]),
        "G": lambda: grid.gather(shard(1152 + ff + 512, ff), orders["G"]),
    }
    start("C", cot_task())
    single = [
        rank_, project_, attend_, ob_move, mid_, gate_, down_, part_move, turn_, back_move, grad_d, grad_g,
        back_, grad_u, attend_back_,
    ]
    for code in SEQUENCE:
        if code < 0:
            grid.arrived.append(grid.moved[-code])
            continue
        grid.label = code if code >= 200 else code & ~8
        if code >= 200:
            single[code - 200]()
            continue
        name = STREAMS[code >> 4]
        if name in later:
            start(name, later.pop(name)())
        grid.advance(name, bool(code & 8))
    norms = got["u"][2].reshape(2, 2, rows)
    return (
        got["turn"][0],
        got["x"],
        jnp.concatenate(got["q"][:3], axis=1)[None],
        got["u"][1][None],
        got["g"][0][None],
        got["u"][0][None],
        got["d"][None],
        norms[0][None],
        norms[1][None],
    )


def solution(mesh):
    grid = Grid(mesh.shape["dp"], mesh.shape["seq"])
    rows = P(AXES, None)
    weight = P(None, AXES, None)
    norm = P(None, None, AXES)
    return jax.shard_map(
        functools.partial(body, grid),
        mesh=mesh,
        in_specs=(rows, P(AXES), P(AXES)) + (weight,) * 5 + (norm,) * 2 + (rows,),
        out_specs=(rows, rows) + (weight,) * 5 + (norm,) * 2,
        check_vma=False,
    )
```

```python
import functools

import jax
import jax.numpy as jnp
import numpy as np
from jax import lax
from jax.experimental import pallas as pl
from jax.experimental.pallas import tpu as pltpu
from jax.sharding import PartitionSpec as P

HEADS = 12
EPS = 1e-05
BASE = 10000.0
AXES = ("dp", "seq")
BF = jnp.bfloat16
F32 = jnp.float32
FAR = -1e30
NOTE = 16
ONES = 64


ORDERS = {"X": "zx", "x": "Z", "Q": "zxy", "U": "xzy", "G": "hyx", "D": "zx", "d": "zx", "g": "yxZ", "u": "xyz", "q": "yxz"}
STREAMS = "XPQUGDCdguqx"
SEQUENCE = [
    17, 1, 18, -18, 33, 65, 81, 34, 49, 2, -49, 43, 82, 74, -33, 3, -34, 83,
    -2, -65, -35, 36, 50, 67, 37, 12, -66, 51, -50, -4, 5, -3, -67, -36, 68, 84,
    60, -37, -84, 97, 85, -97, -5, 53, 6, -85, -52, -6, 94, 200, -68, 87, 201, 202,
    203, -203, -86, 54, -53, 204, 205, -87, 206, 207, 208, 209, 210, 211, 212, 129, 213, 113,
    145, -54, -209, 214, -113, 161, 130, -145, 114, 146, -130, 131, 177, -129, -114, 123, -161, 162,
    -177, 178, 163, 147, -162, -163, 132, 141, -147, -132, 148, 164, 116, -115, -178, -164, 179, -148,
    173, 157, 117, -116, 180, 118, 166, -166, 189, 150, -149, 134, -118, -134, -180, -150,
]


def dot(a, b):
    return jnp.dot(a, b, preferred_element_type=F32)


def dot_t(a, b):
    return lax.dot_general(a, b, (((1,), (1,)), ((), ())), preferred_element_type=F32)


def t_dot(a, b):
    return lax.dot_general(a, b, (((0,), (0,)), ((), ())), preferred_element_type=F32)


def lanes(shape):
    return lax.broadcasted_iota(jnp.int32, shape, len(shape) - 1)


def swap_halves(u):
    width = u.shape[-1]
    low = lanes(u.shape) % 64 < 32
    return jnp.where(low, pltpu.roll(u, width - 32, 1), pltpu.roll(u, 32, 1))


def split3(v):
    hi = v.astype(BF).astype(F32)
    rest = v - hi
    mid = rest.astype(BF).astype(F32)
    return hi, mid, rest - mid


def with_units(base, v):
    at = lanes(base.shape)
    hi, mid, low = split3(v)
    return jnp.where(
        at == ONES,
        -hi,
        jnp.where(at == ONES + 1, -mid, jnp.where(at == ONES + 2, -low, base)),
    )


def fill(target, pieces, places, per):
    n = 0
    for piece in pieces:
        for i in range(piece.shape[0]):
            target[pl.ds(pl.multiple_of(places[n] * per, 16), per), :] = piece[i]
            n += 1


def whole(shape):
    return pl.BlockSpec(shape, lambda *_: (0,) * len(shape))


def scalars():
    return pl.BlockSpec(memory_space=pltpu.SMEM)


def params(mib):
    return pltpu.CompilerParams(vmem_limit_bytes=mib << 20)


def like(*shape, dtype=F32):
    return jax.ShapeDtypeStruct(shape, dtype)


def far(*shape, dtype=F32):
    return pltpu.HBM(shape, dtype)


def kept_far(*arrays):
    return [pltpu.with_memory_space_constraint(a, pltpu.HBM) for a in arrays]


def message_kernel(x_ref, ids_ref, mask_ref, down_ref, out_ref, low_ref, note_s):
    local = x_ref.shape[0]
    note_s[...] = jnp.zeros(note_s.shape, F32)
    note_s[0:1, :local] = ids_ref[...].astype(F32)
    note_s[1:2, :local] = mask_ref[...].astype(F32)
    out_ref[:local] = x_ref[...]
    out_ref[local:] = note_s[...].astype(BF)
    low_ref[...] = down_ref[0].astype(BF)


def make_message(tokens, ids, mask, down):
    local, width = tokens.shape
    args = [tokens, ids.reshape(1, local), mask.reshape(1, local), down]
    return pl.pallas_call(
        message_kernel,
        grid=(1,),
        in_specs=[whole(a.shape) for a in args],
        out_specs=[whole((local + NOTE, width)), whole(down.shape[1:])],
        out_shape=[like(local + NOTE, width, dtype=BF), like(*down.shape[1:], dtype=BF)],
        scratch_shapes=[pltpu.VMEM((NOTE, width), F32)],
        compiler_params=params(8),
        cost_estimate=pl.CostEstimate(flops=1, bytes_accessed=1, transcendentals=0),
        name="message",
    )(*kept_far(*args))


def columns_kernel(me_ref, qkv_ref, up_ref, out_w_ref, gate_ref, gain_ref, bias_ref, mine_ref, theirs_ref, ext_s):
    c = me_ref[3]
    rows = qkv_ref.shape[1]

    def halves(ref, start, size, to):
        for target, which in ((mine_ref, c), (theirs_ref, 1 - c)):
            at = pl.ds(pl.multiple_of(start + which * size, 128), size)
            target[:, to : to + size] = ref[0, :, at].astype(BF)

    for j in range(3):
        halves(qkv_ref, j * 768, 384, j * 384)
    ff = up_ref.shape[2] // 2
    to = 1152
    halves(up_ref, 0, ff, to)
    halves(out_w_ref, 0, 384, to + ff)
    halves(gate_ref, 0, ff, to + ff + 512)
    ext_s[...] = jnp.zeros(ext_s.shape, F32)
    ext_s[0:2, :rows] = gain_ref[0]
    ext_s[2:4, :rows] = bias_ref[0]
    for target in (mine_ref, theirs_ref):
        target[:, to + ff + 384 : to + ff + 512] = ext_s[...].astype(BF)


def make_columns(me, qkv, up, out_w, gate, gain, bias):
    rows = qkv.shape[1]
    shape = like(rows, 1152 + up.shape[2] + 512, dtype=BF)
    args = [qkv, up, out_w, gate, gain, bias]
    return pl.pallas_call(
        columns_kernel,
        grid=(1,),
        in_specs=[scalars()] + [whole(a.shape) for a in args],
        out_specs=[whole(shape.shape)] * 2,
        out_shape=[shape] * 2,
        scratch_shapes=[pltpu.VMEM((rows, 128), F32)],
        compiler_params=params(12),
        cost_estimate=pl.CostEstimate(flops=1, bytes_accessed=1, transcendentals=0),
        name="columns",
    )(me, *kept_far(*args))


def angle_table(count, stride):
    angle = np.arange(count)[:, None] * float(stride) * BASE ** (-2.0 * (np.arange(128) % 32) / 64)[None, :]
    rest = np.concatenate([np.cos(angle), np.sin(angle)], axis=1)
    parts = []
    for _ in range(3):
        part = rest.astype(jnp.bfloat16)
        parts.append(part)
        rest = rest - part.astype(np.float64)
    return np.concatenate(parts, axis=0)


def rank_kernel(
    me_ref, along_ref, beside_ref, note_a_ref, note_b_ref, fine_ref, coarse_ref,
    t_ref, cos_ref, sin_ref, ext_ref, keep_ref, ext_s, count_s, before_s, *, numbers, coarse,
):
    local = cos_ref.shape[0] // 4
    chips = note_a_ref.shape[0]
    step = pl.program_id(0)
    lane = lanes((local, 128))

    @pl.when(step == 0)
    def _():
        def one(i, _):
            for h, ref in enumerate((note_a_ref, note_b_ref)):
                note = ref[i].astype(F32)[:, :256].T
                own = jnp.where(note[:local, 0:1] == lane.astype(F32), 1.0, 0.0)
                ext = jnp.where(lane < 64, own, jnp.where(lane < ONES + 3, 1.0, 0.0))
                ext_s[2 * i + h] = ext.astype(BF)
                count_s[pl.ds(2 * i + h, 1), :] = jnp.sum(own, axis=0, keepdims=True)
            return 0

        lax.fori_loop(0, chips, one, 0)
        for h, ref in enumerate((note_a_ref, note_b_ref)):
            note = ref[0].astype(F32)[:, :256].T
            keep_ref[h * local : (h + 1) * local] = jnp.broadcast_to(note[:local, 1:2], (local, 128))
        blocks = 2 * chips
        mine = numbers(lax.broadcasted_iota(jnp.int32, (blocks, blocks), 0), me_ref)
        other = numbers(lax.broadcasted_iota(jnp.int32, (blocks, blocks), 1), me_ref)
        before_s[...] = dot(jnp.where(other < mine, 1.0, 0.0).astype(BF), count_s[...].astype(BF))

    x = jnp.concatenate([r[i, :local] for i in range(2) for r in (along_ref, beside_ref)], axis=0)
    t_ref[...] = x.T
    up = lax.broadcasted_iota(jnp.int32, (local, local), 0) > lax.broadcasted_iota(jnp.int32, (local, local), 1)
    up = jnp.where(up, 1.0, 0.0).astype(BF)
    for b in range(4):
        block = 4 * step + b
        ext = ext_s[block]
        rank = dot(up, ext) + before_s[pl.ds(block, 1), :]
        position = jnp.sum(jnp.where(lane < 64, ext.astype(F32) * rank, 0.0), axis=1, keepdims=True)
        high = jnp.floor(position * (1.0 / 64))

        def pick(value, size, table_ref):
            at = lanes((local, 3 * size)) & (size - 1)
            chosen = jnp.where(at.astype(F32) == value, 1.0, 0.0).astype(BF)
            return dot(chosen, table_ref[...])

        low = pick(position - 64 * high, 64, fine_ref)
        high = pick(high, coarse, coarse_ref)
        cos = low[:, :128] * high[:, :128] - low[:, 128:] * high[:, 128:]
        sin = low[:, 128:] * high[:, :128] + low[:, :128] * high[:, 128:]
        rows = slice(b * local, (b + 1) * local)
        cos_ref[rows] = cos
        sin_ref[rows] = jnp.where(lane % 64 < 32, -sin, sin)
        ext_ref[rows] = ext


def rank(me, numbers, along, beside):
    chips, padded, width = along.shape
    local = padded - NOTE
    count = chips * 2 * local
    step = 4 * local
    coarse = max(64, 1 << (-(-count // 64) - 1).bit_length())
    note = pl.BlockSpec((chips, NOTE, width), lambda i: (0, local // NOTE, 0))
    rows = pl.BlockSpec((step, 128), lambda i: (i, 0))
    return pl.pallas_call(
        functools.partial(rank_kernel, numbers=numbers, coarse=coarse),
        grid=(chips // 2,),
        in_specs=[scalars()]
        + [pl.BlockSpec((2, padded, width), lambda i: (i, 0, 0))] * 2
        + [note, note, whole((192, 256)), whole((3 * coarse, 256))],
        out_specs=[pl.BlockSpec((width, step), lambda i: (0, i)), rows, rows, rows, whole((2 * local, 128))],
        out_shape=[
            far(width, count, dtype=BF), far(count, 128), far(count, 128), far(count, 128, dtype=BF),
            like(2 * local, 128),
        ],
        scratch_shapes=[
            pltpu.VMEM((2 * chips, local, 128), BF),
            pltpu.VMEM((2 * chips, 128), F32),
            pltpu.VMEM((2 * chips, 128), F32),
        ],
        compiler_params=params(16),
        cost_estimate=pl.CostEstimate(flops=1, bytes_accessed=1, transcendentals=0),
        name="rank",
    )(
        me, along, beside, along, beside,
        jnp.asarray(angle_table(64, 1)), jnp.asarray(angle_table(coarse, 64)),
    )


def project_kernel(me_ref, *refs, places, per, n):
    pieces = refs[:n]
    along_ref, beside_ref, cos_ref, sin_ref, q_ref, k_ref, v_ref, w_ref = refs[n:]
    local = cos_ref.shape[0] // 4
    first = pl.program_id(0) == 0

    @pl.when(first)
    def _():
        fill(w_ref, pieces, places(me_ref), per)

    x = jnp.concatenate([r[i, :local] for i in range(2) for r in (along_ref, beside_ref)], axis=0)
    cos, sin = cos_ref[...], sin_ref[...]
    kv = dot(x, w_ref[:, 384:])
    for p in range(3):
        at = slice(p * 128, p * 128 + 128)
        u = kv[:, at]
        k_ref[p] = (u * cos + swap_halves(u) * sin).astype(BF)
        v_ref[p] = kv[:, 384 + p * 128 : 512 + p * 128].astype(BF)

    @pl.when(first)
    def _():
        q = dot(x[: 2 * local], w_ref[:, :384])
        for p in range(3):
            at = slice(p * 128, p * 128 + 128)
            u = q[:, at]
            r = (u * cos[: 2 * local] + swap_halves(u) * sin[: 2 * local]).astype(BF)
            q_ref[:, at] = r * jnp.asarray(0.125, BF)


def project(me, pieces, places, per, along, beside, cos, sin):
    chips, padded, width = along.shape
    count = cos.shape[0]
    step = 2 * (count // chips)
    rows = pl.BlockSpec((step, 128), lambda i: (i, 0))
    heads = pl.BlockSpec((3, step, 128), lambda i: (0, i, 0))
    return pl.pallas_call(
        functools.partial(project_kernel, places=places, per=per, n=len(pieces)),
        grid=(chips // 2,),
        in_specs=[scalars()]
        + [whole(p.shape) for p in pieces]
        + [pl.BlockSpec((2, padded, width), lambda i: (i, 0, 0))] * 2
        + [rows] * 2,
        out_specs=[whole((step // 2, 384)), heads, heads, whole((width, 1152))],
        out_shape=[
            far(step // 2, 384, dtype=BF), far(3, count, 128, dtype=BF), far(3, count, 128, dtype=BF),
            far(width, 1152, dtype=BF),
        ],
        compiler_params=params(24),
        cost_estimate=pl.CostEstimate(flops=1, bytes_accessed=1, transcendentals=0),
        name="project",
    )(me, *pieces, along, beside, *kept_far(cos, sin))


def attend_kernel(q_ref, k_ref, v_ref, ext_ref, att_ref, ob_ref, lse_ref, *, chunk):
    keys = k_ref.shape[1]
    q = q_ref[...]
    own = q.shape[0]
    first = lanes(q.shape) < 64
    ext = ext_ref[:own].astype(F32)
    ext = jnp.where(lanes(ext.shape) < 64, (1.0 - ext) * FAR, 0.0).astype(BF)
    parts = []
    for h in range(2):
        qh = jnp.where(first if h == 0 else ~first, q, jnp.zeros_like(q))
        qc = jnp.concatenate([qh, ext], axis=1)
        top = jnp.full((own, 1), FAR, F32)
        acc = jnp.zeros((own, 256), F32)
        for j in range(0, keys, chunk):
            rows = slice(j, j + chunk)
            s = dot_t(qc, jnp.concatenate([k_ref[0, rows], ext_ref[rows]], axis=1))
            above = jnp.maximum(top, jnp.max(s, axis=1, keepdims=True))
            e = jnp.exp(s - above).astype(BF)
            acc = acc * jnp.exp(top - above) + dot(e, jnp.concatenate([v_ref[0, rows], ext_ref[rows]], axis=1))
            top = above
        total = acc[:, 128 + ONES : 129 + ONES]
        parts.append(acc[:, :128] / total)
        lse_ref[h] = with_units(ext.astype(F32), top + jnp.log(total)).astype(BF)
    att = jnp.where(first, parts[0], parts[1])
    att_ref[...] = att
    ob_ref[...] = att.astype(BF)


def attend(q, k, v, ext):
    own = q.shape[0]
    keys = k.shape[1]
    return pl.pallas_call(
        functools.partial(attend_kernel, chunk=512),
        grid=(3,),
        in_specs=[
            pl.BlockSpec((own, 128), lambda p: (0, p)),
            pl.BlockSpec((1, keys, 128), lambda p: (p, 0, 0)),
            pl.BlockSpec((1, keys, 128), lambda p: (p, 0, 0)),
            whole(ext.shape),
        ],
        out_specs=[
            pl.BlockSpec((own, 128), lambda p: (0, p)),
            pl.BlockSpec((own, 128), lambda p: (0, p)),
            pl.BlockSpec((2, own, 128), lambda p: (p, 0, 0)),
        ],
        out_shape=[
            far(own, 384),
            like(own, 384, dtype=BF),
            far(6, own, 128, dtype=BF),
        ],
        compiler_params=params(20 if keys <= 4096 else 60),
        cost_estimate=pl.CostEstimate(
            flops=4 * 6 * own * keys * 256,
            bytes_accessed=3 * keys * 1024,
            transcendentals=6 * own * keys,
        ),
        name="attend",
    )(*kept_far(q, k, v, ext))


def normalize(values):
    average = jnp.mean(values, axis=-1, keepdims=True)
    centred = values - average
    factor = lax.rsqrt(jnp.mean(centred * centred, axis=-1, keepdims=True) + EPS)
    return centred * factor, factor


def norm_back(gradient, normed, factor):
    return factor * (
        gradient
        - jnp.mean(gradient, axis=-1, keepdims=True)
        - normed * jnp.mean(gradient * normed, axis=-1, keepdims=True)
    )


def turned(a):
    half = a.shape[0] // 2
    return jnp.concatenate([a[half:], a[:half]], axis=0)


def silu_parts(gate):
    sigmoid = 1.0 / (1.0 + jnp.exp(-gate))
    return sigmoid, gate * sigmoid


def mid_kernel(me_ref, *refs, places, per, n, share_rows):
    pieces = refs[:n]
    ob_ref, got_ref, sib_ref, along_ref, beside_ref = refs[n : n + 5]
    n1_ref, f1_ref, h1_ref, up_ref, all_ref, out_ref, up_w_ref, norm_ref = refs[n + 5 :]
    local = along_ref.shape[1] - NOTE
    c = me_ref[3]
    ff = up_ref.shape[1]
    at = places(me_ref)
    done = 0
    norm = jnp.zeros(norm_ref.shape, F32)
    width = norm.shape[1]
    for piece in pieces:
        for i in range(piece.shape[0]):
            rows = pl.ds(pl.multiple_of(at[done] * per, 16), per)
            block = piece[i, :, ff + 384 : ff + 512].astype(F32)
            for d in range(per // share_rows):
                ext = jnp.concatenate([block[d * share_rows :][:4], jnp.zeros((4, 128), F32)], axis=0)
                ext = jnp.concatenate([ext, jnp.zeros((8, width - 128), F32)], axis=1)
                norm = norm + pltpu.roll(ext, (at[done] * (per // share_rows) + d) * share_rows, 1)
            up_w_ref[rows, :] = piece[i, :, :ff]
            out_ref[c, rows, :] = piece[i, :, ff : ff + 384]
            out_ref[1 - c, rows, :] = sib_ref[done]
            done += 1
    norm_ref[...] = norm
    all_ref[c] = ob_ref[...]
    all_ref[1 - c] = turned(got_ref[...])
    halves = [dot(all_ref[0], out_ref[i, :384]) + dot(all_ref[1], out_ref[i, 384:]) for i in range(2)]
    n1, f1 = normalize(
        jnp.concatenate([along_ref[0, :local], beside_ref[0, :local]], axis=0).astype(F32)
        + jnp.concatenate(halves, axis=1)
    )
    low = (n1 * norm_ref[0:1] + norm_ref[2:3]).astype(BF)
    n1_ref[...] = n1
    f1_ref[...] = jnp.broadcast_to(f1, f1_ref.shape)
    h1_ref[...] = low
    up_ref[...] = dot(low, up_w_ref[...])


def mid(me, pieces, places, per, ob, got, sib, along, beside, ff, share_rows):
    own, width = ob.shape[0], along.shape[2]
    small = [ob, got, sib, along, beside]
    one = pl.BlockSpec((1, *along.shape[1:]), lambda *_: (0, 0, 0))
    return pl.pallas_call(
        functools.partial(mid_kernel, places=places, per=per, n=len(pieces), share_rows=share_rows),
        in_specs=[scalars()]
        + [whole(a.shape) for a in pieces + small[:3]]
        + [one, one],
        out_specs=[
            whole((own, width)), whole((own, 128)), whole((own, width)), whole((own, ff)),
            whole((2, own, 384)), whole((2, width, 384)), whole((width, ff)), whole((8, width)),
        ],
        out_shape=[
            like(own, width), like(own, 128), like(own, width, dtype=BF), like(own, ff),
            like(2, own, 384, dtype=BF), like(2, width, 384, dtype=BF), like(width, ff, dtype=BF), like(8, width),
        ],
        grid=(1,),
        compiler_params=params(22),
        cost_estimate=pl.CostEstimate(flops=2 * own * width * 2304, bytes_accessed=12 << 20, transcendentals=0),
        name="mid",
    )(me, *pieces, *small)


def gate_kernel(me_ref, *refs, places, per, n):
    pieces = refs[:n]
    h1_ref, up_ref, gate_ref, hidden_ref, w_ref = refs[n:]
    fill(w_ref, pieces, places(me_ref), per)
    gate = dot(h1_ref[...], w_ref[...])
    gate_ref[...] = gate
    hidden_ref[...] = (silu_parts(gate)[1] * up_ref[...]).astype(BF)


def gate_up(me, pieces, places, per, h1, up):
    own, ff = up.shape
    width = h1.shape[1]
    return pl.pallas_call(
        functools.partial(gate_kernel, places=places, per=per, n=len(pieces)),
        grid=(1,),
        in_specs=[scalars()] + [whole(a.shape) for a in [*pieces, h1, up]],
        out_specs=[whole((own, ff)), whole((own, ff)), whole((width, ff))],
        out_shape=[like(own, ff), like(own, ff, dtype=BF), like(width, ff, dtype=BF)],
        compiler_params=params(20),
        cost_estimate=pl.CostEstimate(flops=2 * own * width * ff, bytes_accessed=10 << 20, transcendentals=own * ff),
        name="gate_up",
    )(me, *pieces, h1, up)


def down_kernel(me_ref, *refs, places, per, n):
    pieces = refs[:n]
    hidden_ref, part_ref, w_ref, low_ref = refs[n:]
    fill(w_ref, pieces, places(me_ref), per)
    part = dot(hidden_ref[...], w_ref[...])
    part_ref[...] = part
    low_ref[...] = part.astype(BF)


def down(me, pieces, places, per, hidden):
    own, ff = hidden.shape
    width = pieces[0].shape[2]
    return pl.pallas_call(
        functools.partial(down_kernel, places=places, per=per, n=len(pieces)),
        grid=(1,),
        in_specs=[scalars()] + [whole(a.shape) for a in [*pieces, hidden]],
        out_specs=[whole((own, width)), whole((ff, width)), whole((own, width))],
        out_shape=[like(own, width), like(ff, width, dtype=BF), like(own, width, dtype=BF)],
        compiler_params=params(14),
        cost_estimate=pl.CostEstimate(flops=2 * own * width * ff, bytes_accessed=8 << 20, transcendentals=0),
        name="down",
    )(me, *pieces, hidden)


def turn_kernel(
    part_ref, got_ref, n1_ref, norm_ref, cot_ref, cot_got_ref, keep_ref, gate_ref, up_ref, gate_w_ref, up_w_ref, down_w_ref,
    out_ref, dr2_ref, dm_ref, dgate_ref, dup_ref, back_ref, sums_ref, low_ref,
):
    local = out_ref.shape[0]
    h1 = n1_ref[...] * norm_ref[0:1] + norm_ref[2:3]
    n2, f2 = normalize(h1 + part_ref[...] + turned(got_ref[...]).astype(F32))
    keep = keep_ref[:, :1]
    gain = norm_ref[1:2]
    out_ref[...] = ((n2[:local] * gain + norm_ref[3:4]) * keep[:local]).astype(BF)
    masked = jnp.concatenate([cot_ref[...], cot_got_ref[...]], axis=0).astype(F32) * keep
    sums_ref[0:1] = jnp.sum(masked * n2, axis=0, keepdims=True)
    sums_ref[1:2] = jnp.sum(masked, axis=0, keepdims=True)
    sums_ref[2:] = jnp.zeros((6, sums_ref.shape[1]), F32)
    dr2 = norm_back(masked * gain, n2, f2)
    dr2_ref[...] = dr2
    dm = dr2.astype(BF)
    dm_ref[...] = dm
    ff = gate_ref.shape[1]
    step = 512
    back = jnp.zeros(dr2.shape, F32)
    for j in range(0, ff, step):
        at = slice(j, j + step)
        dh = dot_t(dm, down_w_ref[at, :])
        gate = gate_ref[:, at]
        sigmoid, silu = silu_parts(gate)
        dgate = (dh * up_ref[:, at] * sigmoid * (1.0 + gate * (1.0 - sigmoid))).astype(BF)
        dup = (dh * silu).astype(BF)
        dgate_ref[:, at] = dgate
        dup_ref[:, at] = dup
        back = back + dot_t(dgate, gate_w_ref[:, at]) + dot_t(dup, up_w_ref[:, at])
    back_ref[...] = back
    low_ref[...] = back.astype(BF)


def turn(part, got, n1, norm, cot, cot_got, keep, gate, up, gate_w, up_w, down_w):
    own, width = part.shape
    ff = gate.shape[1]
    args = [part, got, n1, norm, cot, cot_got, keep, gate, up, gate_w, up_w, down_w]
    return pl.pallas_call(
        turn_kernel,
        grid=(1,),
        in_specs=[whole(a.shape) for a in args],
        out_specs=[
            whole((own // 2, width)), whole((own, width)), whole((own, width)), whole((own, ff)),
            whole((own, ff)), whole((own, width)), whole((8, width)), whole((own, width)),
        ],
        out_shape=[
            like(own // 2, width, dtype=BF), like(own, width), like(own, width, dtype=BF),
            like(own, ff, dtype=BF), like(own, ff, dtype=BF), like(own, width), like(8, width), like(own, width, dtype=BF),
        ],
        compiler_params=params(34),
        cost_estimate=pl.CostEstimate(flops=6 * own * width * ff, bytes_accessed=20 << 20, transcendentals=own * ff),
        name="turn",
    )(*args)


def back_kernel(me_ref, dr2_ref, part_ref, got_ref, n1_ref, f1_ref, norm_ref, w_ref, dr1_ref, da_ref, dob_ref, sums_ref):
    dh1 = dr2_ref[...] + part_ref[...] + turned(got_ref[...]).astype(F32)
    n1 = n1_ref[...]
    sums_ref[0:1] = jnp.sum(dh1 * n1, axis=0, keepdims=True)
    sums_ref[1:2] = jnp.sum(dh1, axis=0, keepdims=True)
    sums_ref[2:] = jnp.zeros((6, n1.shape[1]), F32)
    dr1 = norm_back(dh1 * norm_ref[0:1], n1, f1_ref[:, :1])
    dr1_ref[...] = dr1[: dr1_ref.shape[0]]
    da = dr1.astype(BF)
    da_ref[...] = da
    rows = pl.ds(pl.multiple_of(me_ref[3] * 384, 128), 384)
    dob_ref[...] = (dot_t(da[:, :384], w_ref[0, rows, :]) + dot_t(da[:, 384:], w_ref[1, rows, :])).astype(BF)


def back(me, dr2, part, got, n1, f1, norm, out_w):
    own, width = dr2.shape
    args = [dr2, part, got, n1, f1, norm, out_w]
    return pl.pallas_call(
        back_kernel,
        grid=(1,),
        in_specs=[scalars()] + [whole(a.shape) for a in args],
        out_specs=[whole((own // 2, width)), whole((own, width)), whole((own, 384)), whole((8, width))],
        out_shape=[like(own // 2, width), like(own, width, dtype=BF), like(own, 384, dtype=BF), like(8, width)],
        compiler_params=params(14),
        cost_estimate=pl.CostEstimate(flops=2 * own * width * 384, bytes_accessed=7 << 20, transcendentals=0),
        name="back",
    )(me, *args)


def share(whole_ref, at, per, mine_ref, theirs_ref):
    half = mine_ref.shape[0]
    for i in range(2 * half):
        block = whole_ref[pl.ds(pl.multiple_of(at[i] * per, 16), per), :]
        if i < half:
            mine_ref[i, :, : block.shape[1]] = block
        else:
            theirs_ref[i - half, :, : block.shape[1]] = block.astype(BF)


def grad_kernel(me_ref, left_ref, right_ref, mine_ref, theirs_ref, acc_ref, *, places, per):
    acc_ref[...] = t_dot(left_ref[...], right_ref[...])
    share(acc_ref, places(me_ref), per, mine_ref, theirs_ref)


def grad(me, places, per, left, right):
    own, rows = left.shape
    cols = right.shape[1]
    half = rows // per // 2
    step = 768 if cols % 768 == 0 else cols
    return pl.pallas_call(
        functools.partial(grad_kernel, places=places, per=per),
        grid=(cols // step,),
        in_specs=[scalars(), whole(left.shape), pl.BlockSpec((own, step), lambda j: (0, j))],
        out_specs=[pl.BlockSpec((half, per, step), lambda j: (0, 0, j))] * 2,
        out_shape=[like(half, per, cols), like(half, per, cols, dtype=BF)],
        scratch_shapes=[pltpu.VMEM((rows, step), F32)],
        compiler_params=params(18),
        cost_estimate=pl.CostEstimate(flops=2 * own * rows * cols, bytes_accessed=6 * rows * cols, transcendentals=0),
        name="grad",
    )(me, left, right)


def grad_up_kernel(
    me_ref, h1_ref, dup_ref, ob_ref, da_ref, one_ref, two_ref, mine_ref, theirs_ref, acc_ref, sums_s, *, places, per, share_rows
):
    width, ff = h1_ref.shape[1], dup_ref.shape[1]
    at = places(me_ref)
    acc_ref[:, :ff] = t_dot(h1_ref[...], dup_ref[...])
    columns = pl.ds(pl.multiple_of(me_ref[3] * 384, 128), 384)
    da = da_ref[:, columns]
    acc_ref[:384, ff:] = t_dot(ob_ref[0], da)
    acc_ref[384:, ff:] = t_dot(ob_ref[1], da)
    share(acc_ref, at, per, mine_ref, theirs_ref)
    for j in range(2):
        sums_s[2 * j : 2 * j + 1] = one_ref[j : j + 1]
        sums_s[2 * j + 1 : 2 * j + 2] = two_ref[j : j + 1]
    sums_s[4:] = jnp.zeros((4, width), F32)
    sums = sums_s[...]
    half = mine_ref.shape[0]
    lane = lanes((4, 128))
    for i in range(2 * half):
        ref, k = (mine_ref, i) if i < half else (theirs_ref, i - half)
        blocks = []
        for d in range(per // share_rows):
            device = at[i] * (per // share_rows) + d
            turn = pltpu.roll(sums, width - device * share_rows, 1)[:4, :128]
            blocks += [jnp.where(lane < share_rows, turn, 0.0), jnp.zeros((share_rows - 4, 128), F32)]
        ref[k, :, ff + 384 :] = jnp.concatenate(blocks, axis=0).astype(ref.dtype)


def grad_up(me, places, per, share_rows, h1, dup, ob_all, da, one, two):
    width, ff = h1.shape[1], dup.shape[1]
    cols = ff + 512
    half = width // per // 2
    args = [h1, dup, ob_all, da, one, two]
    return pl.pallas_call(
        functools.partial(grad_up_kernel, places=places, per=per, share_rows=share_rows),
        grid=(1,),
        in_specs=[scalars()] + [whole(a.shape) for a in args],
        out_specs=[whole((half, per, cols))] * 2,
        out_shape=[like(half, per, cols), like(half, per, cols, dtype=BF)],
        scratch_shapes=[pltpu.VMEM((width, ff + 384), F32), pltpu.VMEM((8, width), F32)],
        compiler_params=params(24),
        cost_estimate=pl.CostEstimate(flops=1, bytes_accessed=1, transcendentals=0),
        name="grad_up",
    )(me, *args)


def attend_back_kernel(
    me_ref, q_ref, lse_ref, d_ref, att_ref, k_ref, v_ref, ext_ref, cos_ref, sin_ref, cosq_ref, sinq_ref, t_ref, w_ref,
    dx_ref, dx_go_ref, dw_ref, dw_go_ref, qc_s, dc_s, dq_s, dkv_s, dw_s, *, places, per,
):
    j = pl.program_id(0)
    own = q_ref.shape[0]
    local = own // 2
    first = lanes((own, 128)) < 64

    @pl.when(j == 0)
    def _():
        for p in range(3):
            at = slice(p * 128, p * 128 + 128)
            q, d = q_ref[:, at], d_ref[:, at]
            prod = d.astype(F32) * att_ref[:, at]
            for h in range(2):
                keep = first if h == 0 else ~first
                rows = slice(h * own, (h + 1) * own)
                qc_s[p, rows, :128] = jnp.where(keep, q, jnp.zeros_like(q))
                qc_s[p, rows, 128:] = lse_ref[2 * p + h]
                dc_s[p, rows, :128] = jnp.where(keep, d, jnp.zeros_like(d))
                delta = jnp.sum(jnp.where(keep, prod, 0.0), axis=1, keepdims=True)
                dc_s[p, rows, 128:] = with_units(jnp.zeros((own, 128), F32), delta).astype(BF)
        dq_s[...] = jnp.zeros_like(dq_s)
        dw_s[...] = jnp.zeros_like(dw_s)

    ext = ext_ref[...]
    for p in range(3):
        k = k_ref[p]
        e = jnp.exp(dot_t(jnp.concatenate([k, ext], axis=1), qc_s[p]))
        ds = (e * dot_t(jnp.concatenate([v_ref[p], ext], axis=1), dc_s[p])).astype(BF)
        dkv_s[:, 384 + p * 128 : 512 + p * 128] = dot(e.astype(BF), dc_s[p, :, :128]).astype(BF)
        dk = dot(ds, qc_s[p, :, :128]).astype(BF).astype(F32)
        dk = dk * cos_ref[...] - swap_halves(dk) * sin_ref[...]
        dkv_s[:, p * 128 : p * 128 + 128] = dk.astype(BF)
        dq_s[p] += t_dot(k, ds)
    dkv = dkv_s[...]
    dw_s[:, 384:] += dot(t_ref[...], dkv)
    dx = dot_t(dkv, w_ref[:, 384:])

    def put(dx):
        for i in range(dx_ref.shape[0]):
            dx_ref[i] = dx[2 * i * local : (2 * i + 1) * local]
            dx_go_ref[i] = dx[(2 * i + 1) * local : (2 * i + 2) * local].astype(BF)

    last = j == pl.num_programs(0) - 1

    @pl.when(~last)
    def _():
        put(dx)

    @pl.when(last)
    def _():
        dqs = []
        for p in range(3):
            t = dq_s[p].T
            dq = jnp.where(first, t[:own], t[own:])
            dq = (dq * 0.125).astype(BF).astype(F32)
            dqs.append((dq * cosq_ref[...] - swap_halves(dq) * sinq_ref[...]).astype(BF))
        dq = jnp.concatenate(dqs, axis=1)
        dw_s[:, :384] = dot(t_ref[:, :own], dq)
        put(jnp.concatenate([dx[:own] + dot_t(dq, w_ref[:, :384]), dx[own:]], axis=0))
        share(dw_s, places(me_ref), per, dw_ref, dw_go_ref)


def attend_back(me, places, per, q, lse, d, att, k, v, ext, cos, sin, t, w):
    own = q.shape[0]
    keys = k.shape[1]
    width = w.shape[0]
    chunk = 2 * own
    steps = keys // chunk
    half = width // per // 2
    return pl.pallas_call(
        functools.partial(attend_back_kernel, places=places, per=per),
        grid=(steps,),
        in_specs=[
            scalars(),
            whole(q.shape),
            whole(lse.shape),
            whole(d.shape),
            whole(att.shape),
            pl.BlockSpec((3, chunk, 128), lambda j: (0, steps - 1 - j, 0)),
            pl.BlockSpec((3, chunk, 128), lambda j: (0, steps - 1 - j, 0)),
            pl.BlockSpec((chunk, 128), lambda j: (steps - 1 - j, 0)),
            pl.BlockSpec((chunk, 128), lambda j: (steps - 1 - j, 0)),
            pl.BlockSpec((chunk, 128), lambda j: (steps - 1 - j, 0)),
            pl.BlockSpec((own, 128), lambda j: (0, 0)),
            pl.BlockSpec((own, 128), lambda j: (0, 0)),
            pl.BlockSpec((width, chunk), lambda j: (0, steps - 1 - j)),
            whole(w.shape),
        ],
        out_specs=[
            pl.BlockSpec((2, own // 2, width), lambda j: (steps - 1 - j, 0, 0)),
            pl.BlockSpec((2, own // 2, width), lambda j: (steps - 1 - j, 0, 0)),
            whole((half, per, 1152)),
            whole((half, per, 1152)),
        ],
        out_shape=[
            like(keys // own, own // 2, width),
            like(keys // own, own // 2, width, dtype=BF),
            like(half, per, 1152),
            like(half, per, 1152, dtype=BF),
        ],
        scratch_shapes=[
            pltpu.VMEM((3, 2 * own, 256), BF),
            pltpu.VMEM((3, 2 * own, 256), BF),
            pltpu.VMEM((3, 128, 2 * own), F32),
            pltpu.VMEM((chunk, 768), BF),
            pltpu.VMEM((width, 1152), F32),
        ],
        compiler_params=params(40),
        cost_estimate=pl.CostEstimate(
            flops=16 * 6 * own * keys * 256,
            bytes_accessed=3 * keys * 1600,
            transcendentals=6 * own * keys,
        ),
        name="attend_back",
    )(me, *kept_far(q, lse), d, *kept_far(att, k, v, ext, cos, sin, cos, sin, t, w))


class Grid:
    def __init__(self, ndp, nseq):
        self.ny, self.nz = ndp, nseq // 4
        self.count = ndp * nseq
        self.ring = [0, 1, 3, 2] if self.nz == 4 else list(range(self.nz))
        self.place = [self.ring.index(z) for z in range(self.nz)]
        step = {z: self.ring[(self.place[z] + 1) % self.nz] for z in range(self.nz)}
        self.across = {
            "c": self.pairs(lambda y, z, x, c: (y, z, x, 1 - c)),
            "x": self.pairs(lambda y, z, x, c: (y, z, 1 - x, c)),
            "y": self.pairs(lambda y, z, x, c: (1 - y, z, x, c)),
            "up": self.pairs(lambda y, z, x, c: (y, step[z], x, c)),
        }
        self.across["down"] = [(b, a) for a, b in self.across["up"]]
        for k in range(1, self.nz):
            by = {z: self.ring[(self.place[z] + k) % self.nz] for z in range(self.nz)}
            self.across[f"up{k}"] = self.pairs(lambda y, z, x, c, by=by: (y, by[z], x, c))
            self.across[f"down{k}"] = [(b, a) for a, b in self.across[f"up{k}"]]
        self.bits = [1 << i for i in range(self.nz.bit_length() - 1)]
        for bit in self.bits:
            self.across[f"z{bit}"] = self.pairs(lambda y, z, x, c, bit=bit: (y, z ^ bit, x, c))
        self.across["spread"] = self.pairs(lambda y, z, x, c: (1 - y, z, x, c) if c == y else None)
        self.across["home"] = self.pairs(lambda y, z, x, c: (1 - y, z, x, c) if c != y else None)
        self.across["give"] = self.pairs(lambda y, z, x, c: (y, z, x, 1 - c) if c == y else None)

    def pairs(self, to):
        def index(y, z, x, c):
            return ((y * self.nz + z) * 2 + x) * 2 + c

        made = []
        for y in range(self.ny):
            for z in range(self.nz):
                for x in range(2):
                    for c in range(2):
                        there = to(y, z, x, c)
                        if there is not None:
                            made.append((index(y, z, x, c), index(*there)))
        return made

    def locate(self):
        s = lax.axis_index("seq")
        self.arrived, self.moved = [], {}
        self.latest, self.streams, self.waiting, self.results = [None, None], {}, {}, {}
        self.y = lax.axis_index("dp")
        self.z, self.x, self.c = s // 4, (s // 2) % 2, s % 2
        return jnp.stack([self.y, self.z, self.x, self.c]).astype(jnp.int32)

    def back_by(self, axis, z, d):
        if axis == "h":
            moved = sum(jnp.where(d & other != 0, bit, 0) for bit, other in zip(self.bits, reversed(self.bits)))
            return z ^ moved
        return self.place_of((self.place_of(z) + self.nz - d) & (self.nz - 1))

    def place_of(self, z):
        return z ^ (z >> 1) if self.nz == 4 else z

    def places(self, order, me):
        size = {"x": 2, "y": self.ny, "z": self.nz, "Z": self.nz, "h": self.nz}
        total = 1
        for axis in order:
            total *= size[axis]
        found = []
        for i in range(total):
            y, z, x = me[0], me[1], me[2]
            for axis in reversed(order):
                d, i = i % size[axis], i // size[axis]
                if d == 0:
                    continue
                if axis == "x":
                    x = 1 - x
                elif axis == "y":
                    y = 1 - y
                elif axis == "h":
                    z = z ^ sum(bit for bit, other in zip(self.bits, reversed(self.bits)) if d & other)
                else:
                    z = self.place_of((self.place_of(z) + self.nz - d) % self.nz)
            if "y" not in order:
                y = 0
            found.append((y * self.nz + z) * 2 + x)
        return found

    def tie(self, arrays):
        tokens = [t for t in self.latest if t is not None] + self.arrived
        self.arrived = []
        if not tokens:
            return list(arrays)
        return list(lax.optimization_barrier((*arrays, *tokens))[: len(arrays)])

    def move(self, way, a):
        a = self.tie([a])[0]
        self.latest[0] = a
        got = self.moved[self.label] = lax.ppermute(a, AXES, self.across[way])
        return got

    def work(self, f, *arrays):
        made = f(*self.tie(arrays))
        self.latest[1] = jax.tree.leaves(made)[0]
        return made

    def advance(self, name, whole_ring):
        while True:
            kind, *what = self.waiting[name]
            value = self.move(*what) if kind == "move" else self.work(*what)
            self.send(name, value)
            if not whole_ring or name not in self.waiting or self.waiting[name][1][0] not in "udz":
                return

    def send(self, name, value):
        try:
            self.waiting[name] = self.streams[name].send(value)
        except StopIteration as stop:
            self.waiting.pop(name, None)
            self.results[name] = stop.value

    def start(self, name, stream):
        self.streams[name] = stream
        self.send(name, None)

    def ways(self, axis):
        return [f"z{bit}" for bit in self.bits] if axis == "h" else [axis]

    def ordered(self, bit, mine, theirs, axis):
        return jnp.where(
            bit == 0,
            jnp.concatenate([mine, theirs], axis=axis),
            jnp.concatenate([theirs, mine], axis=axis),
        )

    def gather(self, shard, order):
        held = [shard[None]]
        for axis in order:
            a = held[0] if len(held) == 1 else jnp.concatenate(held, axis=0)
            if axis == "z":
                held = [a]
                for _ in range(self.nz - 1):
                    held.append((yield "move", "up", held[-1]))
            elif axis == "Z":
                held = [a]
                for k in range(1, self.nz):
                    held.append((yield "move", f"up{k}", a))
            elif axis == "h":
                held = [a]
                for bit in reversed(self.bits):
                    a = held[0] if len(held) == 1 else jnp.concatenate(held, axis=0)
                    held = [a, (yield "move", f"z{bit}", a)]
            else:
                held = [a, (yield "move", axis, a)]
        return held


def sum_blocks(grid, axis, blocks):
    if axis == "z":
        part = blocks[-1]
        for d in range(len(blocks) - 2, -1, -1):
            part = (yield "move", "down", part.astype(BF)).astype(F32) + blocks[d]
        return part
    arrived = []
    for d in range(1, len(blocks)):
        arrived.append((yield "move", f"down{d}", blocks[d].astype(BF)))
    return sum((piece.astype(F32) for piece in arrived), blocks[0])


def halve(grid, ways, part):
    for way in ways:
        n = part.shape[0]
        part = part[: n // 2] + (yield "move", way, part[n // 2 :].astype(BF)).astype(F32)
    return part


def reduce_axes(grid, part, axes):
    for axis in axes:
        if axis in "zZ":
            part = yield from sum_blocks(grid, axis, jnp.split(part, grid.nz))
        else:
            part = yield from halve(grid, grid.ways(axis), part)
    return part[0]


def reduce_shared(grid, mine, theirs, order):
    axis = order[0]
    if axis in "zZ":
        blocks = jnp.split(mine, grid.nz // 2) + jnp.split(theirs, grid.nz // 2)
        part = yield from sum_blocks(grid, axis, blocks)
    else:
        ways = grid.ways(axis)
        part = mine + (yield "move", ways[0], theirs).astype(F32)
        part = yield from halve(grid, ways[1:], part)
    return (yield from reduce_axes(grid, part, order[1:]))


def body(grid, tokens, segment_ids, pad_mask, w_qkv, w_out, w_gate, w_up, w_down, ln_gain, ln_bias, cotangent):
    me = grid.locate()
    y, c = grid.y, grid.c
    local, width = tokens.shape
    own = 2 * local
    chips = grid.nz * 2
    rows = w_qkv.shape[1]
    two = 2 * rows
    down_rows = w_down.shape[1]
    ff = w_gate.shape[2] // 2
    direct = two % 16 == 0

    def tokens_task():
        message, grid.results["low_down"] = yield "work", make_message, tokens, segment_ids, pad_mask, w_down
        along = jnp.concatenate((yield from grid.gather(message, orders["X"])), axis=0)
        return along, (yield "move", "c", along)

    def columns_task():
        mine, theirs = yield "work", functools.partial(make_columns, me), w_qkv, w_up, w_out, w_gate, ln_gain, ln_bias
        return mine, (yield "move", "c", theirs)

    def shard(start, size):
        mine, theirs = grid.results["P"]
        return grid.ordered(c, mine[:, start : start + size], theirs[:, start : start + size], 0)

    def up_task(order):
        pieces = yield from grid.gather(shard(1152, ff + 512), order)
        outs = jnp.concatenate([p[:, :, ff : ff + 384] for p in pieces], axis=0)
        return pieces, (yield "move", "c", outs)

    def down_task(order):
        part = yield "work", lambda w: w, grid.results["low_down"]
        part = grid.ordered(c, part, (yield "move", "c", part), 0)
        part = jnp.where(c == y, part, (yield "move", "spread", part))
        return (yield from grid.gather(part, order))

    def cot_task():
        return (yield "move", "c", cotangent)

    def placed(pieces, order):
        per = pieces[0].shape[1]
        at = functools.partial(grid.places, order[::-1])
        if direct:
            return pieces, at, per
        blocks = jnp.concatenate(pieces, axis=0)
        table = jnp.stack(at(me))
        blocks = jnp.zeros_like(blocks).at[table].set(blocks)
        return [blocks.reshape(1, -1, blocks.shape[2])], lambda _: [0], blocks.shape[0] * per

    def numbers(index, me):
        chip, side = index >> 1, index & 1
        order = orders["X"][::-1]
        inner = grid.nz if order[1] != "x" else 2
        d = chip & (inner - 1), chip >> (inner.bit_length() - 1)
        dz, dx = d if order[1] != "x" else d[::-1]
        z = grid.back_by(order.replace("x", ""), me[1], dz)
        return ((z * 2 + (me[2] ^ dx)) << 1) + (me[3] ^ side)

    def shared(made, order, per):
        if direct:
            return made
        blocks = jnp.concatenate([made[0][0], made[1][0].astype(F32)], axis=0)
        blocks = blocks.reshape(-1, per, blocks.shape[1])[jnp.stack(grid.places(order, me))]
        half = blocks.shape[0] // 2
        return blocks[:half], blocks[half:].astype(BF)

    def places_of(order, per, total):
        if direct:
            return functools.partial(grid.places, order), per
        return (lambda _: [0, 1]), total // 2

    def down_grad(made, order):
        per = 2 * down_rows
        part = yield from reduce_shared(grid, *shared(made, order, per), order)
        part = part + (yield "move", "home", part.astype(BF)).astype(F32)
        sent = jnp.where(c == 0, part[down_rows:], part[:down_rows])
        kept = jnp.where(c == 0, part[:down_rows], part[down_rows:])
        return jnp.where(c == y, kept, (yield "move", "give", sent))

    def columns_grad(made, order, cuts):
        part = yield from reduce_shared(grid, *shared(made, order, two), order)
        sent = jnp.where(c == 0, part[rows:], part[:rows])
        kept = jnp.where(c == 0, part[:rows], part[rows:])
        got = yield "move", "c", sent[:, : cuts[-1]]
        return [
            grid.ordered(c, kept[:, i:j], got[:, i:j], 1) for i, j in zip(cuts, cuts[1:])
        ] + [kept[:4, cuts[-1] : cuts[-1] + rows]]

    def input_grad(dx, dx_go, dr1, order):
        part = dx + (yield "move", "c", dx_go).astype(F32)
        part = yield from reduce_axes(grid, part, order)
        return dr1 + part

    orders = ORDERS
    got, start = grid.results, grid.start

    def rank_():
        got["rank"] = grid.work(functools.partial(rank, me, numbers), *got["X"])

    def project_():
        pieces, at, per = placed(got["Q"], orders["Q"])
        got["project"] = grid.work(
            lambda *a: project(me, list(a[:-4]), at, per, *a[-4:]), *pieces, *got["X"], *got["rank"][1:3]
        )

    def attend_():
        q, k, v = got["project"][:3]
        got["attend"] = grid.work(attend, q, k, v, got["rank"][3])

    def ob_move():
        got["ob"] = grid.move("c", got["attend"][1])

    def mid_():
        pieces, out_sib = got["U"]
        if not direct:
            table = jnp.stack(grid.places(orders["U"][::-1], me))
            out_sib = jnp.zeros_like(out_sib).at[table].set(out_sib).reshape(1, width, 384)
        pieces, at, per = placed(pieces, orders["U"])
        args = [got["attend"][1], got["ob"], out_sib, *got["X"]]
        got["mid"] = grid.work(lambda *a: mid(me, list(a[:-5]), at, per, *a[-5:], ff, rows), *pieces, *args)
        got["norm"] = got["mid"][7]

    def gate_():
        pieces, at, per = placed(got["G"], orders["G"])
        h1, up = got["mid"][2:4]
        got["gate"] = grid.work(lambda *a: gate_up(me, list(a[:-2]), at, per, *a[-2:]), *pieces, h1, up)

    def down_():
        pieces, at, per = placed(got["D"], orders["D"])
        got["down"] = grid.work(lambda *a: down(me, list(a[:-1]), at, per, a[-1]), *pieces, got["gate"][1])

    def part_move():
        got["part"] = grid.move("c", got["down"][2])

    def turn_():
        n1, _, _, up, _, _, up_w, _ = got["mid"]
        gate, _, gate_w = got["gate"]
        part, down_w, _ = got["down"]
        got["turn"] = grid.work(
            turn, part, got["part"], n1, got["norm"], cotangent, got["C"], got["rank"][4], gate, up, gate_w, up_w, down_w
        )

    def back_move():
        got["back_part"] = grid.move("c", got["turn"][7])

    def grad_d():
        order = orders["d"]
        at, per = places_of(order, 2 * down_rows, ff)
        made = grid.work(functools.partial(grad, me, at, per), got["gate"][1], got["turn"][2])
        start("d", down_grad(made, order))

    def grad_g():
        order = orders["g"]
        at, per = places_of(order, two, width)
        made = grid.work(functools.partial(grad, me, at, per), got["mid"][2], got["turn"][3])
        start("g", columns_grad(made, order, [0, ff]))

    def back_():
        n1, f1 = got["mid"][:2]
        got["back"] = grid.work(
            functools.partial(back, me), got["turn"][1], got["turn"][5], got["back_part"], n1, f1, got["norm"], got["mid"][5]
        )

    def grad_u():
        order = orders["u"]
        at, per = places_of(order, two, width)
        made = grid.work(
            functools.partial(grad_up, me, at, per, rows),
            got["mid"][2], got["turn"][4], got["mid"][4], got["back"][1], got["back"][3], got["turn"][6],
        )
        start("u", columns_grad(made, order, [0, ff, ff + 384]))

    def attend_back_():
        q, k, v, qkv_w = got["project"]
        x_t, cos, sin, ext = got["rank"][:4]
        att, _, lse = got["attend"]
        order = orders["q"]
        at, per = places_of(order, two, width)
        dx, dx_go, *made = grid.work(
            functools.partial(attend_back, me, at, per), q, lse, got["back"][2], att, k, v, ext, cos, sin, x_t, qkv_w
        )
        start("q", columns_grad(made, order, [0, 384, 768, 1152]))
        start("x", input_grad(dx, dx_go, got["back"][0], "x" + orders["x"][-1]))

    start("X", tokens_task())
    start("P", columns_task())
    later = {
        "D": lambda: down_task(orders["D"]),
        "Q": lambda: grid.gather(shard(0, 1152), orders["Q"]),
        "U": lambda: up_task(orders["U"]),
        "G": lambda: grid.gather(shard(1152 + ff + 512, ff), orders["G"]),
    }
    start("C", cot_task())
    single = [
        rank_, project_, attend_, ob_move, mid_, gate_, down_, part_move, turn_, back_move, grad_d, grad_g,
        back_, grad_u, attend_back_,
    ]
    for code in SEQUENCE:
        if code < 0:
            grid.arrived.append(grid.moved[-code])
            continue
        grid.label = code if code >= 200 else code & ~8
        if code >= 200:
            single[code - 200]()
            continue
        name = STREAMS[code >> 4]
        if name in later:
            start(name, later.pop(name)())
        grid.advance(name, bool(code & 8))
    norms = got["u"][2].reshape(2, 2, rows)
    return (
        got["turn"][0],
        got["x"],
        jnp.concatenate(got["q"][:3], axis=1)[None],
        got["u"][1][None],
        got["g"][0][None],
        got["u"][0][None],
        got["d"][None],
        norms[0][None],
        norms[1][None],
    )


def solution(mesh):
    grid = Grid(mesh.shape["dp"], mesh.shape["seq"])
    rows = P(AXES, None)
    weight = P(None, AXES, None)
    norm = P(None, None, AXES)
    return jax.shard_map(
        functools.partial(body, grid),
        mesh=mesh,
        in_specs=(rows, P(AXES), P(AXES)) + (weight,) * 5 + (norm,) * 2 + (rows,),
        out_specs=(rows, rows) + (weight,) * 5 + (norm,) * 2,
        check_vma=False,
    )
```
